128 devices in a mesh: ctx: 32 (over x, z, y_lo), head: 4 (over y_hi, core).
Axes of the slice: x: 4, y: 4 (y_hi: 2, y_lo: 2; y = y_hi * 2 + y_lo), z: 4, core: 2. Of those that a mesh axis runs over, the one named last changes fastest.
Arguments:
- query_rows: bfloat16 [8192, 4096], P(('ctx', 'head')), may hold values from -12 to 12
- key_rows: bfloat16 [8192, 512], P('ctx', 'head'), may hold values from -12 to 12
- value_rows: bfloat16 [8192, 512], P('ctx', 'head'), may hold values from -6 to 6
- attn_output: bfloat16 [8192, 4096], P(('ctx', 'head')), may hold values from -3 to 3
- out_grad: bfloat16 [8192, 4096], P(('ctx', 'head')), may hold values from -6 to 6
- segments: int32 [8192], replicated, may hold values from 0 to 1, never falling along the last dimension, each value on 1 to 6144 neighbouring positions
- parents: int32 [64], replicated, may hold values from -1 to 62, as said below
Outputs:
- query_grad: bfloat16 [8192, 4096], P(('ctx', 'head'))
- key_grad: bfloat16 [8192, 512], P('ctx', 'head')
- value_grad: bfloat16 [8192, 512], P('ctx', 'head')
The draws below stay inside these ranges and needn't reach their ends.
Inputs may be any that keep to these rules, and one draw needn't show every extreme that they name: parents[0] is -1; each block b with 0 < b < 32 has parent b - 1; each later block's parent is b - 1 or a block of the first half at least b - 32; the last block's parent is the block before it.
All inputs are finite; a program needn't handle non-finite values.
Results may differ from the reference program's by a relative error of at most 0.005.
Values may be sent and summed in bfloat16 or wider, within the bound.
A program may use at most 64 MiB of HBM per device.

```python
import math
import jax
import jax.numpy as jnp
import numpy as np
from jax import lax

D_HEAD = 128
Q_HEADS = 32
KV_HEADS = 4
BLOCK = 128
TOKENS = 8192


def draw_query_rows(key, part):
    key = jax.random.fold_in(key, 1)
    base = jnp.clip(jax.random.normal(key, (TOKENS, Q_HEADS * D_HEAD), jnp.float32), -6.0, 6.0)
    return base.astype(jnp.bfloat16)


def draw_key_rows(key, part):
    key = jax.random.fold_in(key, 2)
    base = jnp.clip(jax.random.normal(key, (TOKENS, KV_HEADS * D_HEAD), jnp.float32), -6.0, 6.0)
    return base.astype(jnp.bfloat16)


def draw_parents(key, part):
    key = jax.random.fold_in(key, 3)
    blocks_total = TOKENS // BLOCK
    half_blocks = blocks_total // 2
    block_ids = jnp.arange(blocks_total, dtype=jnp.int32)
    branch = jax.random.randint(jax.random.fold_in(key, 1), (blocks_total,), 0, 4)
    lowest = jnp.maximum(block_ids - half_blocks, 0)
    jumped = jax.random.randint(jax.random.fold_in(key, 2), (blocks_total,), lowest, jnp.maximum(jnp.full((blocks_total,), half_blocks, jnp.int32), lowest + 1))
    parent = jnp.where((branch > 0) | (block_ids < half_blocks), block_ids - 1, jumped)
    parent = jnp.where(block_ids == blocks_total - 1, blocks_total - 2, parent)
    return jnp.where(block_ids == 0, -1, parent).astype(jnp.int32)


def block_levels(key, shape, split, least, high):
    loudness = 1.0
    for axis_at, shards_of in split:
        draws = jax.random.uniform(jax.random.fold_in(jax.random.fold_in(key, 6), axis_at), (shards_of,), jnp.float32, least / len(split), high / len(split))
        loudness = loudness * jnp.repeat(jnp.exp(draws), shape[axis_at] // shards_of).reshape((-1,) + (1,) * (len(shape) - 1 - axis_at))
    return loudness


def profile(number_of, total, bound, lean):
    weights = [(1 << 20) // math.isqrt(grade ** lean) + 1 for grade in range(2, number_of + 1)]
    rest, given = total - bound - (number_of - 1), [1] * (number_of - 1)
    while rest > 0:
        movable = [i for i in range(number_of - 1) if given[i] < bound]
        pool, remaining = sum([weights[i] for i in movable]), rest
        for i in movable:
            extra = min(bound - given[i], max(1, remaining * weights[i] // pool), rest)
            given[i] = given[i] + extra
            rest = rest - extra
    return np.array([bound] + given)


def uneven(own_key, count, total, reach, skew):
    if count == 2:
        one = jax.random.randint(own_key, (), max(1, total - reach), min(reach, total - 1) + 1)
        return jnp.stack([one, total - one])
    tallies = jnp.asarray(profile(count, total, reach, skew), jnp.int32)
    couples = (count - 1) // 2
    source_of, sink = tallies[1:1 + 2 * couples:2], tallies[2:2 + 2 * couples:2]
    margin = jnp.minimum(source_of - 1, reach - sink)
    shifted = jax.random.randint(jax.random.fold_in(own_key, 1), (couples,), 0, 1 << 20) % (margin + 1)
    tallies = tallies.at[1:1 + 2 * couples:2].set(source_of - shifted).at[2:2 + 2 * couples:2].set(sink + shifted)
    return tallies[jax.random.permutation(jax.random.fold_in(own_key, 2), count)]


def centred(rng, extent, spread, bound, cuts=(), held_as=jnp.bfloat16):
    gain = block_levels(rng, extent, cuts, -0.22, 0.18) if cuts else 1.0
    array = jax.random.normal(rng, extent, jnp.float32) * spread * gain
    return jnp.minimum(jnp.maximum(array, -bound), bound).astype(held_as)


def setup_inputs(seed: int = 0) -> dict:
    splits = jax.random.split(jax.random.key(seed), 8)
    query_rows = draw_query_rows(jax.random.fold_in(splits[7], 71), 0)
    key_rows = draw_key_rows(jax.random.fold_in(splits[7], 71), 0)
    value_rows = centred(splits[2], (TOKENS, KV_HEADS * D_HEAD), 1.0, 6.0, ((0, 32), (1, 4)))
    attn_output = centred(splits[3], (TOKENS, Q_HEADS * D_HEAD), 0.5, 3.0, ((0, 128),))
    out_grad = centred(splits[4], (TOKENS, Q_HEADS * D_HEAD), 1.0, 6.0, ((0, 128),))
    segments = jnp.searchsorted(jnp.cumsum(uneven(splits[5], 2, TOKENS, TOKENS * 3 // 4, 0)), jnp.arange(TOKENS), side="right").astype(jnp.int32)
    parents = draw_parents(jax.random.fold_in(splits[7], 71), 0)
    return dict(query_rows=query_rows, key_rows=key_rows, value_rows=value_rows, attn_output=attn_output, out_grad=out_grad, segments=segments, parents=parents)


NEG = -1e+30

def ancestors(parents):
    blocks_total = parents.shape[0]
    block_ids = jnp.arange(blocks_total, dtype=jnp.int32)
    reachable = ((block_ids[:, None] == block_ids[None, :]) | (parents[:, None] == block_ids[None, :])).astype(jnp.int32)
    for squaring in range(max(1, (blocks_total - 1).bit_length())):
        reachable = (jnp.matmul(reachable, reachable) > 0).astype(jnp.int32)
    return reachable

def reference(query_rows, key_rows, value_rows, attn_output, out_grad, segments, parents):
    group_size = Q_HEADS // KV_HEADS
    score_scale = 1.0 / math.sqrt(D_HEAD)
    reachable = ancestors(parents)
    query_width = math.gcd(TOKENS, 256)
    block_total = TOKENS // query_width
    key_all = key_rows.astype(jnp.float32).reshape(TOKENS, KV_HEADS, D_HEAD)
    value_all = value_rows.astype(jnp.float32).reshape(TOKENS, KV_HEADS, D_HEAD)
    reach_cols = jnp.repeat(reachable, BLOCK, axis=1)
    positions = jnp.arange(TOKENS, dtype=jnp.int32)

    def one_block(running, block_index):
        key_sum, value_sum = running
        row_start = (block_index * query_width).astype(jnp.int32)
        query_block = lax.dynamic_slice_in_dim(query_rows, row_start, query_width, 0).astype(jnp.float32).reshape(query_width, KV_HEADS, group_size, D_HEAD)
        grad_block = lax.dynamic_slice_in_dim(out_grad, row_start, query_width, 0).astype(jnp.float32).reshape(query_width, KV_HEADS, group_size, D_HEAD)
        output_block = lax.dynamic_slice_in_dim(attn_output, row_start, query_width, 0).astype(jnp.float32).reshape(query_width, KV_HEADS, group_size, D_HEAD)
        block_rows = lax.dynamic_slice_in_dim(reach_cols, (row_start // BLOCK).astype(jnp.int32), query_width // BLOCK, 0)
        block_rows = jnp.repeat(block_rows, BLOCK, axis=0)
        query_segments = lax.dynamic_slice_in_dim(segments, row_start, query_width, 0)
        query_positions = row_start + jnp.arange(query_width, dtype=jnp.int32)
        allowed = (block_rows > 0) & (query_segments[:, None] == segments[None, :]) & (positions[None, :] <= query_positions[:, None])
        scores = jnp.einsum('qkgd,jkd->kgqj', query_block, key_all) * score_scale
        masked = jnp.where(allowed, scores, NEG)
        row_top = lax.optimization_barrier(jnp.max(masked, axis=-1))
        row_total = lax.optimization_barrier(jnp.sum(jnp.where(allowed, jnp.exp(masked - row_top[..., None]), 0.0), axis=-1))
        log_total = row_top + jnp.log(row_total)
        weights = jnp.where(allowed, jnp.exp(masked - log_total[..., None]), 0.0)
        weights_half = weights.astype(jnp.bfloat16).astype(jnp.float32)
        weight_grad = jnp.einsum('qkgd,jkd->kgqj', grad_block, value_all)
        out_dot = jnp.transpose(lax.optimization_barrier(jnp.sum(grad_block * output_block, axis=-1)), (1, 2, 0))
        score_grad = (weights * (weight_grad - out_dot[..., None])).astype(jnp.bfloat16).astype(jnp.float32)
        query_part = jnp.einsum('kgqj,jkd->qkgd', score_grad, key_all) * score_scale
        query_part = query_part.astype(jnp.bfloat16).reshape(query_width, Q_HEADS * D_HEAD)
        key_sum = key_sum + jnp.einsum('kgqj,qkgd->jkd', score_grad, query_block)
        value_sum = value_sum + jnp.einsum('kgqj,qkgd->jkd', weights_half, grad_block)
        return ((key_sum, value_sum), query_part)
    empty_sums = jnp.zeros((TOKENS, KV_HEADS, D_HEAD), jnp.float32)
    (key_sum, value_sum), query_parts = lax.scan(one_block, (empty_sums, empty_sums), jnp.arange(block_total, dtype=jnp.int32))
    query_grad = query_parts.reshape(TOKENS, Q_HEADS * D_HEAD)
    key_grad = (key_sum * score_scale).astype(jnp.bfloat16).reshape(TOKENS, KV_HEADS * D_HEAD)
    value_grad = value_sum.astype(jnp.bfloat16).reshape(TOKENS, KV_HEADS * D_HEAD)
    return (query_grad, key_grad, value_grad)
```

```python
import functools
import math

import jax
import jax.numpy as jnp
from jax import lax
from jax.experimental import pallas as pl
from jax.experimental.pallas import tpu as pltpu
from jax.sharding import PartitionSpec as P

D = 128
BLOCK = 128
TOKENS = 8192
COLUMN = 512
SECTION = 2048
NEAR = 3
GROUP = 4
ROWS = 512
SCALE = 1.0 / math.sqrt(D)
LOG2E = math.log2(math.e)
NEG = -1e30
F32 = jnp.float32
BF16 = jnp.bfloat16
MESH = pl.DeviceIdType.MESH
NT = (((1,), (1,)), ((), ()))
TN = (((0,), (0,)), ((), ()))


class Place:
    def __init__(self):
        ctx = lax.axis_index("ctx")
        head = lax.axis_index("head")
        self.x = ctx // 8
        self.z = (ctx // 2) % 4
        self.ylo = ctx % 2
        self.yhi = head // 2
        self.core = head % 2
        self.y = self.yhi * 2 + self.ylo

    def at(self, x=None, z=None, ylo=None, yhi=None, core=None):
        x = self.x if x is None else x
        z = self.z if z is None else z
        ylo = self.ylo if ylo is None else ylo
        yhi = self.yhi if yhi is None else yhi
        core = self.core if core is None else core
        return ((x * 4 + z) * 2 + ylo, yhi * 2 + core)

    def in_column(self, t):
        return self.at(ylo=(t // 2) % 2, yhi=t // 4, core=t % 2)

    @property
    def own(self):
        return self.y * 2 + self.core

    def home_row(self, t=None):
        if t is None:
            return (self.ylo * 2 + self.yhi) * 128 + self.core * 64
        return (((t // 2) % 2) * 2 + t // 4) * 128 + (t % 2) * 64


def greet(place):
    barrier = pltpu.get_barrier_semaphore()
    for t in range(8):
        @pl.when(place.own != t)
        def _():
            pl.semaphore_signal(barrier, inc=1, device_id=place.in_column(t), device_id_type=MESH)
    for step in range(1, 4):
        pl.semaphore_signal(
            barrier, inc=1, device_id=place.at(x=(place.x + step) % 4), device_id_type=MESH)
        pl.semaphore_signal(
            barrier, inc=1, device_id=place.at(z=(place.z + step) % 4), device_id_type=MESH)
    pl.semaphore_wait(barrier, 13)


def rcopy(src, dst, send, recv, device):
    return pltpu.make_async_remote_copy(
        src_ref=src, dst_ref=dst, send_sem=send, recv_sem=recv,
        device_id=device, device_id_type=MESH)


class Sends:
    def __init__(self, sems):
        self.sems = sems
        self.items = []

    def start(self, cond, src, dst, recv, device):
        copy = rcopy(src, dst, self.sems.at[len(self.items)], recv, device)
        self.items.append((cond, copy))
        if cond is None:
            copy.start()
        else:
            pl.when(cond)(copy.start)

    def finish(self):
        for cond, copy in self.items:
            if cond is None:
                copy.wait_send()
            else:
                pl.when(cond)(copy.wait_send)


def spread_kernel(q_ref, do_ref, o_ref, k_ref, v_ref,
                  qg_ref, dog_ref, dg_ref, kv_ref,
                  dsrc, col_send, q_recv, do_recv, d_recv, local_sem,
                  first_send, first_recv, piece_send, prim_recv, sib_recv):
    place = Place()
    x, z, core = place.x, place.z, place.core
    greet(place)

    first_row = pl.multiple_of((x * 4 + z) * COLUMN + place.ylo * 256, 256)
    firsts = []
    for p, src in ((0, k_ref), (1, v_ref)):
        dst = kv_ref.at[p, pl.ds(first_row, 256), :]
        here = (place.ylo == core) & (core == p)
        away = jnp.logical_not(here)
        copy = rcopy(src, dst, first_send.at[p], first_recv.at[place.ylo],
                     place.at(ylo=core, core=p))
        local = pltpu.make_async_copy(src, dst, local_sem.at[3])
        pl.when(away)(copy.start)
        pl.when(here)(local.start)
        firsts.append((here, away, copy, local))

    my_row = pl.multiple_of(place.home_row(), 64)
    columns = Sends(col_send)
    locals_ = []
    for t in range(8):
        cols = pl.ds(t * ROWS, ROWS)
        for n, (src, dst, recv) in enumerate(
                ((q_ref, qg_ref, q_recv), (do_ref, dog_ref, do_recv))):
            target = dst.at[pl.ds(my_row, 64), :]
            columns.start(place.own != t, src.at[:, cols], target, recv.at[place.own],
                          place.in_column(t))
            local = pltpu.make_async_copy(src.at[:, cols], target, local_sem.at[n])
            pl.when(place.own == t)(local.start)
            locals_.append((place.own == t, local))

    lane = lax.broadcasted_iota(jnp.int32, (8, 128), 1)
    line = lax.broadcasted_iota(jnp.int32, (8, 128), 0)
    mine = (lane // 64) == core
    ones = jnp.ones((8, D), BF16)
    for t in range(8):
        tile = jnp.zeros((8, 128), F32)
        for r in range(4):
            cols = slice((t * 4 + r) * D, (t * 4 + r + 1) * D)
            prod = do_ref[:, cols].astype(F32) * o_ref[:, cols].astype(F32)
            high = prod.astype(BF16)
            low = (prod - high.astype(F32)).astype(BF16)
            row = (lax.dot_general(ones, high, NT, preferred_element_type=F32)
                   + lax.dot_general(ones, low, NT, preferred_element_type=F32))
            row = jnp.concatenate([row, row], axis=1)
            tile = jnp.where(mine & (line == r), row, tile)
        dsrc[t] = tile
    for t in range(8):
        target = dg_ref.at[place.own]
        columns.start(place.own != t, dsrc.at[t], target, d_recv.at[place.own],
                      place.in_column(t))
        local = pltpu.make_async_copy(dsrc.at[t], target, local_sem.at[2])
        pl.when(place.own == t)(local.start)
        locals_.append((place.own == t, local))

    for half in range(2):
        here = (place.ylo == core) & (place.ylo == half)
        wait = rcopy(k_ref, kv_ref.at[core, pl.ds(0, 256), :], first_send.at[0],
                     first_recv.at[half], place.at(core=1 - core))
        pl.when(jnp.logical_not(here))(wait.wait_recv)
    for here, away, copy, local in firsts:
        pl.when(here)(local.wait)

    def piece(p, xx, zz):
        return kv_ref.at[p, pl.ds(pl.multiple_of((xx * 4 + zz) * COLUMN, COLUMN), COLUMN), :]

    sibling = place.at(core=1 - core)

    def run(c):
        sends = Sends(piece_send)

        def share(cond, xx, zz):
            part = piece(c, xx, zz)
            sends.start(cond, part, part, sib_recv.at[xx * 4 + zz], sibling)

        def along_x(cond, xx, zz):
            part = piece(c, xx, zz)
            for d in (1, 2):
                ok = x + d <= 3
                ok = ok if cond is None else ok & cond
                sends.start(ok, part, part, prim_recv.at[xx * 4 + zz],
                            place.at(x=(x + d) % 4))

        def along_z(cond, xx, zz):
            part = piece(c, xx, zz)
            for d in (1, 3, 2):
                sends.start(cond, part, part, prim_recv.at[xx * 4 + zz],
                            place.at(z=(z + d) % 4))

        def arrive(cond, xx, zz):
            part = piece(c, xx, zz)
            wait = rcopy(part, part, piece_send.at[0], prim_recv.at[xx * 4 + zz], sibling)
            if cond is None:
                wait.wait_recv()
            else:
                pl.when(cond)(wait.wait_recv)

        if c == 0:
            along_z(None, x, z)
            along_x(None, x, z)
            share(None, x, z)
            for dz in (1, 3, 2):
                zz = (z + dz) % 4
                arrive(None, x, zz)
                along_x(None, x, zz)
                share(None, x, zz)
            for dz in (0, 1, 3, 2):
                zz = (z + dz) % 4
                for d in (1, 2):
                    xx = (x + 4 - d) % 4
                    arrive(x >= d, xx, zz)
                    share(x >= d, xx, zz)
        else:
            along_x(None, x, z)
            along_z(None, x, z)
            share(None, x, z)
            for d in (1, 2):
                xx = (x + 4 - d) % 4
                arrive(x >= d, xx, z)
                along_z(x >= d, xx, z)
                share(x >= d, xx, z)
            for d in range(NEAR):
                xx = (x + 4 - d) % 4
                for dz in (1, 3, 2):
                    zz = (z + dz) % 4
                    arrive(None if d == 0 else x >= d, xx, zz)
                    share(None if d == 0 else x >= d, xx, zz)
        for d in range(NEAR):
            xx = (x + 4 - d) % 4
            for zz in range(4):
                part = piece(1 - c, xx, zz)
                wait = rcopy(part, part, piece_send.at[0], sib_recv.at[xx * 4 + zz], sibling)
                pl.when(x >= d)(wait.wait_recv)
        sends.finish()

    pl.when(core == 0)(lambda: run(0))
    pl.when(core == 1)(lambda: run(1))

    for t in range(8):
        @pl.when(place.own != t)
        def _():
            row = place.home_row(t)
            for src, dst, recv in ((q_ref, qg_ref, q_recv), (do_ref, dog_ref, do_recv)):
                rcopy(src.at[:, pl.ds(0, ROWS)], dst.at[pl.ds(row, 64), :], col_send.at[0],
                      recv.at[t], place.in_column(t)).wait_recv()
            rcopy(dsrc.at[t], dg_ref.at[t], col_send.at[0], d_recv.at[t],
                  place.in_column(t)).wait_recv()
    for cond, local in locals_:
        pl.when(cond)(local.wait)
    columns.finish()
    for here, away, copy, local in firsts:
        pl.when(away)(copy.wait_send)


def grad_kernel(parents_ref, seg_ref, q_ref, do_ref, dg_ref, kv_ref,
                dkv_ref, dq_ref,
                acc, expd, keys, values, qr, dor, tops, listed):
    place = Place()
    column = place.x * 4 + place.z
    n0 = jnp.sum((seg_ref[...] == 0).astype(jnp.int32))
    factor = SCALE * LOG2E

    acc[...] = jnp.zeros_like(acc)

    def one_block(qb, carry):
        gb = column * 4 + qb
        q_start = gb * BLOCK
        lowest = jnp.where(q_start >= n0, n0, 0)

        def more(state):
            b, n = state
            return (b >= 0) & (b * BLOCK + (BLOCK - 1) >= lowest)

        def note(state):
            b, n = state
            listed[n] = b
            return (parents_ref[b], n + 1)

        _, count = lax.while_loop(more, note, (gb, jnp.int32(0)))
        for i in range(GROUP - 1):
            listed[count + i] = gb
        groups = (count + GROUP - 1) // GROUP

        row = pl.multiple_of(qb * BLOCK, BLOCK)
        q_rows = q_ref[pl.ds(row, BLOCK), :]
        do_rows = do_ref[pl.ds(row, BLOCK), :]
        for h in range(4):
            qr[h * D:(h + 1) * D, :] = q_rows[:, h * D:(h + 1) * D]
            dor[h * D:(h + 1) * D, :] = do_rows[:, h * D:(h + 1) * D]
        source = ((qb % 2) * 2 + qb // 2) * 2
        pair = dg_ref[source] + dg_ref[source + 1]
        out_dot = jnp.concatenate([pair[h:h + 1, :] for h in range(4)], axis=1)

        query_at = q_start + lax.broadcasted_iota(jnp.int32, (1, ROWS), 1) % BLOCK
        least = jnp.where(query_at >= n0, n0, 0)
        edge = jnp.where(q_start + BLOCK - 1 >= n0, n0, 0)

        def scores_turn(g, state):
            top, total = state
            base = pl.multiple_of(g * GROUP * BLOCK, GROUP * BLOCK)
            at = pl.ds(base, GROUP * BLOCK)
            masked = (g == 0) | (g * GROUP + GROUP > count)
            for i in range(GROUP):
                b = listed[g * GROUP + i]
                masked = masked | (b * BLOCK < edge)
                rows = pl.ds(pl.multiple_of(b * BLOCK, BLOCK), BLOCK)
                dest = pl.ds(pl.multiple_of(base + i * BLOCK, BLOCK), BLOCK)
                keys[dest, :] = kv_ref[0, rows, :]
                values[dest, :] = kv_ref[1, rows, :]
            expd[at, :] = lax.dot_general(keys[at, :], qr[...], NT, preferred_element_type=F32)

            @pl.when(masked)
            def _():
                for i in range(GROUP):
                    b = listed[g * GROUP + i]
                    start = jnp.where(g * GROUP + i < count, b * BLOCK, 2 * TOKENS)
                    dest = pl.ds(pl.multiple_of(base + i * BLOCK, BLOCK), BLOCK)
                    key_at = start + lax.broadcasted_iota(jnp.int32, (BLOCK, ROWS), 0)
                    ok = (key_at <= query_at) & (key_at >= least)
                    expd[dest, :] = jnp.where(ok, expd[dest, :], NEG)

            scores = expd[at, :]
            new_top = jnp.maximum(top, jnp.max(scores, axis=0, keepdims=True))
            e = jnp.exp2((scores - new_top) * factor)
            expd[at, :] = e
            tops[g] = jnp.broadcast_to(new_top, (8, ROWS))
            total = total * jnp.exp2((top - new_top) * factor) + jnp.sum(e, axis=0, keepdims=True)
            return (new_top, total)

        top, total = lax.fori_loop(
            0, groups, scores_turn,
            (jnp.full((1, ROWS), NEG, F32), jnp.zeros((1, ROWS), F32)))
        inverse = 1.0 / total

        def grad_turn(g, dqt):
            base = pl.multiple_of(g * GROUP * BLOCK, GROUP * BLOCK)
            at = pl.ds(base, GROUP * BLOCK)
            share = jnp.exp2((tops[g][0:1, :] - top) * factor) * inverse
            weights = expd[at, :] * share
            half = weights.astype(BF16)
            weight_grad = lax.dot_general(values[at, :], dor[...], NT, preferred_element_type=F32)
            score_grad = (weights * (weight_grad - out_dot)).astype(BF16)
            dv = jnp.dot(half, dor[...], preferred_element_type=F32)
            dk = jnp.dot(score_grad, qr[...], preferred_element_type=F32)
            for i in range(GROUP):
                b = listed[g * GROUP + i]
                rows = pl.ds(pl.multiple_of(b * BLOCK, BLOCK), BLOCK)
                acc[0, rows, :] += dk[i * BLOCK:(i + 1) * BLOCK, :]
                acc[1, rows, :] += dv[i * BLOCK:(i + 1) * BLOCK, :]
            return dqt + lax.dot_general(keys[at, :], score_grad, TN, preferred_element_type=F32)

        dqt = lax.fori_loop(0, groups, grad_turn, jnp.zeros((D, ROWS), F32))
        for h in range(4):
            part = dqt[:, h * D:(h + 1) * D].T * SCALE
            dq_ref[pl.ds(row, BLOCK), h * D:(h + 1) * D] = part.astype(BF16)
        return carry

    lax.fori_loop(0, 4, one_block, 0)
    dkv_ref[0] = (acc[0] * SCALE).astype(BF16)
    dkv_ref[1] = acc[1].astype(BF16)


def home_kernel(dkv_ref, dq_ref,
                qg_ref, kg_ref, vg_ref,
                own, sib, acc, snd, hop, rx, rz, rzz, rx2, done,
                col_send, q_recv, local_sem, own_sem, sib_send, sib_recv,
                send_sems, rx_recv, rz_recv, rzz_recv, rx2_recv, end_send, end_recv):
    place = Place()
    x, z, core = place.x, place.z, place.core
    greet(place)
    sibling = place.at(core=1 - core)

    def section(p, d):
        start = pl.multiple_of(((x + 4 - d) % 4) * SECTION, SECTION)
        return dkv_ref.at[p, pl.ds(start, SECTION), :]

    sib_copies = []
    own_copies = []
    for d in (2, 1, 0):
        copy = rcopy(section(1 - core, d), sib.at[d], sib_send.at[d], sib_recv.at[d], sibling)
        mine = pltpu.make_async_copy(section(core, d), own.at[d], own_sem.at[d])
        pl.when(x >= d)(copy.start)
        pl.when(x >= d)(mine.start)
        sib_copies.append((d, copy))
        own_copies.append((d, mine))

    columns = Sends(col_send)
    col = pl.multiple_of(place.own * ROWS, ROWS)
    target = qg_ref.at[:, pl.ds(col, ROWS)]
    for t in range(8):
        src = dq_ref.at[pl.ds(place.home_row(t), 64), :]
        columns.start(place.own != t, src, target, q_recv.at[place.own], place.in_column(t))
        pl.when(place.own == t)(pltpu.make_async_copy(src, target, local_sem.at[0]).start)

    for (d, copy), (_, mine) in zip(sib_copies, own_copies):
        @pl.when(x >= d)
        def _():
            mine.wait()
            copy.wait_recv()
            both = own[d].astype(F32) + sib[d].astype(F32)
            acc[d] = both
            snd[d] = both.astype(BF16)

    my_rows = pl.ds(pl.multiple_of(z * COLUMN, COLUMN), COLUMN)

    def finish(p, out_ref, total):
        done[...] = total.astype(BF16)
        for half in range(2):
            src = done.at[pl.ds(half * 256, 256), :]
            here = (place.ylo == half) & (core == place.ylo)
            copy = rcopy(src, out_ref, end_send.at[half], end_recv.at[p],
                         place.at(ylo=half, core=place.ylo))
            local = pltpu.make_async_copy(src, out_ref, local_sem.at[1])
            pl.when(here)(local.start)
            pl.when(jnp.logical_not(here))(copy.start)
            pl.when(here)(local.wait)
            pl.when(jnp.logical_not(here))(copy.wait_send)

    @pl.when(core == 0)
    def _():
        sends = Sends(send_sems)
        for d in (2, 1):
            sends.start(x >= d, snd.at[d], rx.at[d - 1], rx_recv.at[d - 1],
                        place.at(x=(x + 4 - d) % 4))
        for d in (1, 2):
            @pl.when(x + d <= 3)
            def _():
                rcopy(snd.at[d], rx.at[d - 1], send_sems.at[0], rx_recv.at[d - 1],
                      sibling).wait_recv()
                acc[0] += rx[d - 1].astype(F32)
        hop[...] = acc[0].astype(BF16)
        for d in (1, 3, 2):
            zz = (z + d) % 4
            src = hop.at[pl.ds(pl.multiple_of(zz * COLUMN, COLUMN), COLUMN), :]
            sends.start(None, src, rz.at[d - 1], rz_recv.at[d - 1], place.at(z=zz))
        total = acc[0, my_rows, :]
        for d in (1, 3, 2):
            rcopy(rz.at[d - 1], rz.at[d - 1], send_sems.at[0], rz_recv.at[d - 1],
                  sibling).wait_recv()
            total = total + rz[d - 1].astype(F32)
        finish(0, kg_ref, total)
        sends.finish()

    @pl.when(core == 1)
    def _():
        sends = Sends(send_sems)
        for e in (2, 1, 0):
            for d in (1, 3, 2):
                zz = (z + d) % 4
                src = snd.at[e, pl.ds(pl.multiple_of(zz * COLUMN, COLUMN), COLUMN), :]
                sends.start(x >= e, src, rzz.at[d - 1, e], rzz_recv.at[d - 1, e], place.at(z=zz))
        total = None
        for e in (2, 1, 0):
            @pl.when(x >= e)
            def _():
                part = acc[e, my_rows, :]
                for d in (1, 3, 2):
                    rcopy(rzz.at[d - 1, e], rzz.at[d - 1, e], send_sems.at[0],
                          rzz_recv.at[d - 1, e], sibling).wait_recv()
                    part = part + rzz[d - 1, e].astype(F32)
                if e == 0:
                    acc[0, my_rows, :] = part
                else:
                    hop[e * COLUMN:(e + 1) * COLUMN, :] = part.astype(BF16)
            if e > 0:
                sends.start(x >= e, hop.at[pl.ds(e * COLUMN, COLUMN), :], rx2.at[e - 1],
                            rx2_recv.at[e - 1], place.at(x=(x + 4 - e) % 4))
        for d in (1, 2):
            @pl.when(x + d <= 3)
            def _():
                rcopy(rx2.at[d - 1], rx2.at[d - 1], send_sems.at[0], rx2_recv.at[d - 1],
                      sibling).wait_recv()
                acc[0, my_rows, :] += rx2[d - 1].astype(F32)
        finish(1, vg_ref, acc[0, my_rows, :])
        sends.finish()

    for p, out_ref in ((0, kg_ref), (1, vg_ref)):
        here = (place.ylo == core) & (core == p)
        wait = rcopy(done.at[pl.ds(0, 256), :], out_ref, end_send.at[0], end_recv.at[p], sibling)
        pl.when(jnp.logical_not(here))(wait.wait_recv)
    for t in range(8):
        @pl.when(place.own != t)
        def _():
            src = dq_ref.at[pl.ds(0, 64), :]
            rcopy(src, qg_ref.at[:, pl.ds(t * ROWS, ROWS)], col_send.at[0], q_recv.at[t],
                  sibling).wait_recv()
    pltpu.make_async_copy(dq_ref.at[pl.ds(0, 64), :], target, local_sem.at[0]).wait()
    columns.finish()
    for d, copy in sib_copies:
        pl.when(x >= d)(copy.wait_send)


ANY = pl.BlockSpec(memory_space=pl.ANY)
VMEM = pl.BlockSpec(memory_space=pltpu.VMEM)
SMEM = pl.BlockSpec(memory_space=pltpu.SMEM)
DMA = pltpu.SemaphoreType.DMA
MIB = 1 << 20


def struct(shape, dtype):
    return jax.ShapeDtypeStruct(shape, dtype)


def spread(q, do, o, k, v):
    return pl.pallas_call(
        spread_kernel,
        out_shape=(struct((COLUMN, ROWS), BF16), struct((COLUMN, ROWS), BF16),
                   struct((8, 8, 128), F32), struct((2, TOKENS, D), BF16)),
        in_specs=[ANY, VMEM, VMEM, ANY, ANY],
        out_specs=(ANY, ANY, ANY, ANY),
        scratch_shapes=[
            pltpu.VMEM((8, 8, 128), F32),
            DMA((24,)), DMA((8,)), DMA((8,)), DMA((8,)), DMA((4,)),
            DMA((2,)), DMA((2,)), DMA((32,)), DMA((16,)), DMA((16,)),
        ],
        compiler_params=pltpu.CompilerParams(
            collective_id=0, has_side_effects=True, vmem_limit_bytes=16 * MIB),
        name="spread",
    )(q, do, o, k, v)


def grads(parents, seg, q, do, dg, kv):
    return pl.pallas_call(
        grad_kernel,
        out_shape=(struct((2, TOKENS, D), BF16), struct((COLUMN, ROWS), BF16)),
        in_specs=[SMEM, VMEM, VMEM, VMEM, VMEM, VMEM],
        out_specs=(VMEM, VMEM),
        scratch_shapes=[
            pltpu.VMEM((2, TOKENS, D), F32),
            pltpu.VMEM((48 * BLOCK, ROWS), F32),
            pltpu.VMEM((48 * BLOCK, D), BF16),
            pltpu.VMEM((48 * BLOCK, D), BF16),
            pltpu.VMEM((ROWS, D), BF16),
            pltpu.VMEM((ROWS, D), BF16),
            pltpu.VMEM((12, 8, ROWS), F32),
            pltpu.SMEM((64,), jnp.int32),
        ],
        compiler_params=pltpu.CompilerParams(vmem_limit_bytes=56 * MIB),
        name="grads",
    )(parents, seg, q, do, dg, kv)


def home(dkv, dq):
    return pl.pallas_call(
        home_kernel,
        out_shape=(struct((64, 4096), BF16), struct((256, D), BF16), struct((256, D), BF16)),
        in_specs=[ANY, ANY],
        out_specs=(ANY, ANY, ANY),
        scratch_shapes=[
            pltpu.VMEM((NEAR, SECTION, D), BF16),
            pltpu.VMEM((NEAR, SECTION, D), BF16),
            pltpu.VMEM((NEAR, SECTION, D), F32),
            pltpu.VMEM((NEAR, SECTION, D), BF16),
            pltpu.VMEM((SECTION, D), BF16),
            pltpu.VMEM((2, SECTION, D), BF16),
            pltpu.VMEM((3, COLUMN, D), BF16),
            pltpu.VMEM((3, NEAR, COLUMN, D), BF16),
            pltpu.VMEM((2, COLUMN, D), BF16),
            pltpu.VMEM((COLUMN, D), BF16),
            DMA((8,)), DMA((8,)), DMA((2,)), DMA((3,)), DMA((3,)), DMA((3,)),
            DMA((12,)), DMA((2,)), DMA((3,)), DMA((3, 3)), DMA((2,)), DMA((2,)), DMA((2,)),
        ],
        compiler_params=pltpu.CompilerParams(
            collective_id=1, has_side_effects=True, vmem_limit_bytes=32 * MIB),
        name="home",
    )(dkv, dq)


def local(query_rows, key_rows, value_rows, attn_output, out_grad, segments, parents):
    q, do, dg, kv = spread(query_rows, out_grad, attn_output, key_rows, value_rows)
    dkv, dq = grads(parents, segments.reshape(64, 128), q, do, dg, kv)
    return home(dkv, dq)


def solution(mesh):
    placed = (
        P(("ctx", "head"), None),
        P("ctx", "head"),
        P("ctx", "head"),
        P(("ctx", "head"), None),
        P(("ctx", "head"), None),
        P(),
        P(),
    )
    return jax.shard_map(
        local,
        mesh=mesh,
        in_specs=placed,
        out_specs=(P(("ctx", "head"), None), P("ctx", "head"), P("ctx", "head")),
        check_vma=False,
    )
```

```python
import functools
import math

import jax
import jax.numpy as jnp
from jax import lax
from jax.experimental import pallas as pl
from jax.experimental.pallas import tpu as pltpu
from jax.sharding import PartitionSpec as P

D = 128
BLOCK = 128
TOKENS = 8192
COLUMN = 512
SECTION = 2048
NEAR = 3
GROUP = 4
ROWS = 512
SCALE = 1.0 / math.sqrt(D)
LOG2E = math.log2(math.e)
NEG = -1e30
F32 = jnp.float32
BF16 = jnp.bfloat16
MESH = pl.DeviceIdType.MESH
NT = (((1,), (1,)), ((), ()))
TN = (((0,), (0,)), ((), ()))


class Place:
    def __init__(self):
        ctx = lax.axis_index("ctx")
        head = lax.axis_index("head")
        self.x = ctx // 8
        self.z = (ctx // 2) % 4
        self.ylo = ctx % 2
        self.yhi = head // 2
        self.core = head % 2
        self.y = self.yhi * 2 + self.ylo

    def at(self, x=None, z=None, ylo=None, yhi=None, core=None):
        x = self.x if x is None else x
        z = self.z if z is None else z
        ylo = self.ylo if ylo is None else ylo
        yhi = self.yhi if yhi is None else yhi
        core = self.core if core is None else core
        return ((x * 4 + z) * 2 + ylo, yhi * 2 + core)

    def in_column(self, t):
        return self.at(ylo=(t // 2) % 2, yhi=t // 4, core=t % 2)

    @property
    def own(self):
        return self.y * 2 + self.core

    def home_row(self, t=None):
        if t is None:
            return (self.ylo * 2 + self.yhi) * 128 + self.core * 64
        return (((t // 2) % 2) * 2 + t // 4) * 128 + (t % 2) * 64


def greet(place):
    barrier = pltpu.get_barrier_semaphore()
    for t in range(8):
        @pl.when(place.own != t)
        def _():
            pl.semaphore_signal(barrier, inc=1, device_id=place.in_column(t), device_id_type=MESH)
    for step in range(1, 4):
        pl.semaphore_signal(
            barrier, inc=1, device_id=place.at(x=(place.x + step) % 4), device_id_type=MESH)
        pl.semaphore_signal(
            barrier, inc=1, device_id=place.at(z=(place.z + step) % 4), device_id_type=MESH)
    pl.semaphore_wait(barrier, 13)


def rcopy(src, dst, send, recv, device):
    return pltpu.make_async_remote_copy(
        src_ref=src, dst_ref=dst, send_sem=send, recv_sem=recv,
        device_id=device, device_id_type=MESH)


class Sends:
    def __init__(self, sems):
        self.sems = sems
        self.items = []

    def start(self, cond, src, dst, recv, device):
        copy = rcopy(src, dst, self.sems.at[len(self.items)], recv, device)
        self.items.append((cond, copy))
        if cond is None:
            copy.start()
        else:
            pl.when(cond)(copy.start)

    def finish(self):
        for cond, copy in self.items:
            if cond is None:
                copy.wait_send()
            else:
                pl.when(cond)(copy.wait_send)


def spread_kernel(q_ref, do_ref, o_ref, k_ref, v_ref,
                  qg_ref, dog_ref, dg_ref, kv_ref,
                  dsrc, col_send, q_recv, do_recv, d_recv, local_sem,
                  first_send, first_recv, piece_send, prim_recv, sib_recv):
    place = Place()
    x, z, core = place.x, place.z, place.core
    greet(place)

    first_row = pl.multiple_of((x * 4 + z) * COLUMN + place.ylo * 256, 256)
    firsts = []
    for p, src in ((0, k_ref), (1, v_ref)):
        dst = kv_ref.at[p, pl.ds(first_row, 256), :]
        here = (place.ylo == core) & (core == p)
        away = jnp.logical_not(here)
        copy = rcopy(src, dst, first_send.at[p], first_recv.at[place.ylo],
                     place.at(ylo=core, core=p))
        local = pltpu.make_async_copy(src, dst, local_sem.at[3])
        pl.when(away)(copy.start)
        pl.when(here)(local.start)
        firsts.append((here, away, copy, local))

    my_row = pl.multiple_of(place.home_row(), 64)
    columns = Sends(col_send)
    locals_ = []
    for t in range(8):
        cols = pl.ds(t * ROWS, ROWS)
        for n, (src, dst, recv) in enumerate(
                ((q_ref, qg_ref, q_recv), (do_ref, dog_ref, do_recv))):
            target = dst.at[pl.ds(my_row, 64), :]
            columns.start(place.own != t, src.at[:, cols], target, recv.at[place.own],
                          place.in_column(t))
            local = pltpu.make_async_copy(src.at[:, cols], target, local_sem.at[n])
            pl.when(place.own == t)(local.start)
            locals_.append((place.own == t, local))

    lane = lax.broadcasted_iota(jnp.int32, (8, 128), 1)
    line = lax.broadcasted_iota(jnp.int32, (8, 128), 0)
    mine = (lane // 64) == core
    ones = jnp.ones((8, D), BF16)
    for t in range(8):
        tile = jnp.zeros((8, 128), F32)
        for r in range(4):
            cols = slice((t * 4 + r) * D, (t * 4 + r + 1) * D)
            prod = do_ref[:, cols].astype(F32) * o_ref[:, cols].astype(F32)
            high = prod.astype(BF16)
            low = (prod - high.astype(F32)).astype(BF16)
            row = (lax.dot_general(ones, high, NT, preferred_element_type=F32)
                   + lax.dot_general(ones, low, NT, preferred_element_type=F32))
            row = jnp.concatenate([row, row], axis=1)
            tile = jnp.where(mine & (line == r), row, tile)
        dsrc[t] = tile
    for t in range(8):
        target = dg_ref.at[place.own]
        columns.start(place.own != t, dsrc.at[t], target, d_recv.at[place.own],
                      place.in_column(t))
        local = pltpu.make_async_copy(dsrc.at[t], target, local_sem.at[2])
        pl.when(place.own == t)(local.start)
        locals_.append((place.own == t, local))

    for half in range(2):
        here = (place.ylo == core) & (place.ylo == half)
        wait = rcopy(k_ref, kv_ref.at[core, pl.ds(0, 256), :], first_send.at[0],
                     first_recv.at[half], place.at(core=1 - core))
        pl.when(jnp.logical_not(here))(wait.wait_recv)
    for here, away, copy, local in firsts:
        pl.when(here)(local.wait)

    def piece(p, xx, zz):
        return kv_ref.at[p, pl.ds(pl.multiple_of((xx * 4 + zz) * COLUMN, COLUMN), COLUMN), :]

    sibling = place.at(core=1 - core)

    def run(c):
        sends = Sends(piece_send)

        def share(cond, xx, zz):
            part = piece(c, xx, zz)
            sends.start(cond, part, part, sib_recv.at[xx * 4 + zz], sibling)

        def along_x(cond, xx, zz):
            part = piece(c, xx, zz)
            for d in (1, 2):
                ok = x + d <= 3
                ok = ok if cond is None else ok & cond
                sends.start(ok, part, part, prim_recv.at[xx * 4 + zz],
                            place.at(x=(x + d) % 4))

        def along_z(cond, xx, zz):
            part = piece(c, xx, zz)
            for d in (1, 3, 2):
                sends.start(cond, part, part, prim_recv.at[xx * 4 + zz],
                            place.at(z=(z + d) % 4))

        def arrive(cond, xx, zz):
            part = piece(c, xx, zz)
            wait = rcopy(part, part, piece_send.at[0], prim_recv.at[xx * 4 + zz], sibling)
            if cond is None:
                wait.wait_recv()
            else:
                pl.when(cond)(wait.wait_recv)

        if c == 0:
            along_z(None, x, z)
            along_x(None, x, z)
            share(None, x, z)
            for dz in (1, 3, 2):
                zz = (z + dz) % 4
                arrive(None, x, zz)
                along_x(None, x, zz)
                share(None, x, zz)
            for dz in (0, 1, 3, 2):
                zz = (z + dz) % 4
                for d in (1, 2):
                    xx = (x + 4 - d) % 4
                    arrive(x >= d, xx, zz)
                    share(x >= d, xx, zz)
        else:
            along_x(None, x, z)
            along_z(None, x, z)
            share(None, x, z)
            for d in (1, 2):
                xx = (x + 4 - d) % 4
                arrive(x >= d, xx, z)
                along_z(x >= d, xx, z)
                share(x >= d, xx, z)
            for d in range(NEAR):
                xx = (x + 4 - d) % 4
                for dz in (1, 3, 2):
                    zz = (z + dz) % 4
                    arrive(None if d == 0 else x >= d, xx, zz)
                    share(None if d == 0 else x >= d, xx, zz)
        for d in range(NEAR):
            xx = (x + 4 - d) % 4
            for zz in range(4):
                part = piece(1 - c, xx, zz)
                wait = rcopy(part, part, piece_send.at[0], sib_recv.at[xx * 4 + zz], sibling)
                pl.when(x >= d)(wait.wait_recv)
        sends.finish()

    pl.when(core == 0)(lambda: run(0))
    pl.when(core == 1)(lambda: run(1))

    for t in range(8):
        @pl.when(place.own != t)
        def _():
            row = place.home_row(t)
            for src, dst, recv in ((q_ref, qg_ref, q_recv), (do_ref, dog_ref, do_recv)):
                rcopy(src.at[:, pl.ds(0, ROWS)], dst.at[pl.ds(row, 64), :], col_send.at[0],
                      recv.at[t], place.in_column(t)).wait_recv()
            rcopy(dsrc.at[t], dg_ref.at[t], col_send.at[0], d_recv.at[t],
                  place.in_column(t)).wait_recv()
    for cond, local in locals_:
        pl.when(cond)(local.wait)
    columns.finish()
    for here, away, copy, local in firsts:
        pl.when(away)(copy.wait_send)


def grad_kernel(parents_ref, seg_ref, q_ref, do_ref, dg_ref, kv_ref,
                dkv_ref, dq_ref,
                acc, expd, keys, values, qr, dor, qt, dot_, tops, listed):
    place = Place()
    column = place.x * 4 + place.z
    n0 = jnp.sum((seg_ref[...] == 0).astype(jnp.int32))
    factor = SCALE * LOG2E
    PIECE = 256

    acc[...] = jnp.zeros_like(acc)

    def one_block(qb, carry):
        gb = column * 4 + qb
        q_start = gb * BLOCK
        lowest = jnp.where(q_start >= n0, n0, 0)

        def more(state):
            b, n = state
            return (b >= 0) & (b * BLOCK + (BLOCK - 1) >= lowest)

        def note(state):
            b, n = state
            listed[n] = b
            return (parents_ref[b], n + 1)

        _, count = lax.while_loop(more, note, (gb, jnp.int32(0)))
        for i in range(GROUP - 1):
            listed[count + i] = gb
        groups = (count + GROUP - 1) // GROUP

        row = pl.multiple_of(qb * BLOCK, BLOCK)
        q_rows = q_ref[pl.ds(row, BLOCK), :]
        do_rows = do_ref[pl.ds(row, BLOCK), :]
        for h in range(4):
            cols = slice(h * D, (h + 1) * D)
            qr[cols, :] = q_rows[:, cols]
            dor[cols, :] = do_rows[:, cols]
            qt[:, cols] = q_rows[:, cols].T
            dot_[:, cols] = do_rows[:, cols].T
        source = ((qb % 2) * 2 + qb // 2) * 2
        pair = dg_ref[source] + dg_ref[source + 1]
        out_dot = jnp.concatenate([pair[h:h + 1, :] for h in range(4)], axis=1)

        query_at = q_start + lax.broadcasted_iota(jnp.int32, (1, ROWS), 1) % BLOCK
        least = jnp.where(query_at >= n0, n0, 0)
        edge = jnp.where(q_start + BLOCK - 1 >= n0, n0, 0)

        def fetch(g):
            base = pl.multiple_of(g * GROUP * BLOCK, GROUP * BLOCK)
            for i in range(GROUP):
                b = listed[g * GROUP + i]
                rows = pl.ds(pl.multiple_of(b * BLOCK, BLOCK), BLOCK)
                dest = pl.ds(pl.multiple_of(base + i * BLOCK, BLOCK), BLOCK)
                keys[dest, :] = kv_ref[0, rows, :]
                values[dest, :] = kv_ref[1, rows, :]

        def scores_of(g, i, masked):
            at = pl.ds(pl.multiple_of((g * GROUP + i) * BLOCK, BLOCK), BLOCK)
            scores = lax.dot_general(kv_ref[0, pl.ds(pl.multiple_of(listed[g * GROUP + i] * BLOCK, BLOCK), BLOCK), :], qr[...], NT, preferred_element_type=F32)
            if masked:
                start = jnp.where(g * GROUP + i < count, listed[g * GROUP + i] * BLOCK, 2 * TOKENS)
                key_at = start + lax.broadcasted_iota(jnp.int32, (BLOCK, ROWS), 0)
                ok = (key_at <= query_at) & (key_at >= least)
                scores = jnp.where(ok, scores, NEG)
            return at, scores

        def fold(e):
            return jnp.sum(e.reshape(BLOCK // 8, 8, ROWS), axis=0)

        def fast_turn(masked, top, g, total):
            fetch(g)
            for i in range(GROUP):
                at, scores = scores_of(g, i, masked)
                e = jnp.exp2((scores - top) * factor)
                expd[at, :] = e
                total = total + fold(e)
            return total

        def slow_turn(g, state):
            top, total = state
            for i in range(GROUP):
                at, scores = scores_of(g, i, True)
                new_top = jnp.maximum(top, jnp.max(scores, axis=0, keepdims=True))
                e = jnp.exp2((scores - new_top) * factor)
                expd[at, :] = e
                tops[pl.ds(pl.multiple_of((g * GROUP + i) * 8, 8), 8), :] = jnp.broadcast_to(new_top, (8, ROWS))
                total = total * jnp.exp2((top - new_top) * factor) + jnp.sum(e, axis=0, keepdims=True)
                top = new_top
            return (top, total)

        fetch(0)
        firsts = [scores_of(0, i, True) for i in range(GROUP)]
        top = functools.reduce(jnp.maximum, [jnp.max(f[1], axis=0, keepdims=True) for f in firsts])
        total = jnp.zeros((8, ROWS), F32)
        for at, scores in firsts:
            e = jnp.exp2((scores - top) * factor)
            expd[at, :] = e
            total = total + fold(e)

        def clear(g, n):
            last = listed[jnp.minimum(g * GROUP + GROUP, count) - 1]
            return jnp.where((g * GROUP + GROUP <= count) & (last * BLOCK >= edge), g + 1, n)

        plain = lax.fori_loop(1, groups, clear, jnp.int32(1))
        total = lax.fori_loop(1, plain, functools.partial(fast_turn, False, top), total)
        total = lax.fori_loop(plain, groups, functools.partial(fast_turn, True, top), total)
        total = jnp.sum(total, axis=0, keepdims=True)
        tops[0:8, :] = jnp.broadcast_to(1.0 / total, (8, ROWS))
        safe = jnp.max(total) < 1e30

        @pl.when(jnp.logical_not(safe))
        def _():
            state = (jnp.full((1, ROWS), NEG, F32), jnp.zeros((1, ROWS), F32))
            top, total = lax.fori_loop(0, groups, slow_turn, state)
            inverse = 1.0 / total

            def rescale(n, c):
                at = pl.ds(pl.multiple_of(n * BLOCK, BLOCK), BLOCK)
                share = jnp.exp2((tops[pl.ds(pl.multiple_of(n * 8, 8), 8), :][0:1] - top) * factor) * inverse
                expd[at, :] = expd[at, :] * share
                return c

            lax.fori_loop(0, groups * GROUP, rescale, 0)
            tops[0:8, :] = jnp.ones((8, ROWS), F32)

        inverse = tops[0:1, :]

        def grad_turn(g, dqt):
            for i in range(GROUP * BLOCK // PIECE):
                base = pl.multiple_of(g * GROUP * BLOCK + i * PIECE, PIECE)
                at = pl.ds(base, PIECE)
                weights = expd[at, :] * inverse
                half = weights.astype(BF16)
                weight_grad = lax.dot_general(values[at, :], dor[...], NT, preferred_element_type=F32)
                score_grad = (weights * (weight_grad - out_dot)).astype(BF16)
                dv = jnp.dot(half, dor[...], preferred_element_type=F32)
                dk = jnp.dot(score_grad, qr[...], preferred_element_type=F32)
                for n in range(PIECE // BLOCK):
                    b = listed[g * GROUP + i * (PIECE // BLOCK) + n]
                    rows = pl.ds(pl.multiple_of(b * BLOCK, BLOCK), BLOCK)
                    acc[0, rows, :] += dk[n * BLOCK:(n + 1) * BLOCK, :]
                    acc[1, rows, :] += dv[n * BLOCK:(n + 1) * BLOCK, :]
                dqt = dqt + lax.dot_general(keys[at, :], score_grad, TN, preferred_element_type=F32)
            return dqt

        dqt = lax.fori_loop(0, groups, grad_turn, jnp.zeros((D, ROWS), F32))
        for h in range(4):
            part = dqt[:, h * D:(h + 1) * D].T * SCALE
            dq_ref[pl.ds(row, BLOCK), h * D:(h + 1) * D] = part.astype(BF16)
        return carry

    lax.fori_loop(0, 4, one_block, 0)
    dkv_ref[0] = (acc[0] * SCALE).astype(BF16)
    dkv_ref[1] = acc[1].astype(BF16)


def home_kernel(dkv_ref, dq_ref,
                qg_ref, kg_ref, vg_ref,
                own, sib, acc, snd, hop, rx, rz, rzz, rx2, done,
                col_send, q_recv, local_sem, own_sem, sib_send, sib_recv,
                send_sems, rx_recv, rz_recv, rzz_recv, rx2_recv, end_send, end_recv):
    place = Place()
    x, z, core = place.x, place.z, place.core
    greet(place)
    sibling = place.at(core=1 - core)

    def section(p, d):
        start = pl.multiple_of(((x + 4 - d) % 4) * SECTION, SECTION)
        return dkv_ref.at[p, pl.ds(start, SECTION), :]

    sib_copies = []
    own_copies = []
    for d in (2, 1, 0):
        copy = rcopy(section(1 - core, d), sib.at[d], sib_send.at[d], sib_recv.at[d], sibling)
        mine = pltpu.make_async_copy(section(core, d), own.at[d], own_sem.at[d])
        pl.when(x >= d)(copy.start)
        pl.when(x >= d)(mine.start)
        sib_copies.append((d, copy))
        own_copies.append((d, mine))

    columns = Sends(col_send)
    col = pl.multiple_of(place.own * ROWS, ROWS)
    target = qg_ref.at[:, pl.ds(col, ROWS)]
    for t in range(8):
        src = dq_ref.at[pl.ds(place.home_row(t), 64), :]
        columns.start(place.own != t, src, target, q_recv.at[place.own], place.in_column(t))
        pl.when(place.own == t)(pltpu.make_async_copy(src, target, local_sem.at[0]).start)

    for (d, copy), (_, mine) in zip(sib_copies, own_copies):
        @pl.when(x >= d)
        def _():
            mine.wait()
            copy.wait_recv()
            both = own[d].astype(F32) + sib[d].astype(F32)
            acc[d] = both
            snd[d] = both.astype(BF16)

    my_rows = pl.ds(pl.multiple_of(z * COLUMN, COLUMN), COLUMN)

    def finish(p, out_ref, total):
        done[...] = total.astype(BF16)
        for half in range(2):
            src = done.at[pl.ds(half * 256, 256), :]
            here = (place.ylo == half) & (core == place.ylo)
            copy = rcopy(src, out_ref, end_send.at[half], end_recv.at[p],
                         place.at(ylo=half, core=place.ylo))
            local = pltpu.make_async_copy(src, out_ref, local_sem.at[1])
            pl.when(here)(local.start)
            pl.when(jnp.logical_not(here))(copy.start)
            pl.when(here)(local.wait)
            pl.when(jnp.logical_not(here))(copy.wait_send)

    @pl.when(core == 0)
    def _():
        sends = Sends(send_sems)
        for d in (2, 1):
            sends.start(x >= d, snd.at[d], rx.at[d - 1], rx_recv.at[d - 1],
                        place.at(x=(x + 4 - d) % 4))
        for d in (1, 2):
            @pl.when(x + d <= 3)
            def _():
                rcopy(snd.at[d], rx.at[d - 1], send_sems.at[0], rx_recv.at[d - 1],
                      sibling).wait_recv()
                acc[0] += rx[d - 1].astype(F32)
        hop[...] = acc[0].astype(BF16)
        for d in (1, 3, 2):
            zz = (z + d) % 4
            src = hop.at[pl.ds(pl.multiple_of(zz * COLUMN, COLUMN), COLUMN), :]
            sends.start(None, src, rz.at[d - 1], rz_recv.at[d - 1], place.at(z=zz))
        total = acc[0, my_rows, :]
        for d in (1, 3, 2):
            rcopy(rz.at[d - 1], rz.at[d - 1], send_sems.at[0], rz_recv.at[d - 1],
                  sibling).wait_recv()
            total = total + rz[d - 1].astype(F32)
        finish(0, kg_ref, total)
        sends.finish()

    @pl.when(core == 1)
    def _():
        sends = Sends(send_sems)
        for e in (2, 1, 0):
            for d in (1, 3, 2):
                zz = (z + d) % 4
                src = snd.at[e, pl.ds(pl.multiple_of(zz * COLUMN, COLUMN), COLUMN), :]
                sends.start(x >= e, src, rzz.at[d - 1, e], rzz_recv.at[d - 1, e], place.at(z=zz))
        total = None
        for e in (2, 1, 0):
            @pl.when(x >= e)
            def _():
                part = acc[e, my_rows, :]
                for d in (1, 3, 2):
                    rcopy(rzz.at[d - 1, e], rzz.at[d - 1, e], send_sems.at[0],
                          rzz_recv.at[d - 1, e], sibling).wait_recv()
                    part = part + rzz[d - 1, e].astype(F32)
                if e == 0:
                    acc[0, my_rows, :] = part
                else:
                    hop[e * COLUMN:(e + 1) * COLUMN, :] = part.astype(BF16)
            if e > 0:
                sends.start(x >= e, hop.at[pl.ds(e * COLUMN, COLUMN), :], rx2.at[e - 1],
                            rx2_recv.at[e - 1], place.at(x=(x + 4 - e) % 4))
        for d in (1, 2):
            @pl.when(x + d <= 3)
            def _():
                rcopy(rx2.at[d - 1], rx2.at[d - 1], send_sems.at[0], rx2_recv.at[d - 1],
                      sibling).wait_recv()
                acc[0, my_rows, :] += rx2[d - 1].astype(F32)
        finish(1, vg_ref, acc[0, my_rows, :])
        sends.finish()

    for p, out_ref in ((0, kg_ref), (1, vg_ref)):
        here = (place.ylo == core) & (core == p)
        wait = rcopy(done.at[pl.ds(0, 256), :], out_ref, end_send.at[0], end_recv.at[p], sibling)
        pl.when(jnp.logical_not(here))(wait.wait_recv)
    for t in range(8):
        @pl.when(place.own != t)
        def _():
            src = dq_ref.at[pl.ds(0, 64), :]
            rcopy(src, qg_ref.at[:, pl.ds(t * ROWS, ROWS)], col_send.at[0], q_recv.at[t],
                  sibling).wait_recv()
    pltpu.make_async_copy(dq_ref.at[pl.ds(0, 64), :], target, local_sem.at[0]).wait()
    columns.finish()
    for d, copy in sib_copies:
        pl.when(x >= d)(copy.wait_send)


ANY = pl.BlockSpec(memory_space=pl.ANY)
VMEM = pl.BlockSpec(memory_space=pltpu.VMEM)
SMEM = pl.BlockSpec(memory_space=pltpu.SMEM)
DMA = pltpu.SemaphoreType.DMA
MIB = 1 << 20


def struct(shape, dtype):
    return jax.ShapeDtypeStruct(shape, dtype)


def spread(q, do, o, k, v):
    return pl.pallas_call(
        spread_kernel,
        out_shape=(struct((COLUMN, ROWS), BF16), struct((COLUMN, ROWS), BF16),
                   struct((8, 8, 128), F32), struct((2, TOKENS, D), BF16)),
        in_specs=[ANY, VMEM, VMEM, ANY, ANY],
        out_specs=(ANY, ANY, ANY, ANY),
        scratch_shapes=[
            pltpu.VMEM((8, 8, 128), F32),
            DMA((24,)), DMA((8,)), DMA((8,)), DMA((8,)), DMA((4,)),
            DMA((2,)), DMA((2,)), DMA((32,)), DMA((16,)), DMA((16,)),
        ],
        compiler_params=pltpu.CompilerParams(
            collective_id=0, has_side_effects=True, vmem_limit_bytes=60 * MIB),
        name="spread",
    )(q, do, o, k, v)


def grads(parents, seg, q, do, dg, kv):
    return pl.pallas_call(
        grad_kernel,
        out_shape=(struct((2, TOKENS, D), BF16), struct((COLUMN, ROWS), BF16)),
        in_specs=[SMEM, VMEM, VMEM, VMEM, VMEM, VMEM],
        out_specs=(VMEM, VMEM),
        scratch_shapes=[
            pltpu.VMEM((2, TOKENS, D), F32),
            pltpu.VMEM((48 * BLOCK, ROWS), F32),
            pltpu.VMEM((48 * BLOCK, D), BF16),
            pltpu.VMEM((48 * BLOCK, D), BF16),
            pltpu.VMEM((ROWS, D), BF16),
            pltpu.VMEM((ROWS, D), BF16),
            pltpu.VMEM((D, ROWS), BF16),
            pltpu.VMEM((D, ROWS), BF16),
            pltpu.VMEM((48 * 8, ROWS), F32),
            pltpu.SMEM((64,), jnp.int32),
        ],
        compiler_params=pltpu.CompilerParams(vmem_limit_bytes=60 * MIB),
        name="grads",
    )(parents, seg, q, do, dg, kv)


def home(dkv, dq):
    return pl.pallas_call(
        home_kernel,
        out_shape=(struct((64, 4096), BF16), struct((256, D), BF16), struct((256, D), BF16)),
        in_specs=[ANY, ANY],
        out_specs=(ANY, ANY, ANY),
        scratch_shapes=[
            pltpu.VMEM((NEAR, SECTION, D), BF16),
            pltpu.VMEM((NEAR, SECTION, D), BF16),
            pltpu.VMEM((NEAR, SECTION, D), F32),
            pltpu.VMEM((NEAR, SECTION, D), BF16),
            pltpu.VMEM((SECTION, D), BF16),
            pltpu.VMEM((2, SECTION, D), BF16),
            pltpu.VMEM((3, COLUMN, D), BF16),
            pltpu.VMEM((3, NEAR, COLUMN, D), BF16),
            pltpu.VMEM((2, COLUMN, D), BF16),
            pltpu.VMEM((COLUMN, D), BF16),
            DMA((8,)), DMA((8,)), DMA((2,)), DMA((3,)), DMA((3,)), DMA((3,)),
            DMA((12,)), DMA((2,)), DMA((3,)), DMA((3, 3)), DMA((2,)), DMA((2,)), DMA((2,)),
        ],
        compiler_params=pltpu.CompilerParams(
            collective_id=1, has_side_effects=True, vmem_limit_bytes=60 * MIB),
        name="home",
    )(dkv, dq)


def local(query_rows, key_rows, value_rows, attn_output, out_grad, segments, parents):
    q, do, dg, kv = spread(query_rows, out_grad, attn_output, key_rows, value_rows)
    dkv, dq = grads(parents, segments.reshape(64, 128), q, do, dg, kv)
    return home(dkv, dq)


def solution(mesh):
    placed = (
        P(("ctx", "head"), None),
        P("ctx", "head"),
        P("ctx", "head"),
        P(("ctx", "head"), None),
        P(("ctx", "head"), None),
        P(),
        P(),
    )
    return jax.shard_map(
        local,
        mesh=mesh,
        in_specs=placed,
        out_specs=(P(("ctx", "head"), None), P("ctx", "head"), P("ctx", "head")),
        check_vma=False,
    )
```

```python
import functools
import math

import jax
import jax.numpy as jnp
from jax import lax
from jax.experimental import pallas as pl
from jax.experimental.pallas import tpu as pltpu
from jax.sharding import PartitionSpec as P

D = 128
BLOCK = 128
TOKENS = 8192
COLUMN = 512
SECTION = 2048
NEAR = 3
GROUP = 4
SCORES_AT_ONCE = 4
GRADS_AT_ONCE = 2
SLOTS = 30
ROWS = 512
SCALE = 1.0 / math.sqrt(D)
LOG2E = math.log2(math.e)
NEG = -1e30
F32 = jnp.float32
BF16 = jnp.bfloat16
MESH = pl.DeviceIdType.MESH
NT = (((1,), (1,)), ((), ()))
TN = (((0,), (0,)), ((), ()))


class Place:
    def __init__(self):
        ctx = lax.axis_index("ctx")
        head = lax.axis_index("head")
        self.x = ctx // 8
        self.z = (ctx // 2) % 4
        self.ylo = ctx % 2
        self.yhi = head // 2
        self.core = head % 2
        self.y = self.yhi * 2 + self.ylo

    def at(self, x=None, z=None, ylo=None, yhi=None, core=None):
        x = self.x if x is None else x
        z = self.z if z is None else z
        ylo = self.ylo if ylo is None else ylo
        yhi = self.yhi if yhi is None else yhi
        core = self.core if core is None else core
        return ((x * 4 + z) * 2 + ylo, yhi * 2 + core)

    def in_column(self, t):
        return self.at(ylo=(t // 2) % 2, yhi=t // 4, core=t % 2)

    @property
    def own(self):
        return self.y * 2 + self.core

    def home_row(self, t=None):
        if t is None:
            return (self.ylo * 2 + self.yhi) * 128 + self.core * 64
        return (((t // 2) % 2) * 2 + t // 4) * 128 + (t % 2) * 64


def greet(place):
    barrier = pltpu.get_barrier_semaphore()
    for t in range(8):
        @pl.when(place.own != t)
        def _():
            pl.semaphore_signal(barrier, inc=1, device_id=place.in_column(t), device_id_type=MESH)
    for step in range(1, 4):
        pl.semaphore_signal(
            barrier, inc=1, device_id=place.at(x=(place.x + step) % 4), device_id_type=MESH)
        pl.semaphore_signal(
            barrier, inc=1, device_id=place.at(z=(place.z + step) % 4), device_id_type=MESH)
    pl.semaphore_wait(barrier, 13)


def rcopy(src, dst, send, recv, device):
    return pltpu.make_async_remote_copy(
        src_ref=src, dst_ref=dst, send_sem=send, recv_sem=recv,
        device_id=device, device_id_type=MESH)


class Sends:
    def __init__(self, sems):
        self.sems = sems
        self.items = []

    def start(self, cond, src, dst, recv, device):
        copy = rcopy(src, dst, self.sems.at[len(self.items)], recv, device)
        self.items.append((cond, copy))
        if cond is None:
            copy.start()
        else:
            pl.when(cond)(copy.start)

    def finish(self):
        for cond, copy in self.items:
            if cond is None:
                copy.wait_send()
            else:
                pl.when(cond)(copy.wait_send)


def spread_kernel(q_ref, do_ref, o_ref, k_ref, v_ref,
                  qg_ref, dog_ref, dg_ref, kv_ref,
                  dsrc, col_send, q_recv, do_recv, d_recv, local_sem,
                  first_send, first_recv, piece_send, prim_recv, sib_recv):
    place = Place()
    x, z, core = place.x, place.z, place.core
    greet(place)

    first_row = pl.multiple_of((x * 4 + z) * COLUMN + place.ylo * 256, 256)
    firsts = []
    for p, src in ((0, k_ref), (1, v_ref)):
        dst = kv_ref.at[p, pl.ds(first_row, 256), :]
        here = (place.ylo == core) & (core == p)
        away = jnp.logical_not(here)
        copy = rcopy(src, dst, first_send.at[p], first_recv.at[place.ylo],
                     place.at(ylo=core, core=p))
        local = pltpu.make_async_copy(src, dst, local_sem.at[3])
        pl.when(away)(copy.start)
        pl.when(here)(local.start)
        firsts.append((here, away, copy, local))

    my_row = pl.multiple_of(place.home_row(), 64)
    columns = Sends(col_send)
    locals_ = []
    for t in range(8):
        cols = pl.ds(t * ROWS, ROWS)
        for n, (src, dst, recv) in enumerate(
                ((q_ref, qg_ref, q_recv), (do_ref, dog_ref, do_recv))):
            target = dst.at[pl.ds(my_row, 64), :]
            columns.start(place.own != t, src.at[:, cols], target, recv.at[place.own],
                          place.in_column(t))
            local = pltpu.make_async_copy(src.at[:, cols], target, local_sem.at[n])
            pl.when(place.own == t)(local.start)
            locals_.append((place.own == t, local))

    lane = lax.broadcasted_iota(jnp.int32, (8, 128), 1)
    line = lax.broadcasted_iota(jnp.int32, (8, 128), 0)
    mine = (lane // 64) == core
    ones = jnp.ones((8, D), BF16)
    for t in range(8):
        tile = jnp.zeros((8, 128), F32)
        for r in range(4):
            cols = slice((t * 4 + r) * D, (t * 4 + r + 1) * D)
            prod = do_ref[:, cols].astype(F32) * o_ref[:, cols].astype(F32)
            high = prod.astype(BF16)
            low = (prod - high.astype(F32)).astype(BF16)
            row = (lax.dot_general(ones, high, NT, preferred_element_type=F32)
                   + lax.dot_general(ones, low, NT, preferred_element_type=F32))
            row = jnp.concatenate([row, row], axis=1)
            tile = jnp.where(mine & (line == r), row, tile)
        dsrc[t] = tile
    for t in range(8):
        target = dg_ref.at[place.own]
        columns.start(place.own != t, dsrc.at[t], target, d_recv.at[place.own],
                      place.in_column(t))
        local = pltpu.make_async_copy(dsrc.at[t], target, local_sem.at[2])
        pl.when(place.own == t)(local.start)
        locals_.append((place.own == t, local))

    for half in range(2):
        here = (place.ylo == core) & (place.ylo == half)
        wait = rcopy(k_ref, kv_ref.at[core, pl.ds(0, 256), :], first_send.at[0],
                     first_recv.at[half], place.at(core=1 - core))
        pl.when(jnp.logical_not(here))(wait.wait_recv)
    for here, away, copy, local in firsts:
        pl.when(here)(local.wait)

    def piece(p, xx, zz):
        return kv_ref.at[p, pl.ds(pl.multiple_of((xx * 4 + zz) * COLUMN, COLUMN), COLUMN), :]

    sibling = place.at(core=1 - core)

    def run(c):
        sends = Sends(piece_send)

        def share(cond, xx, zz):
            part = piece(c, xx, zz)
            sends.start(cond, part, part, sib_recv.at[xx * 4 + zz], sibling)

        def along_x(cond, xx, zz):
            part = piece(c, xx, zz)
            for d in (1, 2):
                ok = x + d <= 3
                ok = ok if cond is None else ok & cond
                sends.start(ok, part, part, prim_recv.at[xx * 4 + zz],
                            place.at(x=(x + d) % 4))

        def along_z(cond, xx, zz):
            part = piece(c, xx, zz)
            for d in (1, 3, 2):
                sends.start(cond, part, part, prim_recv.at[xx * 4 + zz],
                            place.at(z=(z + d) % 4))

        def arrive(cond, xx, zz):
            part = piece(c, xx, zz)
            wait = rcopy(part, part, piece_send.at[0], prim_recv.at[xx * 4 + zz], sibling)
            if cond is None:
                wait.wait_recv()
            else:
                pl.when(cond)(wait.wait_recv)

        if c == 0:
            along_z(None, x, z)
            along_x(None, x, z)
            share(None, x, z)
            for dz in (1, 3, 2):
                zz = (z + dz) % 4
                arrive(None, x, zz)
                along_x(None, x, zz)
                share(None, x, zz)
            for dz in (0, 1, 3, 2):
                zz = (z + dz) % 4
                for d in (1, 2):
                    xx = (x + 4 - d) % 4
                    arrive(x >= d, xx, zz)
                    share(x >= d, xx, zz)
        else:
            along_x(None, x, z)
            along_z(None, x, z)
            share(None, x, z)
            for d in (1, 2):
                xx = (x + 4 - d) % 4
                arrive(x >= d, xx, z)
                along_z(x >= d, xx, z)
                share(x >= d, xx, z)
            for d in range(NEAR):
                xx = (x + 4 - d) % 4
                for dz in (1, 3, 2):
                    zz = (z + dz) % 4
                    arrive(None if d == 0 else x >= d, xx, zz)
                    share(None if d == 0 else x >= d, xx, zz)
        for d in range(NEAR):
            xx = (x + 4 - d) % 4
            for zz in range(4):
                part = piece(1 - c, xx, zz)
                wait = rcopy(part, part, piece_send.at[0], sib_recv.at[xx * 4 + zz], sibling)
                pl.when(x >= d)(wait.wait_recv)
        sends.finish()

    pl.when(core == 0)(lambda: run(0))
    pl.when(core == 1)(lambda: run(1))

    for t in range(8):
        @pl.when(place.own != t)
        def _():
            row = place.home_row(t)
            for src, dst, recv in ((q_ref, qg_ref, q_recv), (do_ref, dog_ref, do_recv)):
                rcopy(src.at[:, pl.ds(0, ROWS)], dst.at[pl.ds(row, 64), :], col_send.at[0],
                      recv.at[t], place.in_column(t)).wait_recv()
            rcopy(dsrc.at[t], dg_ref.at[t], col_send.at[0], d_recv.at[t],
                  place.in_column(t)).wait_recv()
    for cond, local in locals_:
        pl.when(cond)(local.wait)
    columns.finish()
    for here, away, copy, local in firsts:
        pl.when(away)(copy.wait_send)


def grad_kernel(parents_ref, seg_ref, q_hbm, do_hbm, dg_ref, kv_hbm,
                dkv_hbm, dq_ref,
                acc, expd, kv, stage, q_all, do_all, qr, dor, tops, cuts, inv, dqt,
                chain, in_sem, kv_sem, out_sem):
    place = Place()
    x = place.x
    column = x * 4 + place.z
    first_block = (x - (NEAR - 1)) * (SECTION // BLOCK)
    factor = SCALE * LOG2E

    loads = []
    for slot in (2, 1, 0):
        d = 2 - slot
        rows = pl.ds(pl.multiple_of(((x + 4 - d) % 4) * SECTION, SECTION), SECTION)
        for p in range(2):
            copy = pltpu.make_async_copy(
                kv_hbm.at[p, rows, :], kv.at[p, pl.ds(slot * SECTION, SECTION), :],
                kv_sem.at[p, slot])
            pl.when(x >= d)(copy.start)
            loads.append((x >= d, copy))
    q_copy = pltpu.make_async_copy(q_hbm, q_all, in_sem.at[0])
    do_copy = pltpu.make_async_copy(do_hbm, do_all, in_sem.at[1])
    q_copy.start()
    do_copy.start()

    n0 = jnp.sum((seg_ref[...] == 0).astype(jnp.int32))

    chains = [None] * 4
    free = jnp.int32(0)
    for qb in (3, 2, 1, 0):
        gb = column * 4 + qb
        lowest = jnp.where(gb * BLOCK >= n0, n0, 0)
        if qb == 3:
            shared = jnp.bool_(False)
        else:
            base, count, low = chains[qb + 1]
            shared = (parents_ref[gb + 1] == gb) & (low == lowest)

        def more(state):
            b, n = state
            return (b >= 0) & (b * BLOCK + (BLOCK - 1) >= lowest)

        def note(state):
            b, n = state
            chain[n] = b
            return (parents_ref[b], n + 1)

        _, stop = lax.while_loop(more, note, (jnp.where(shared, -1, gb), free))
        own = (free, stop - free, lowest)
        if qb < 3:
            own = (jnp.where(shared, base + 1, free), jnp.where(shared, count - 1, stop - free), lowest)
        chains[qb] = own
        free = stop

    for slot in range(NEAR):
        @pl.when(x >= 2 - slot)
        def _():
            for p in range(2):
                acc[p, slot * SECTION:(slot + 1) * SECTION, :] = jnp.zeros((SECTION, D), F32)
    dqt[...] = jnp.zeros_like(dqt)

    q_copy.wait()
    do_copy.wait()
    for qb in range(4):
        for h in range(4):
            rows, cols = slice(qb * BLOCK, (qb + 1) * BLOCK), slice(h * D, (h + 1) * D)
            qr[qb * ROWS + h * D:qb * ROWS + (h + 1) * D, :] = q_all[rows, cols]
            dor[qb * ROWS + h * D:qb * ROWS + (h + 1) * D, :] = do_all[rows, cols]
    for cond, copy in loads:
        pl.when(cond)(copy.wait)

    def block_rows(b):
        return pl.ds(pl.multiple_of((b - first_block) * BLOCK, BLOCK), BLOCK)

    def gathered(p, blocks):
        return jnp.concatenate([kv[p, block_rows(b), :] for b in blocks], axis=0)

    def row_of(q):
        return pl.ds(pl.multiple_of(q * 8, 8), 1)

    def lines_of(q):
        return pl.ds(pl.multiple_of(q * 8, 8), 8)

    def rows_of(qb):
        return pl.ds(pl.multiple_of(qb * ROWS, ROWS), ROWS)

    def fold(e):
        return jnp.sum(e.reshape(-1, 8, ROWS), axis=0)

    def one_half(half, carry):
        def pick(even, odd):
            return jnp.where(half == 0, even, odd)

        bases = [pick(chains[q][0], chains[q + 2][0]) for q in range(2)]
        counts = [pick(chains[q][1], chains[q + 2][1]) for q in range(2)]
        lows = [pick(chains[q][2], chains[q + 2][2]) for q in range(2)]
        starts = [(column * 4 + half * 2 + q) * BLOCK for q in range(2)]
        steps = [(counts[q] + GROUP - 1) // GROUP - 1 for q in range(2)]
        items = steps[0] + steps[1]

        def blocks_of(q, g):
            base = jnp.where(q == 0, bases[0], bases[1])
            count = jnp.where(q == 0, counts[0], counts[1])
            diagonal = column * 4 + half * 2 + q
            blocks, real = [], []
            for i in range(GROUP):
                at = g * GROUP + i
                here = at < count
                index = base + jnp.where(at == 0, 0, jnp.where(at == 1, count - 1, at - 1))
                blocks.append(jnp.where(here, chain[jnp.where(here, index, 0)], diagonal))
                real.append(here)
            return blocks, real

        def item(slot):
            t = slot - 2
            late = t >= steps[0]
            q = jnp.where(slot < 2, slot, late.astype(jnp.int32))
            g = jnp.where(slot < 2, 0, t - jnp.where(late, steps[0], 0) + 1)
            return q, g

        def expd_rows(slot, i=0, n=GROUP):
            return pl.ds(pl.multiple_of(slot * GROUP * BLOCK + i * BLOCK, BLOCK), n * BLOCK)

        def masked_scores(q, g):
            blocks, real = blocks_of(q, g)
            start = (column * 4 + half * 2 + q) * BLOCK
            query_at = start + lax.broadcasted_iota(jnp.int32, (1, ROWS), 1) % BLOCK
            least = jnp.where(query_at >= n0, n0, 0)
            scores = lax.dot_general(gathered(0, blocks), qr[rows_of(half * 2 + q), :], NT,
                                     preferred_element_type=F32)
            parts = []
            for i in range(GROUP):
                first = jnp.where(real[i], blocks[i] * BLOCK, 2 * TOKENS)
                key_at = first + lax.broadcasted_iota(jnp.int32, (BLOCK, ROWS), 0)
                ok = (key_at <= query_at) & (key_at >= least)
                parts.append(jnp.where(ok, scores[i * BLOCK:(i + 1) * BLOCK, :], NEG))
            return jnp.concatenate(parts, axis=0)

        for q in range(2):
            scores = masked_scores(q, 0)
            top = jnp.max(scores, axis=0, keepdims=True)
            e = jnp.exp2((scores - top) * factor)
            expd[expd_rows(q), :] = e
            inv[lines_of(q), :] = fold(e)
            query_at = starts[q] + lax.broadcasted_iota(jnp.int32, (1, ROWS), 1) % BLOCK
            cut = jnp.where((query_at >= n0) & (starts[q] < n0), -NEG, 0.0)
            cuts[lines_of(q), :] = jnp.broadcast_to(top + cut, (8, ROWS))

        def scores_turn(n, c):
            for u in range(SCORES_AT_ONCE):
                slot = 2 + n * SCORES_AT_ONCE + u
                q, g = item(slot)
                blocks, real = blocks_of(q, g)
                scores = lax.dot_general(gathered(0, blocks), qr[rows_of(half * 2 + q), :], NT,
                                         preferred_element_type=F32)
                top = cuts[row_of(q), :]
                sums = None
                for i in range(GROUP):
                    away = top + jnp.where(real[i], 0.0, -NEG)
                    e = jnp.exp2((scores[i * BLOCK:(i + 1) * BLOCK, :] - away) * factor)
                    expd[expd_rows(slot, i, 1), :] = e
                    sums = fold(e) if sums is None else sums + fold(e)
                inv[lines_of(q), :] += sums
            return c

        lax.fori_loop(0, (items + SCORES_AT_ONCE - 1) // SCORES_AT_ONCE, scores_turn, 0)
        totals = [jnp.sum(inv[q * 8:(q + 1) * 8, :], axis=0, keepdims=True) for q in range(2)]
        safe = jnp.max(jnp.maximum(totals[0], totals[1])) < 1e30
        for q in range(2):
            inv[q * 8:(q + 1) * 8, :] = jnp.broadcast_to(1.0 / totals[q], (8, ROWS))

        @pl.when(jnp.logical_not(safe))
        def _():
            cuts[...] = jnp.full_like(cuts, NEG)
            inv[...] = jnp.zeros_like(inv)

            def again(slot, c):
                q, g = item(slot)
                scores = masked_scores(q, g)
                top, total = cuts[row_of(q), :], inv[row_of(q), :]
                new_top = jnp.maximum(top, jnp.max(scores, axis=0, keepdims=True))
                e = jnp.exp2((scores - new_top) * factor)
                expd[expd_rows(slot), :] = e
                total = total * jnp.exp2((top - new_top) * factor) + jnp.sum(
                    e, axis=0, keepdims=True)
                cuts[lines_of(q), :] = jnp.broadcast_to(new_top, (8, ROWS))
                tops[lines_of(slot), :] = jnp.broadcast_to(new_top, (8, ROWS))
                inv[lines_of(q), :] = jnp.broadcast_to(total, (8, ROWS))
                return c

            def settle(slot, c):
                q, g = item(slot)
                share = jnp.exp2((tops[row_of(slot), :] - cuts[row_of(q), :]) * factor)
                expd[expd_rows(slot), :] = expd[expd_rows(slot), :] * (share / inv[row_of(q), :])
                return c

            lax.fori_loop(0, items + 2, again, 0)
            lax.fori_loop(0, items + 2, settle, 0)
            inv[...] = jnp.ones_like(inv)

        def grads_turn(n, c):
            work = []
            for u in range(GRADS_AT_ONCE):
                slot = n * GRADS_AT_ONCE + u
                q, g = item(slot)
                blocks, _ = blocks_of(q, g)
                do_rows = dor[rows_of(half * 2 + q), :]
                weight_grad = lax.dot_general(gathered(1, blocks), do_rows, NT,
                                              preferred_element_type=F32)
                work.append((slot, q, blocks, do_rows, weight_grad))
            for slot, q, blocks, do_rows, weight_grad in work:
                qb = half * 2 + q
                source = ((qb % 2) * 2 + qb // 2) * 2
                pair = dg_ref[source] + dg_ref[source + 1]
                out_dot = jnp.concatenate([pair[h:h + 1, :] for h in range(4)], axis=1)
                weights = expd[expd_rows(slot), :] * inv[row_of(q), :]
                halved = weights.astype(BF16)
                score_grad = (weights * (weight_grad - out_dot)).astype(BF16)
                dv = jnp.dot(halved, do_rows, preferred_element_type=F32)
                dk = jnp.dot(score_grad, qr[rows_of(qb), :], preferred_element_type=F32)
                into = pl.ds(pl.multiple_of(qb * D, D), D)
                dqt[into, :] += lax.dot_general(gathered(0, blocks), score_grad, TN,
                                                preferred_element_type=F32)
                for i, b in enumerate(blocks):
                    rows = block_rows(b)
                    acc[0, rows, :] += dk[i * BLOCK:(i + 1) * BLOCK, :]
                    acc[1, rows, :] += dv[i * BLOCK:(i + 1) * BLOCK, :]
            return c

        lax.fori_loop(0, (items + 2 + GRADS_AT_ONCE - 1) // GRADS_AT_ONCE, grads_turn, 0)
        return carry

    lax.fori_loop(0, 2, one_half, 0)

    stores = []
    for slot in range(NEAR):
        for p, by in ((0, SCALE), (1, 1.0)):
            at = slice(slot * SECTION, (slot + 1) * SECTION)
            copy = pltpu.make_async_copy(
                stage.at[p, pl.ds(slot * SECTION, SECTION), :], dkv_hbm.at[p, slot],
                out_sem.at[p, slot])

            @pl.when(x >= 2 - slot)
            def _():
                stage[p, at, :] = (acc[p, at, :] * by).astype(BF16)
                copy.start()
            stores.append((x >= 2 - slot, copy))
    for qb in range(4):
        for h in range(4):
            part = dqt[qb * D:(qb + 1) * D, h * D:(h + 1) * D].T * SCALE
            dq_ref[qb * BLOCK:(qb + 1) * BLOCK, h * D:(h + 1) * D] = part.astype(BF16)
    for cond, copy in stores:
        pl.when(cond)(copy.wait)


def home_kernel(dkv_ref, dq_ref,
                qg_ref, kg_ref, vg_ref,
                own, sib, acc, snd, hop, rx, rz, rzz, rx2, done,
                col_send, q_recv, local_sem, own_sem, sib_send, sib_recv,
                send_sems, rx_recv, rz_recv, rzz_recv, rx2_recv, end_send, end_recv):
    place = Place()
    x, z, core = place.x, place.z, place.core
    greet(place)
    sibling = place.at(core=1 - core)

    def section(p, d):
        return dkv_ref.at[p, 2 - d]

    sib_copies = []
    own_copies = []
    for d in (2, 1, 0):
        copy = rcopy(section(1 - core, d), sib.at[d], sib_send.at[d], sib_recv.at[d], sibling)
        mine = pltpu.make_async_copy(section(core, d), own.at[d], own_sem.at[d])
        pl.when(x >= d)(copy.start)
        pl.when(x >= d)(mine.start)
        sib_copies.append((d, copy))
        own_copies.append((d, mine))

    columns = Sends(col_send)
    col = pl.multiple_of(place.own * ROWS, ROWS)
    target = qg_ref.at[:, pl.ds(col, ROWS)]
    for t in range(8):
        src = dq_ref.at[pl.ds(place.home_row(t), 64), :]
        columns.start(place.own != t, src, target, q_recv.at[place.own], place.in_column(t))
        pl.when(place.own == t)(pltpu.make_async_copy(src, target, local_sem.at[0]).start)

    for (d, copy), (_, mine) in zip(sib_copies, own_copies):
        @pl.when(x >= d)
        def _():
            mine.wait()
            copy.wait_recv()
            both = own[d].astype(F32) + sib[d].astype(F32)
            acc[d] = both
            snd[d] = both.astype(BF16)

    my_rows = pl.ds(pl.multiple_of(z * COLUMN, COLUMN), COLUMN)

    def finish(p, out_ref, total):
        done[...] = total.astype(BF16)
        for half in range(2):
            src = done.at[pl.ds(half * 256, 256), :]
            here = (place.ylo == half) & (core == place.ylo)
            copy = rcopy(src, out_ref, end_send.at[half], end_recv.at[p],
                         place.at(ylo=half, core=place.ylo))
            local = pltpu.make_async_copy(src, out_ref, local_sem.at[1])
            pl.when(here)(local.start)
            pl.when(jnp.logical_not(here))(copy.start)
            pl.when(here)(local.wait)
            pl.when(jnp.logical_not(here))(copy.wait_send)

    @pl.when(core == 0)
    def _():
        sends = Sends(send_sems)
        for d in (2, 1):
            sends.start(x >= d, snd.at[d], rx.at[d - 1], rx_recv.at[d - 1],
                        place.at(x=(x + 4 - d) % 4))
        for d in (1, 2):
            @pl.when(x + d <= 3)
            def _():
                rcopy(snd.at[d], rx.at[d - 1], send_sems.at[0], rx_recv.at[d - 1],
                      sibling).wait_recv()
                acc[0] += rx[d - 1].astype(F32)
        hop[...] = acc[0].astype(BF16)
        for d in (1, 3, 2):
            zz = (z + d) % 4
            src = hop.at[pl.ds(pl.multiple_of(zz * COLUMN, COLUMN), COLUMN), :]
            sends.start(None, src, rz.at[d - 1], rz_recv.at[d - 1], place.at(z=zz))
        total = acc[0, my_rows, :]
        for d in (1, 3, 2):
            rcopy(rz.at[d - 1], rz.at[d - 1], send_sems.at[0], rz_recv.at[d - 1],
                  sibling).wait_recv()
            total = total + rz[d - 1].astype(F32)
        finish(0, kg_ref, total)
        sends.finish()

    @pl.when(core == 1)
    def _():
        sends = Sends(send_sems)
        for e in (2, 1, 0):
            for d in (1, 3, 2):
                zz = (z + d) % 4
                src = snd.at[e, pl.ds(pl.multiple_of(zz * COLUMN, COLUMN), COLUMN), :]
                sends.start(x >= e, src, rzz.at[d - 1, e], rzz_recv.at[d - 1, e], place.at(z=zz))
        total = None
        for e in (2, 1, 0):
            @pl.when(x >= e)
            def _():
                part = acc[e, my_rows, :]
                for d in (1, 3, 2):
                    rcopy(rzz.at[d - 1, e], rzz.at[d - 1, e], send_sems.at[0],
                          rzz_recv.at[d - 1, e], sibling).wait_recv()
                    part = part + rzz[d - 1, e].astype(F32)
                if e == 0:
                    acc[0, my_rows, :] = part
                else:
                    hop[e * COLUMN:(e + 1) * COLUMN, :] = part.astype(BF16)
            if e > 0:
                sends.start(x >= e, hop.at[pl.ds(e * COLUMN, COLUMN), :], rx2.at[e - 1],
                            rx2_recv.at[e - 1], place.at(x=(x + 4 - e) % 4))
        for d in (1, 2):
            @pl.when(x + d <= 3)
            def _():
                rcopy(rx2.at[d - 1], rx2.at[d - 1], send_sems.at[0], rx2_recv.at[d - 1],
                      sibling).wait_recv()
                acc[0, my_rows, :] += rx2[d - 1].astype(F32)
        finish(1, vg_ref, acc[0, my_rows, :])
        sends.finish()

    for p, out_ref in ((0, kg_ref), (1, vg_ref)):
        here = (place.ylo == core) & (core == p)
        wait = rcopy(done.at[pl.ds(0, 256), :], out_ref, end_send.at[0], end_recv.at[p], sibling)
        pl.when(jnp.logical_not(here))(wait.wait_recv)
    for t in range(8):
        @pl.when(place.own != t)
        def _():
            src = dq_ref.at[pl.ds(0, 64), :]
            rcopy(src, qg_ref.at[:, pl.ds(t * ROWS, ROWS)], col_send.at[0], q_recv.at[t],
                  sibling).wait_recv()
    pltpu.make_async_copy(dq_ref.at[pl.ds(0, 64), :], target, local_sem.at[0]).wait()
    columns.finish()
    for d, copy in sib_copies:
        pl.when(x >= d)(copy.wait_send)


ANY = pl.BlockSpec(memory_space=pl.ANY)
VMEM = pl.BlockSpec(memory_space=pltpu.VMEM)
SMEM = pl.BlockSpec(memory_space=pltpu.SMEM)
DMA = pltpu.SemaphoreType.DMA
MIB = 1 << 20


def struct(shape, dtype):
    return jax.ShapeDtypeStruct(shape, dtype)


def spread(q, do, o, k, v):
    return pl.pallas_call(
        spread_kernel,
        out_shape=(struct((COLUMN, ROWS), BF16), struct((COLUMN, ROWS), BF16),
                   struct((8, 8, 128), F32), struct((2, TOKENS, D), BF16)),
        in_specs=[ANY, VMEM, VMEM, ANY, ANY],
        out_specs=(ANY, ANY, ANY, ANY),
        scratch_shapes=[
            pltpu.VMEM((8, 8, 128), F32),
            DMA((24,)), DMA((8,)), DMA((8,)), DMA((8,)), DMA((4,)),
            DMA((2,)), DMA((2,)), DMA((32,)), DMA((16,)), DMA((16,)),
        ],
        compiler_params=pltpu.CompilerParams(
            collective_id=0, has_side_effects=True, vmem_limit_bytes=60 * MIB),
        name="spread",
    )(q, do, o, k, v)


def grads(parents, seg, q, do, dg, kv):
    return pl.pallas_call(
        grad_kernel,
        out_shape=(struct((2, NEAR, SECTION, D), BF16), struct((COLUMN, ROWS), BF16)),
        in_specs=[SMEM, VMEM, ANY, ANY, VMEM, ANY],
        out_specs=(ANY, VMEM),
        scratch_shapes=[
            pltpu.VMEM((2, NEAR * SECTION, D), F32),
            pltpu.VMEM((SLOTS * GROUP * BLOCK, ROWS), F32),
            pltpu.VMEM((2, NEAR * SECTION, D), BF16),
            pltpu.VMEM((2, NEAR * SECTION, D), BF16),
            pltpu.VMEM((COLUMN, ROWS), BF16),
            pltpu.VMEM((COLUMN, ROWS), BF16),
            pltpu.VMEM((4 * ROWS, D), BF16),
            pltpu.VMEM((4 * ROWS, D), BF16),
            pltpu.VMEM((SLOTS * 8, ROWS), F32),
            pltpu.VMEM((16, ROWS), F32),
            pltpu.VMEM((16, ROWS), F32),
            pltpu.VMEM((4 * D, ROWS), F32),
            pltpu.SMEM((256,), jnp.int32),
            DMA((2,)), DMA((2, NEAR)), DMA((2, NEAR)),
        ],
        compiler_params=pltpu.CompilerParams(vmem_limit_bytes=60 * MIB),
        name="grads",
    )(parents, seg, q, do, dg, kv)


def home(dkv, dq):
    return pl.pallas_call(
        home_kernel,
        out_shape=(struct((64, 4096), BF16), struct((256, D), BF16), struct((256, D), BF16)),
        in_specs=[ANY, ANY],
        out_specs=(ANY, ANY, ANY),
        scratch_shapes=[
            pltpu.VMEM((NEAR, SECTION, D), BF16),
            pltpu.VMEM((NEAR, SECTION, D), BF16),
            pltpu.VMEM((NEAR, SECTION, D), F32),
            pltpu.VMEM((NEAR, SECTION, D), BF16),
            pltpu.VMEM((SECTION, D), BF16),
            pltpu.VMEM((2, SECTION, D), BF16),
            pltpu.VMEM((3, COLUMN, D), BF16),
            pltpu.VMEM((3, NEAR, COLUMN, D), BF16),
            pltpu.VMEM((2, COLUMN, D), BF16),
            pltpu.VMEM((COLUMN, D), BF16),
            DMA((8,)), DMA((8,)), DMA((2,)), DMA((3,)), DMA((3,)), DMA((3,)),
            DMA((12,)), DMA((2,)), DMA((3,)), DMA((3, 3)), DMA((2,)), DMA((2,)), DMA((2,)),
        ],
        compiler_params=pltpu.CompilerParams(
            collective_id=1, has_side_effects=True, vmem_limit_bytes=60 * MIB),
        name="home",
    )(dkv, dq)


def hand_over_kernel(*refs):
    copies = []
    for n in range(3):
        src, dst = refs[n], refs[3 + n]
        rows = src.shape[0] // 4
        for i in range(4):
            at = pl.ds(i * rows, rows)
            copies.append(pltpu.make_async_copy(src.at[at, :], dst.at[at, :], refs[6].at[n, i]))
    for copy in copies:
        copy.start()
    for copy in copies:
        copy.wait()


def hand_over(*arrays):
    return pl.pallas_call(
        hand_over_kernel,
        out_shape=tuple(struct(a.shape, a.dtype) for a in arrays),
        in_specs=[ANY] * 3,
        out_specs=(ANY,) * 3,
        scratch_shapes=[DMA((3, 4))],
        compiler_params=pltpu.CompilerParams(vmem_limit_bytes=60 * MIB),
        name="hand_over",
    )(*arrays)


def local(query_rows, key_rows, value_rows, attn_output, out_grad, segments, parents):
    q, do, dg, kv = spread(query_rows, out_grad, attn_output, key_rows, value_rows)
    dkv, dq = grads(parents, segments.reshape(64, 128), q, do, dg, kv)
    return hand_over(*home(dkv, dq))


def solution(mesh):
    placed = (
        P(("ctx", "head"), None),
        P("ctx", "head"),
        P("ctx", "head"),
        P(("ctx", "head"), None),
        P(("ctx", "head"), None),
        P(),
        P(),
    )
    return jax.shard_map(
        local,
        mesh=mesh,
        in_specs=placed,
        out_specs=(P(("ctx", "head"), None), P("ctx", "head"), P("ctx", "head")),
        check_vma=False,
    )
```

```python
import functools
import math

import jax
import jax.numpy as jnp
from jax import lax
from jax.experimental import pallas as pl
from jax.experimental.pallas import tpu as pltpu
from jax.sharding import PartitionSpec as P

D = 128
BLOCK = 128
TOKENS = 8192
COLUMN = 512
SECTION = 2048
NEAR = 3
FAR_FIRST = (2, 1, 3, 0)
GROUP = 4
SCORES_AT_ONCE = 4
GRADS_AT_ONCE = 2
SLOTS = 26
ROWS = 512
SCALE = 1.0 / math.sqrt(D)
LOG2E = math.log2(math.e)
NEG = -1e30
F32 = jnp.float32
BF16 = jnp.bfloat16
MESH = pl.DeviceIdType.MESH
NT = (((1,), (1,)), ((), ()))
TN = (((0,), (0,)), ((), ()))


class Place:
    def __init__(self):
        ctx = lax.axis_index("ctx")
        head = lax.axis_index("head")
        self.x = ctx // 8
        self.z = (ctx // 2) % 4
        self.ylo = ctx % 2
        self.yhi = head // 2
        self.core = head % 2
        self.y = self.yhi * 2 + self.ylo

    def at(self, x=None, z=None, ylo=None, yhi=None, core=None):
        x = self.x if x is None else x
        z = self.z if z is None else z
        ylo = self.ylo if ylo is None else ylo
        yhi = self.yhi if yhi is None else yhi
        core = self.core if core is None else core
        return ((x * 4 + z) * 2 + ylo, yhi * 2 + core)

    def in_column(self, t):
        return self.at(ylo=(t // 2) % 2, yhi=t // 4, core=t % 2)

    @property
    def own(self):
        return self.y * 2 + self.core

    def home_row(self, t=None):
        if t is None:
            return (self.ylo * 2 + self.yhi) * 128 + self.core * 64
        return (((t // 2) % 2) * 2 + t // 4) * 128 + (t % 2) * 64


def greet(place):
    barrier = pltpu.get_barrier_semaphore()
    for t in range(8):
        @pl.when(place.own != t)
        def _():
            pl.semaphore_signal(barrier, inc=1, device_id=place.in_column(t), device_id_type=MESH)
    for step in range(1, 4):
        pl.semaphore_signal(
            barrier, inc=1, device_id=place.at(x=(place.x + step) % 4), device_id_type=MESH)
        pl.semaphore_signal(
            barrier, inc=1, device_id=place.at(z=(place.z + step) % 4), device_id_type=MESH)
    pl.semaphore_wait(barrier, 13)


def rcopy(src, dst, send, recv, device):
    return pltpu.make_async_remote_copy(
        src_ref=src, dst_ref=dst, send_sem=send, recv_sem=recv,
        device_id=device, device_id_type=MESH)


class Sends:
    def __init__(self, sems):
        self.sems = sems
        self.items = []

    def start(self, cond, src, dst, recv, device):
        copy = rcopy(src, dst, self.sems.at[len(self.items)], recv, device)
        self.items.append((cond, copy))
        if cond is None:
            copy.start()
        else:
            pl.when(cond)(copy.start)

    def finish(self):
        for cond, copy in self.items:
            if cond is None:
                copy.wait_send()
            else:
                pl.when(cond)(copy.wait_send)


def spread_kernel(q_ref, do_ref, o_ref, k_ref, v_ref, seg_ref, parents_ref,
                  qg_ref, dog_ref, dg_ref, kv_ref, seg_near, parents_near,
                  do_near, o_near, near_sem, dsrc, col_send, q_recv, do_recv, d_recv, local_sem,
                  first_send, first_recv, piece_send, prim_recv, sib_recv):
    place = Place()
    x, z, core = place.x, place.z, place.core
    nears = [pltpu.make_async_copy(do_ref, do_near, near_sem.at[0]),
             pltpu.make_async_copy(o_ref, o_near, near_sem.at[1]),
             pltpu.make_async_copy(seg_ref, seg_near, near_sem.at[2]),
             pltpu.make_async_copy(parents_ref, parents_near, near_sem.at[3])]
    for copy in nears:
        copy.start()
    greet(place)

    first_row = pl.multiple_of((x * 4 + z) * COLUMN + place.ylo * 256, 256)
    firsts = []
    for p, src in ((0, k_ref), (1, v_ref)):
        dst = kv_ref.at[p, pl.ds(first_row, 256), :]
        here = (place.ylo == core) & (core == p)
        away = jnp.logical_not(here)
        copy = rcopy(src, dst, first_send.at[p], first_recv.at[place.ylo],
                     place.at(ylo=core, core=p))
        local = pltpu.make_async_copy(src, dst, local_sem.at[3])
        pl.when(away)(copy.start)
        pl.when(here)(local.start)
        firsts.append((here, away, copy, local))

    my_row = pl.multiple_of(place.home_row(), 64)
    columns = Sends(col_send)
    locals_ = []
    for away in (4, 5, 2, 3, 6, 7, 1, 0):
        t = ((place.y + away // 2) % 4) * 2 + (core + away) % 2
        cols = pl.ds(pl.multiple_of(t * ROWS, ROWS), ROWS)
        for n, (src, dst, recv) in enumerate(
                ((q_ref, qg_ref, q_recv), (do_ref, dog_ref, do_recv))):
            target = dst.at[pl.ds(my_row, 64), :]
            if away:
                columns.start(None, src.at[:, cols], target, recv.at[place.own],
                              place.in_column(t))
            else:
                local = pltpu.make_async_copy(src.at[:, cols], target, local_sem.at[n])
                local.start()
                locals_.append((None, local))

    lane = lax.broadcasted_iota(jnp.int32, (8, 128), 1)
    line = lax.broadcasted_iota(jnp.int32, (8, 128), 0)
    mine = (lane // 64) == core
    ones = jnp.ones((8, D), BF16)
    for copy in nears:
        copy.wait()
    for t in range(8):
        tile = jnp.zeros((8, 128), F32)
        for r in range(4):
            cols = slice((t * 4 + r) * D, (t * 4 + r + 1) * D)
            prod = do_near[:, cols].astype(F32) * o_near[:, cols].astype(F32)
            high = prod.astype(BF16)
            low = (prod - high.astype(F32)).astype(BF16)
            row = (lax.dot_general(ones, high, NT, preferred_element_type=F32)
                   + lax.dot_general(ones, low, NT, preferred_element_type=F32))
            row = jnp.concatenate([row, row], axis=1)
            tile = jnp.where(mine & (line == r), row, tile)
        dsrc[t] = tile
    for t in range(8):
        target = dg_ref.at[place.own]
        columns.start(place.own != t, dsrc.at[t], target, d_recv.at[place.own],
                      place.in_column(t))
        local = pltpu.make_async_copy(dsrc.at[t], target, local_sem.at[2])
        pl.when(place.own == t)(local.start)
        locals_.append((place.own == t, local))

    for half in range(2):
        here = (place.ylo == core) & (place.ylo == half)
        wait = rcopy(k_ref, kv_ref.at[core, pl.ds(0, 256), :], first_send.at[0],
                     first_recv.at[half], place.at(core=1 - core))
        pl.when(jnp.logical_not(here))(wait.wait_recv)
    for here, away, copy, local in firsts:
        pl.when(here)(local.wait)

    def piece(p, xx, zz):
        return kv_ref.at[p, pl.ds(pl.multiple_of((xx * 4 + zz) * COLUMN, COLUMN), COLUMN), :]

    sibling = place.at(core=1 - core)

    def run(c):
        sends = Sends(piece_send)

        def share(cond, xx, zz):
            part = piece(c, xx, zz)
            sends.start(cond, part, part, sib_recv.at[xx * 4 + zz], sibling)

        def along_x(cond, xx, zz):
            part = piece(c, xx, zz)
            for d in (1, 2):
                ok = x + d <= 3
                ok = ok if cond is None else ok & cond
                sends.start(ok, part, part, prim_recv.at[xx * 4 + zz],
                            place.at(x=(x + d) % 4))

        def along_z(cond, xx, zz):
            part = piece(c, xx, zz)
            for d in (1, 3, 2):
                sends.start(cond, part, part, prim_recv.at[xx * 4 + zz],
                            place.at(z=(z + d) % 4))

        def arrive(cond, xx, zz):
            part = piece(c, xx, zz)
            wait = rcopy(part, part, piece_send.at[0], prim_recv.at[xx * 4 + zz], sibling)
            if cond is None:
                wait.wait_recv()
            else:
                pl.when(cond)(wait.wait_recv)

        if c == 0:
            along_z(None, x, z)
            along_x(None, x, z)
            share(None, x, z)
            for dz in (1, 3, 2):
                zz = (z + dz) % 4
                arrive(None, x, zz)
                along_x(None, x, zz)
                share(None, x, zz)
            for dz in (0, 1, 3, 2):
                zz = (z + dz) % 4
                for d in (1, 2):
                    xx = (x + 4 - d) % 4
                    arrive(x >= d, xx, zz)
                    share(x >= d, xx, zz)
        else:
            along_x(None, x, z)
            along_z(None, x, z)
            share(None, x, z)
            for d in (1, 2):
                xx = (x + 4 - d) % 4
                arrive(x >= d, xx, z)
                along_z(x >= d, xx, z)
                share(x >= d, xx, z)
            for d in range(NEAR):
                xx = (x + 4 - d) % 4
                for dz in (1, 3, 2):
                    zz = (z + dz) % 4
                    arrive(None if d == 0 else x >= d, xx, zz)
                    share(None if d == 0 else x >= d, xx, zz)
        for d in range(NEAR):
            xx = (x + 4 - d) % 4
            for zz in range(4):
                part = piece(1 - c, xx, zz)
                wait = rcopy(part, part, piece_send.at[0], sib_recv.at[xx * 4 + zz], sibling)
                pl.when(x >= d)(wait.wait_recv)
        sends.finish()

    pl.when(core == 0)(lambda: run(0))
    pl.when(core == 1)(lambda: run(1))

    for t in range(8):
        @pl.when(place.own != t)
        def _():
            row = place.home_row(t)
            for src, dst, recv in ((q_ref, qg_ref, q_recv), (do_ref, dog_ref, do_recv)):
                rcopy(src.at[:, pl.ds(0, ROWS)], dst.at[pl.ds(row, 64), :], col_send.at[0],
                      recv.at[t], place.in_column(t)).wait_recv()
            rcopy(dsrc.at[t], dg_ref.at[t], col_send.at[0], d_recv.at[t],
                  place.in_column(t)).wait_recv()
    for cond, local in locals_:
        if cond is None:
            local.wait()
        else:
            pl.when(cond)(local.wait)
    columns.finish()
    for here, away, copy, local in firsts:
        pl.when(away)(copy.wait_send)


def grad_kernel(parents_near, seg_ref, q_all, do_all, dg_ref, kv,
                dkv_ref, dq_ref,
                acc, expd, qr, dor, tops, cuts, inv, dqt, chain,
                parents_ref, parents_sem):
    place = Place()
    x = place.x
    column = x * 4 + place.z
    first_block = (x - (NEAR - 1)) * (SECTION // BLOCK)
    factor = SCALE * LOG2E

    parents_copy = pltpu.make_async_copy(parents_near, parents_ref, parents_sem)
    parents_copy.start()
    n0 = jnp.sum((seg_ref[...] == 0).astype(jnp.int32))

    parents_copy.wait()

    chains = [None] * 4
    free = jnp.int32(0)
    for qb in (3, 2, 1, 0):
        gb = column * 4 + qb
        lowest = jnp.where(gb * BLOCK >= n0, n0, 0)
        if qb == 3:
            shared = jnp.bool_(False)
        else:
            base, count, low = chains[qb + 1]
            shared = (parents_ref[gb + 1] == gb) & (low == lowest)

        def more(state):
            b, n = state
            return (b >= 0) & (b * BLOCK + (BLOCK - 1) >= lowest)

        def note(state):
            b, n = state
            chain[n] = b
            return (parents_ref[b], n + 1)

        _, stop = lax.while_loop(more, note, (jnp.where(shared, -1, gb), free))
        own = (free, stop - free, lowest)
        if qb < 3:
            own = (jnp.where(shared, base + 1, free), jnp.where(shared, count - 1, stop - free), lowest)
        chains[qb] = own
        free = stop

    for slot in range(NEAR):
        @pl.when(x >= 2 - slot)
        def _():
            for p in range(2):
                acc[p, slot * SECTION:(slot + 1) * SECTION, :] = jnp.zeros((SECTION, D), F32)
    dqt[...] = jnp.zeros_like(dqt)

    for qb in range(4):
        for h in range(4):
            rows, cols = slice(qb * BLOCK, (qb + 1) * BLOCK), slice(h * D, (h + 1) * D)
            qr[qb * ROWS + h * D:qb * ROWS + (h + 1) * D, :] = q_all[rows, cols]
            dor[qb * ROWS + h * D:qb * ROWS + (h + 1) * D, :] = do_all[rows, cols]

    def block_rows(b):
        return pl.ds(pl.multiple_of((b - first_block) * BLOCK, BLOCK), BLOCK)

    def gathered(p, blocks):
        return jnp.concatenate(
            [kv[p, pl.ds(pl.multiple_of(b * BLOCK, BLOCK), BLOCK), :] for b in blocks], axis=0)

    def row_of(q):
        return pl.ds(pl.multiple_of(q * 8, 8), 1)

    def lines_of(q):
        return pl.ds(pl.multiple_of(q * 8, 8), 8)

    def rows_of(qb):
        return pl.ds(pl.multiple_of(qb * ROWS, ROWS), ROWS)

    def fold(e):
        return jnp.sum(e.reshape(-1, 8, ROWS), axis=0)

    def one_half(half, carry):
        def pick(even, odd):
            return jnp.where(half == 0, even, odd)

        bases = [pick(chains[q][0], chains[q + 2][0]) for q in range(2)]
        counts = [pick(chains[q][1], chains[q + 2][1]) for q in range(2)]
        lows = [pick(chains[q][2], chains[q + 2][2]) for q in range(2)]
        starts = [(column * 4 + half * 2 + q) * BLOCK for q in range(2)]
        steps = [(counts[q] + GROUP - 1) // GROUP - 1 for q in range(2)]
        items = steps[0] + steps[1]

        def blocks_of(q, g):
            base = jnp.where(q == 0, bases[0], bases[1])
            count = jnp.where(q == 0, counts[0], counts[1])
            diagonal = column * 4 + half * 2 + q
            blocks, real = [], []
            for i in range(GROUP):
                at = g * GROUP + i
                here = at < count
                index = base + jnp.where(at == 0, 0, jnp.where(at == 1, count - 1, at - 1))
                blocks.append(jnp.where(here, chain[jnp.where(here, index, 0)], diagonal))
                real.append(here)
            return blocks, real

        def item(slot):
            t = slot - 2
            late = t >= steps[0]
            q = jnp.where(slot < 2, slot, late.astype(jnp.int32))
            g = jnp.where(slot < 2, 0, t - jnp.where(late, steps[0], 0) + 1)
            return q, g

        def expd_rows(slot, i=0, n=GROUP):
            return pl.ds(pl.multiple_of(slot * GROUP * BLOCK + i * BLOCK, BLOCK), n * BLOCK)

        def masked_scores(q, g):
            blocks, real = blocks_of(q, g)
            start = (column * 4 + half * 2 + q) * BLOCK
            query_at = start + lax.broadcasted_iota(jnp.int32, (1, ROWS), 1) % BLOCK
            least = jnp.where(query_at >= n0, n0, 0)
            scores = lax.dot_general(gathered(0, blocks), qr[rows_of(half * 2 + q), :], NT,
                                     preferred_element_type=F32)
            parts = []
            for i in range(GROUP):
                first = jnp.where(real[i], blocks[i] * BLOCK, 2 * TOKENS)
                key_at = first + lax.broadcasted_iota(jnp.int32, (BLOCK, ROWS), 0)
                ok = (key_at <= query_at) & (key_at >= least)
                parts.append(jnp.where(ok, scores[i * BLOCK:(i + 1) * BLOCK, :], NEG))
            return jnp.concatenate(parts, axis=0)

        for q in range(2):
            scores = masked_scores(q, 0)
            top = jnp.max(scores, axis=0, keepdims=True)
            e = jnp.exp2((scores - top) * factor)
            expd[expd_rows(q), :] = e
            inv[lines_of(q), :] = fold(e)
            query_at = starts[q] + lax.broadcasted_iota(jnp.int32, (1, ROWS), 1) % BLOCK
            cut = jnp.where((query_at >= n0) & (starts[q] < n0), -NEG, 0.0)
            cuts[lines_of(q), :] = jnp.broadcast_to(top + cut, (8, ROWS))

        def scores_turn(n, c):
            for u in range(SCORES_AT_ONCE):
                slot = 2 + n * SCORES_AT_ONCE + u
                q, g = item(slot)
                blocks, real = blocks_of(q, g)
                scores = lax.dot_general(gathered(0, blocks), qr[rows_of(half * 2 + q), :], NT,
                                         preferred_element_type=F32)
                top = cuts[row_of(q), :]
                sums = None
                for i in range(GROUP):
                    away = top + jnp.where(real[i], 0.0, -NEG)
                    e = jnp.exp2((scores[i * BLOCK:(i + 1) * BLOCK, :] - away) * factor)
                    expd[expd_rows(slot, i, 1), :] = e
                    sums = fold(e) if sums is None else sums + fold(e)
                inv[lines_of(q), :] += sums
            return c

        lax.fori_loop(0, (items + SCORES_AT_ONCE - 1) // SCORES_AT_ONCE, scores_turn, 0)
        totals = [jnp.sum(inv[q * 8:(q + 1) * 8, :], axis=0, keepdims=True) for q in range(2)]
        safe = jnp.max(jnp.maximum(totals[0], totals[1])) < 1e30
        for q in range(2):
            inv[q * 8:(q + 1) * 8, :] = jnp.broadcast_to(1.0 / totals[q], (8, ROWS))

        @pl.when(jnp.logical_not(safe))
        def _():
            cuts[...] = jnp.full_like(cuts, NEG)
            inv[...] = jnp.zeros_like(inv)

            def again(slot, c):
                q, g = item(slot)
                scores = masked_scores(q, g)
                top, total = cuts[row_of(q), :], inv[row_of(q), :]
                new_top = jnp.maximum(top, jnp.max(scores, axis=0, keepdims=True))
                e = jnp.exp2((scores - new_top) * factor)
                expd[expd_rows(slot), :] = e
                total = total * jnp.exp2((top - new_top) * factor) + jnp.sum(
                    e, axis=0, keepdims=True)
                cuts[lines_of(q), :] = jnp.broadcast_to(new_top, (8, ROWS))
                tops[lines_of(slot), :] = jnp.broadcast_to(new_top, (8, ROWS))
                inv[lines_of(q), :] = jnp.broadcast_to(total, (8, ROWS))
                return c

            def settle(slot, c):
                q, g = item(slot)
                share = jnp.exp2((tops[row_of(slot), :] - cuts[row_of(q), :]) * factor)
                expd[expd_rows(slot), :] = expd[expd_rows(slot), :] * (share / inv[row_of(q), :])
                return c

            lax.fori_loop(0, items + 2, again, 0)
            lax.fori_loop(0, items + 2, settle, 0)
            inv[...] = jnp.ones_like(inv)

        def grads_turn(n, c):
            work = []
            for u in range(GRADS_AT_ONCE):
                slot = n * GRADS_AT_ONCE + u
                q, g = item(slot)
                blocks, _ = blocks_of(q, g)
                do_rows = dor[rows_of(half * 2 + q), :]
                weight_grad = lax.dot_general(gathered(1, blocks), do_rows, NT,
                                              preferred_element_type=F32)
                work.append((slot, q, blocks, do_rows, weight_grad))
            for slot, q, blocks, do_rows, weight_grad in work:
                qb = half * 2 + q
                source = ((qb % 2) * 2 + qb // 2) * 2
                pair = dg_ref[source] + dg_ref[source + 1]
                out_dot = jnp.concatenate([pair[h:h + 1, :] for h in range(4)], axis=1)
                weights = expd[expd_rows(slot), :] * inv[row_of(q), :]
                halved = weights.astype(BF16)
                score_grad = (weights * (weight_grad - out_dot)).astype(BF16)
                dv = jnp.dot(halved, do_rows, preferred_element_type=F32)
                dk = jnp.dot(score_grad, qr[rows_of(qb), :], preferred_element_type=F32)
                into = pl.ds(pl.multiple_of(qb * D, D), D)
                dqt[into, :] += lax.dot_general(gathered(0, blocks), score_grad, TN,
                                                preferred_element_type=F32)
                for i, b in enumerate(blocks):
                    rows = block_rows(b)
                    acc[0, rows, :] += dk[i * BLOCK:(i + 1) * BLOCK, :]
                    acc[1, rows, :] += dv[i * BLOCK:(i + 1) * BLOCK, :]
            return c

        lax.fori_loop(0, (items + 2 + GRADS_AT_ONCE - 1) // GRADS_AT_ONCE, grads_turn, 0)
        return carry

    lax.fori_loop(0, 2, one_half, 0)

    for slot in range(NEAR):
        @pl.when(x >= 2 - slot)
        def _():
            for p, by in ((0, SCALE), (1, 1.0)):
                at = slice(slot * SECTION, (slot + 1) * SECTION)
                dkv_ref[p, slot] = (acc[p, at, :] * by).astype(BF16)
    for qb in range(4):
        for h in range(4):
            part = dqt[qb * D:(qb + 1) * D, h * D:(h + 1) * D].T * SCALE
            dq_ref[qb * BLOCK:(qb + 1) * BLOCK, h * D:(h + 1) * D] = part.astype(BF16)


def home_kernel(dkv_ref, dq_ref,
                qg_ref, kg_ref, vg_ref,
                sib, acc, snd, hop, rx, rz, rzz, rx2, done,
                col_send, q_recv, local_sem, sib_send, sib_recv,
                send_sems, rx_recv, rz_recv, rzz_recv, rx2_recv, end_send, end_recv):
    place = Place()
    x, z, core = place.x, place.z, place.core
    greet(place)
    sibling = place.at(core=1 - core)

    def rows_at(dz):
        return pl.ds(pl.multiple_of(((z + dz) % 4) * COLUMN, COLUMN), COLUMN)

    def share(p):
        order = [(d, dz) for dz in FAR_FIRST for d in (2, 1, 0)]
        if p == 1:
            order = [(d, dz) for d in (2, 1, 0) for dz in FAR_FIRST]
        copies = []
        for d, dz in order:
            copy = rcopy(dkv_ref.at[p, 2 - d, rows_at(dz), :], sib.at[d, rows_at(dz), :],
                         sib_send.at[d, dz], sib_recv.at[d, dz], sibling)
            pl.when(x >= d)(copy.start)
            copies.append((d, copy))
        return copies

    pl.when(core == 1)(lambda: share(0) and None)
    pl.when(core == 0)(lambda: share(1) and None)

    columns = Sends(col_send)
    col = pl.multiple_of(place.own * ROWS, ROWS)
    target = qg_ref.at[:, pl.ds(col, ROWS)]
    for away in (4, 5, 2, 3, 6, 7, 1):
        t = ((place.y + away // 2) % 4) * 2 + (core + away) % 2
        src = dq_ref.at[pl.ds(pl.multiple_of(place.home_row(t), 64), 64), :]
        columns.start(None, src, target, q_recv.at[place.own], place.in_column(t))
    src = dq_ref.at[pl.ds(pl.multiple_of(place.home_row(), 64), 64), :]
    stay = pltpu.make_async_copy(src, target, local_sem.at[0])
    stay.start()

    def both(p, d, dz):
        part = sib.at[d, rows_at(dz), :]
        rcopy(part, part, sib_send.at[d, dz], sib_recv.at[d, dz], sibling).wait_recv()
        return dkv_ref[p, 2 - d, rows_at(dz), :].astype(F32) + part[...].astype(F32)

    def arrived(ref, sem):
        rcopy(ref, ref, send_sems.at[0], sem, sibling).wait_recv()
        return ref[...].astype(F32)

    def finish(p, out_ref, total):
        done[...] = total.astype(BF16)
        for half in range(2):
            src = done.at[pl.ds(half * 256, 256), :]
            here = (place.ylo == half) & (core == place.ylo)
            copy = rcopy(src, out_ref, end_send.at[half], end_recv.at[p],
                         place.at(ylo=half, core=place.ylo))
            local = pltpu.make_async_copy(src, out_ref, local_sem.at[1])
            pl.when(here)(local.start)
            pl.when(jnp.logical_not(here))(copy.start)
            pl.when(here)(local.wait)
            pl.when(jnp.logical_not(here))(copy.wait_send)

    def keys_home():
        sends = Sends(send_sems)
        for dz in FAR_FIRST:
            for d in (2, 1):
                @pl.when(x >= d)
                def _():
                    snd[d, rows_at(dz), :] = both(0, d, dz).astype(BF16)
                sends.start(x >= d, snd.at[d, rows_at(dz), :], rx.at[d - 1, rows_at(dz), :],
                            rx_recv.at[d - 1, dz], place.at(x=(x + 4 - d) % 4))
            acc[0, rows_at(dz), :] = both(0, 0, dz)
        for dz in FAR_FIRST:
            for d in (1, 2):
                @pl.when(x + d <= 3)
                def _():
                    acc[0, rows_at(dz), :] += arrived(rx.at[d - 1, rows_at(dz), :],
                                                      rx_recv.at[d - 1, dz])
            if dz:
                hop[rows_at(dz), :] = acc[0, rows_at(dz), :].astype(BF16)
                sends.start(None, hop.at[rows_at(dz), :], rz.at[dz - 1], rz_recv.at[dz - 1],
                            place.at(z=(z + dz) % 4))
        total = acc[0, rows_at(0), :]
        for dz in (1, 3, 2):
            total = total + arrived(rz.at[dz - 1], rz_recv.at[dz - 1])
        finish(0, kg_ref, total)
        sends.finish()

    def values_home():
        sends = Sends(send_sems)
        for d in (2, 1, 0):
            for dz in (2, 1, 3):
                @pl.when(x >= d)
                def _():
                    snd[d, rows_at(dz), :] = both(1, d, dz).astype(BF16)
                sends.start(x >= d, snd.at[d, rows_at(dz), :], rzz.at[dz - 1, d],
                            rzz_recv.at[dz - 1, d], place.at(z=(z + dz) % 4))

            @pl.when(x >= d)
            def _():
                acc[d, rows_at(0), :] = both(1, d, 0)
        for d in (2, 1, 0):
            @pl.when(x >= d)
            def _():
                part = acc[d, rows_at(0), :]
                for dz in (1, 3, 2):
                    part = part + arrived(rzz.at[dz - 1, d], rzz_recv.at[dz - 1, d])
                if d == 0:
                    acc[0, rows_at(0), :] = part
                else:
                    hop[d * COLUMN:(d + 1) * COLUMN, :] = part.astype(BF16)
            if d > 0:
                sends.start(x >= d, hop.at[pl.ds(d * COLUMN, COLUMN), :], rx2.at[d - 1],
                            rx2_recv.at[d - 1], place.at(x=(x + 4 - d) % 4))
        for d in (1, 2):
            @pl.when(x + d <= 3)
            def _():
                acc[0, rows_at(0), :] += arrived(rx2.at[d - 1], rx2_recv.at[d - 1])
        finish(1, vg_ref, acc[0, rows_at(0), :])
        sends.finish()

    pl.when(core == 0)(keys_home)
    pl.when(core == 1)(values_home)

    for p, out_ref in ((0, kg_ref), (1, vg_ref)):
        here = (place.ylo == core) & (core == p)
        wait = rcopy(done.at[pl.ds(0, 256), :], out_ref, end_send.at[0], end_recv.at[p], sibling)
        pl.when(jnp.logical_not(here))(wait.wait_recv)
    for t in range(8):
        @pl.when(place.own != t)
        def _():
            src = dq_ref.at[pl.ds(0, 64), :]
            rcopy(src, qg_ref.at[:, pl.ds(t * ROWS, ROWS)], col_send.at[0], q_recv.at[t],
                  sibling).wait_recv()
    stay.wait()
    columns.finish()
    for d in range(NEAR):
        for dz in range(4):
            part = dkv_ref.at[0, 2 - d, rows_at(dz), :]
            pl.when(x >= d)(rcopy(part, part, sib_send.at[d, dz], sib_recv.at[d, dz],
                                  sibling).wait_send)


ANY = pl.BlockSpec(memory_space=pl.ANY)
VMEM = pl.BlockSpec(memory_space=pltpu.VMEM)
HBM = pl.BlockSpec(memory_space=pltpu.HBM)
SMEM = pl.BlockSpec(memory_space=pltpu.SMEM)
DMA = pltpu.SemaphoreType.DMA
MIB = 1 << 20


def struct(shape, dtype):
    return jax.ShapeDtypeStruct(shape, dtype)


def spread(q, do, o, k, v, seg, parents):
    return pl.pallas_call(
        spread_kernel,
        out_shape=(pltpu.VMEM((COLUMN, ROWS), BF16), pltpu.VMEM((COLUMN, ROWS), BF16),
                   pltpu.VMEM((8, 8, 128), F32), pltpu.VMEM((2, TOKENS, D), BF16),
                   pltpu.VMEM((64, 128), jnp.int32), pltpu.VMEM((64,), jnp.int32)),
        in_specs=[HBM] * 7,
        out_specs=(VMEM,) * 6,
        scratch_shapes=[
            pltpu.VMEM((64, 4096), BF16), pltpu.VMEM((64, 4096), BF16), DMA((4,)),
            pltpu.VMEM((8, 8, 128), F32),
            DMA((24,)), DMA((8,)), DMA((8,)), DMA((8,)), DMA((4,)),
            DMA((2,)), DMA((2,)), DMA((32,)), DMA((16,)), DMA((16,)),
        ],
        compiler_params=pltpu.CompilerParams(
            collective_id=0, has_side_effects=True, vmem_limit_bytes=56 * MIB),
        name="spread",
    )(q, do, o, k, v, seg, parents)


def grads(parents, seg, q, do, dg, kv):
    return pl.pallas_call(
        grad_kernel,
        out_shape=(pltpu.VMEM((2, NEAR, SECTION, D), BF16), pltpu.VMEM((COLUMN, ROWS), BF16)),
        in_specs=[VMEM] * 6,
        out_specs=(VMEM, VMEM),
        scratch_shapes=[
            pltpu.VMEM((2, NEAR * SECTION, D), F32),
            pltpu.VMEM((SLOTS * GROUP * BLOCK, ROWS), F32),
            pltpu.VMEM((4 * ROWS, D), BF16),
            pltpu.VMEM((4 * ROWS, D), BF16),
            pltpu.VMEM((SLOTS * 8, ROWS), F32),
            pltpu.VMEM((16, ROWS), F32),
            pltpu.VMEM((16, ROWS), F32),
            pltpu.VMEM((4 * D, ROWS), F32),
            pltpu.SMEM((256,), jnp.int32), pltpu.SMEM((64,), jnp.int32), DMA,
        ],
        compiler_params=pltpu.CompilerParams(vmem_limit_bytes=38 * MIB),
        name="grads",
    )(parents, seg, q, do, dg, kv)


def home(dkv, dq):
    return pl.pallas_call(
        home_kernel,
        out_shape=(pltpu.VMEM((64, 4096), BF16), pltpu.VMEM((256, D), BF16),
                   pltpu.VMEM((256, D), BF16)),
        in_specs=[VMEM, VMEM],
        out_specs=(VMEM,) * 3,
        scratch_shapes=[
            pltpu.VMEM((NEAR, SECTION, D), BF16),
            pltpu.VMEM((NEAR, SECTION, D), F32),
            pltpu.VMEM((NEAR, SECTION, D), BF16),
            pltpu.VMEM((SECTION, D), BF16),
            pltpu.VMEM((2, SECTION, D), BF16),
            pltpu.VMEM((3, COLUMN, D), BF16),
            pltpu.VMEM((3, NEAR, COLUMN, D), BF16),
            pltpu.VMEM((2, COLUMN, D), BF16),
            pltpu.VMEM((COLUMN, D), BF16),
            DMA((8,)), DMA((8,)), DMA((2,)), DMA((3, 4)), DMA((3, 4)),
            DMA((16,)), DMA((2, 4)), DMA((3,)), DMA((3, 3)), DMA((2,)), DMA((2,)),
            DMA((2,)),
        ],
        compiler_params=pltpu.CompilerParams(
            collective_id=1, has_side_effects=True, vmem_limit_bytes=24 * MIB),
        name="home",
    )(dkv, dq)


def hand_over_kernel(*refs):
    copies = [pltpu.make_async_copy(refs[n], refs[3 + n], refs[6].at[n]) for n in range(3)]
    for copy in copies:
        copy.start()
    for copy in copies:
        copy.wait()


def hand_over(*arrays):
    return pl.pallas_call(
        hand_over_kernel,
        out_shape=tuple(struct(a.shape, a.dtype) for a in arrays),
        in_specs=[VMEM] * 3,
        out_specs=(HBM,) * 3,
        scratch_shapes=[DMA((3,))],
        compiler_params=pltpu.CompilerParams(vmem_limit_bytes=8 * MIB),
        name="hand_over",
    )(*arrays)


def local(query_rows, key_rows, value_rows, attn_output, out_grad, segments, parents):
    q, do, dg, kv, seg, parents = spread(
        query_rows, out_grad, attn_output, key_rows, value_rows, segments.reshape(64, 128), parents)
    dkv, dq = grads(parents, seg, q, do, dg, kv)
    return hand_over(*home(dkv, dq))


def solution(mesh):
    placed = (
        P(("ctx", "head"), None),
        P("ctx", "head"),
        P("ctx", "head"),
        P(("ctx", "head"), None),
        P(("ctx", "head"), None),
        P(),
        P(),
    )
    return jax.shard_map(
        local,
        mesh=mesh,
        in_specs=placed,
        out_specs=(P(("ctx", "head"), None), P("ctx", "head"), P("ctx", "head")),
        check_vma=False,
    )
```

```python
import functools
import math

import jax
import jax.numpy as jnp
from jax import lax
from jax.experimental import pallas as pl
from jax.experimental.pallas import tpu as pltpu
from jax.sharding import PartitionSpec as P

D = 128
BLOCK = 128
TOKENS = 8192
COLUMN = 512
SECTION = 2048
NEAR = 3
FAR_FIRST = (2, 1, 3, 0)
RELAYED = (0, 1)
GROUP = 4
SCORES_AT_ONCE = 4
GRADS_AT_ONCE = 2
SLOTS = 26
ROWS = 512
SCALE = 1.0 / math.sqrt(D)
LOG2E = math.log2(math.e)
NEG = -1e30
F32 = jnp.float32
BF16 = jnp.bfloat16
MESH = pl.DeviceIdType.MESH
NT = (((1,), (1,)), ((), ()))
TN = (((0,), (0,)), ((), ()))


class Place:
    def __init__(self):
        ctx = lax.axis_index("ctx")
        head = lax.axis_index("head")
        self.x = ctx // 8
        self.z = (ctx // 2) % 4
        self.ylo = ctx % 2
        self.yhi = head // 2
        self.core = head % 2
        self.y = self.yhi * 2 + self.ylo

    def at(self, x=None, z=None, ylo=None, yhi=None, core=None):
        x = self.x if x is None else x
        z = self.z if z is None else z
        ylo = self.ylo if ylo is None else ylo
        yhi = self.yhi if yhi is None else yhi
        core = self.core if core is None else core
        return ((x * 4 + z) * 2 + ylo, yhi * 2 + core)

    def in_column(self, t):
        return self.at(ylo=(t // 2) % 2, yhi=t // 4, core=t % 2)

    @property
    def own(self):
        return self.y * 2 + self.core

    def home_row(self, t=None):
        if t is None:
            return (self.ylo * 2 + self.yhi) * 128 + self.core * 64
        return (((t // 2) % 2) * 2 + t // 4) * 128 + (t % 2) * 64


def greet(place, homeward=False):
    barrier = pltpu.get_barrier_semaphore()
    for t in range(8):
        @pl.when(place.own != t)
        def _():
            pl.semaphore_signal(barrier, inc=1, device_id=place.in_column(t), device_id_type=MESH)
    for step in range(1, 4):
        pl.semaphore_signal(
            barrier, inc=1, device_id=place.at(x=(place.x + step) % 4), device_id_type=MESH)
        pl.semaphore_signal(
            barrier, inc=1, device_id=place.at(z=(place.z + step) % 4), device_id_type=MESH)
    if not homeward:
        pl.semaphore_wait(barrier, 13)
        return
    for step in range(1, 4):
        pl.semaphore_signal(
            barrier, inc=1, device_id=place.at(z=(place.z + step) % 4, ylo=place.core, core=0),
            device_id_type=MESH)
    for d in (1, 2):
        @pl.when(place.x + d <= 3)
        def _():
            pl.semaphore_signal(
                barrier, inc=1,
                device_id=place.at(x=(place.x + d) % 4, ylo=place.core, core=1),
                device_id_type=MESH)
    pl.semaphore_wait(barrier, 13 + jnp.where(place.core == 0, 6, 2 * jnp.minimum(place.x, 2)))


def rcopy(src, dst, send, recv, device):
    return pltpu.make_async_remote_copy(
        src_ref=src, dst_ref=dst, send_sem=send, recv_sem=recv,
        device_id=device, device_id_type=MESH)


class Sends:
    def __init__(self, sems):
        self.sems = sems
        self.items = []

    def start(self, cond, src, dst, recv, device):
        copy = rcopy(src, dst, self.sems.at[len(self.items)], recv, device)
        self.items.append((cond, copy))
        if cond is None:
            copy.start()
        else:
            pl.when(cond)(copy.start)

    def finish(self):
        for cond, copy in self.items:
            if cond is None:
                copy.wait_send()
            else:
                pl.when(cond)(copy.wait_send)


def spread_kernel(q_ref, do_ref, o_ref, k_ref, v_ref, seg_ref, parents_ref,
                  qg_ref, dog_ref, dg_ref, kv_ref, seg_near, parents_near,
                  do_near, o_near, near_sem, dsrc, col_send, q_recv, do_recv, d_recv, local_sem,
                  first_send, first_recv, piece_send, prim_recv, sib_recv, dot_send):
    place = Place()
    x, z, core = place.x, place.z, place.core
    nears = [pltpu.make_async_copy(do_ref, do_near, near_sem.at[0]),
             pltpu.make_async_copy(o_ref, o_near, near_sem.at[1]),
             pltpu.make_async_copy(seg_ref, seg_near, near_sem.at[2]),
             pltpu.make_async_copy(parents_ref, parents_near, near_sem.at[3])]
    for copy in nears:
        copy.start()
    greet(place)

    first_row = pl.multiple_of((x * 4 + z) * COLUMN + place.ylo * 256, 256)
    firsts = []
    for p, src in ((0, k_ref), (1, v_ref)):
        dst = kv_ref.at[p, pl.ds(first_row, 256), :]
        here = (place.ylo == core) & (core == p)
        away = jnp.logical_not(here)
        copy = rcopy(src, dst, first_send.at[p], first_recv.at[place.ylo],
                     place.at(ylo=core, core=p))
        local = pltpu.make_async_copy(src, dst, local_sem.at[3])
        pl.when(away)(copy.start)
        pl.when(here)(local.start)
        firsts.append((here, away, copy, local))

    my_row = pl.multiple_of(place.home_row(), 64)
    columns = Sends(col_send)
    locals_ = []

    def across(src, dst, recv, sem):
        target = dst.at[pl.ds(my_row, 64), :]
        for away in (4, 5, 2, 3, 6, 7, 1, 0):
            t = ((place.y + away // 2) % 4) * 2 + (core + away) % 2
            cols = pl.ds(pl.multiple_of(t * ROWS, ROWS), ROWS)
            if away:
                columns.start(None, src.at[:, cols], target, recv.at[place.own],
                              place.in_column(t))
            else:
                local = pltpu.make_async_copy(src.at[:, cols], target, sem)
                local.start()
                locals_.append(local)

    across(q_ref, qg_ref, q_recv, local_sem.at[0])

    lane = lax.broadcasted_iota(jnp.int32, (8, 128), 1)
    line = lax.broadcasted_iota(jnp.int32, (8, 128), 0)
    mine = (lane // 64) == core
    ones = jnp.ones((8, D), BF16)
    for copy in nears:
        copy.wait()
    for t in range(8):
        tile = jnp.zeros((8, 128), F32)
        for r in range(4):
            cols = slice((t * 4 + r) * D, (t * 4 + r + 1) * D)
            prod = do_near[:, cols].astype(F32) * o_near[:, cols].astype(F32)
            high = prod.astype(BF16)
            low = (prod - high.astype(F32)).astype(BF16)
            row = (lax.dot_general(ones, high, NT, preferred_element_type=F32)
                   + lax.dot_general(ones, low, NT, preferred_element_type=F32))
            row = jnp.concatenate([row, row], axis=1)
            tile = jnp.where(mine & (line == r), row, tile)
        dsrc[t] = tile
    dots = Sends(dot_send)
    target = dg_ref.at[place.own]
    for t in range(8):
        dots.start(place.own != t, dsrc.at[t], target, d_recv.at[place.own],
                   place.in_column(t))
    stay = pltpu.make_async_copy(dsrc.at[place.own], target, local_sem.at[2])
    stay.start()

    across(do_ref, dog_ref, do_recv, local_sem.at[1])

    for half in range(2):
        here = (place.ylo == core) & (place.ylo == half)
        wait = rcopy(k_ref, kv_ref.at[core, pl.ds(0, 256), :], first_send.at[0],
                     first_recv.at[half], place.at(core=1 - core))
        pl.when(jnp.logical_not(here))(wait.wait_recv)
    for here, away, copy, local in firsts:
        pl.when(here)(local.wait)

    def piece(p, xx, zz, half=None):
        start = pl.multiple_of((xx * 4 + zz) * COLUMN, COLUMN)
        if half is None:
            return kv_ref.at[p, pl.ds(start, COLUMN), :]
        return kv_ref.at[p, pl.ds(pl.multiple_of(start + half * 256, 256), 256), :]

    sibling = place.at(core=1 - core)

    def run(c):
        sends = Sends(piece_send)

        def share(cond, xx, zz):
            part = piece(c, xx, zz)
            sends.start(cond, part, part, sib_recv.at[xx * 4 + zz], sibling)

        def along_x(zz, dz):
            part = piece(c, x, zz)
            recv = prim_recv.at[x * 4 + zz, 0]
            sends.start(x <= 2, part, part, recv, place.at(x=(x + 1) % 4))
            step = 3 if c == 0 and dz in RELAYED else 2
            sends.start(x <= 1, part, part, recv, place.at(x=(x + step) % 4))

        def pass_on(dz):
            xx, zz = (x + 1) % 4, (z + dz) % 4
            between = (x == 0) | (x == 3)
            arrive(between, xx, zz)
            part = piece(c, xx, zz)
            sends.start(between, part, part, prim_recv.at[xx * 4 + zz, 0],
                        place.at(x=(x + 3) % 4))

        def along_z(cond, xx):
            part = piece(c, xx, z)
            for d in (1, 3, 2):
                sends.start(cond, part, part, prim_recv.at[xx * 4 + z, 0],
                            place.at(z=(z + d) % 4))

        def arrive(cond, xx, zz, halves=False):
            parts = [piece(c, xx, zz, h) for h in (0, 1)] if halves else [piece(c, xx, zz)]
            for h, part in enumerate(parts):
                wait = rcopy(part, part, piece_send.at[0], prim_recv.at[xx * 4 + zz, h], sibling)
                if cond is None:
                    wait.wait_recv()
                else:
                    pl.when(cond)(wait.wait_recv)

        if c == 0:
            along_z(None, x)
            along_x(z, 0)
            share(None, x, z)
            for dz in (1, 3, 2):
                zz = (z + dz) % 4
                arrive(None, x, zz)
                along_x(zz, dz)
                share(None, x, zz)
                if {1: 0, 3: 1, 2: 3}[dz] in RELAYED:
                    pass_on({1: 0, 3: 1, 2: 3}[dz])
            for dz in (0, 1, 3, 2):
                zz = (z + dz) % 4
                for d in (1, 2):
                    xx = (x + 4 - d) % 4
                    arrive(x >= d, xx, zz)
                    share(x >= d, xx, zz)
        else:
            along_x(z, 0)
            along_z(None, x)
            share(None, x, z)
            for d in (1, 2):
                xx = (x + 4 - d) % 4
                arrive(x >= d, xx, z)
                along_z(x >= d, xx)
                share(x >= d, xx, z)
            for dz in (1, 3, 2):
                zz = (z + dz) % 4
                for d in range(NEAR):
                    xx = (x + 4 - d) % 4
                    arrive(x >= d, xx, zz)
                    share(x >= d, xx, zz)
        for d in range(NEAR):
            xx = (x + 4 - d) % 4
            for zz in range(4):
                part = piece(1 - c, xx, zz)
                wait = rcopy(part, part, piece_send.at[0], sib_recv.at[xx * 4 + zz], sibling)
                pl.when(x >= d)(wait.wait_recv)
        sends.finish()

    pl.when(core == 0)(lambda: run(0))
    pl.when(core == 1)(lambda: run(1))

    for t in range(8):
        @pl.when(place.own != t)
        def _():
            row = place.home_row(t)
            for src, dst, recv in ((q_ref, qg_ref, q_recv), (do_ref, dog_ref, do_recv)):
                rcopy(src.at[:, pl.ds(0, ROWS)], dst.at[pl.ds(row, 64), :], col_send.at[0],
                      recv.at[t], place.in_column(t)).wait_recv()
    for local in locals_:
        local.wait()
    for t in range(8):
        pl.when(place.own != t)(rcopy(dsrc.at[t], dg_ref.at[t], dot_send.at[0], d_recv.at[t],
                                      place.in_column(t)).wait_recv)
    stay.wait()
    dots.finish()
    columns.finish()
    for here, away, copy, local in firsts:
        pl.when(away)(copy.wait_send)


def grad_kernel(parents_near, seg_ref, q_all, do_all, dg_ref, kv,
                dkv_ref, dq_ref,
                acc, expd, qr, dor, tops, cuts, inv, dqt, chain,
                parents_ref, parents_sem):
    place = Place()
    x = place.x
    column = x * 4 + place.z
    first_block = (x - (NEAR - 1)) * (SECTION // BLOCK)
    factor = SCALE * LOG2E

    parents_copy = pltpu.make_async_copy(parents_near, parents_ref, parents_sem)
    parents_copy.start()
    n0 = jnp.sum((seg_ref[...] == 0).astype(jnp.int32))

    parents_copy.wait()

    chains = [None] * 4
    free = jnp.int32(0)
    for qb in (3, 2, 1, 0):
        gb = column * 4 + qb
        lowest = jnp.where(gb * BLOCK >= n0, n0, 0)
        if qb == 3:
            shared = jnp.bool_(False)
        else:
            base, count, low = chains[qb + 1]
            shared = (parents_ref[gb + 1] == gb) & (low == lowest)

        def more(state):
            b, n = state
            return (b >= 0) & (b * BLOCK + (BLOCK - 1) >= lowest)

        def note(state):
            b, n = state
            chain[n] = b
            return (parents_ref[b], n + 1)

        _, stop = lax.while_loop(more, note, (jnp.where(shared, -1, gb), free))
        own = (free, stop - free, lowest)
        if qb < 3:
            own = (jnp.where(shared, base + 1, free), jnp.where(shared, count - 1, stop - free), lowest)
        chains[qb] = own
        free = stop

    for slot in range(NEAR):
        @pl.when(x >= 2 - slot)
        def _():
            for p in range(2):
                acc[p, slot * SECTION:(slot + 1) * SECTION, :] = jnp.zeros((SECTION, D), F32)
    dqt[...] = jnp.zeros_like(dqt)

    for qb in range(4):
        for h in range(4):
            rows, cols = slice(qb * BLOCK, (qb + 1) * BLOCK), slice(h * D, (h + 1) * D)
            qr[qb * ROWS + h * D:qb * ROWS + (h + 1) * D, :] = q_all[rows, cols]
            dor[qb * ROWS + h * D:qb * ROWS + (h + 1) * D, :] = do_all[rows, cols]

    def block_rows(b):
        return pl.ds(pl.multiple_of((b - first_block) * BLOCK, BLOCK), BLOCK)

    def gathered(p, blocks):
        return jnp.concatenate(
            [kv[p, pl.ds(pl.multiple_of(b * BLOCK, BLOCK), BLOCK), :] for b in blocks], axis=0)

    def row_of(q):
        return pl.ds(pl.multiple_of(q * 8, 8), 1)

    def lines_of(q):
        return pl.ds(pl.multiple_of(q * 8, 8), 8)

    def rows_of(qb):
        return pl.ds(pl.multiple_of(qb * ROWS, ROWS), ROWS)

    def fold(e):
        return jnp.sum(e.reshape(-1, 8, ROWS), axis=0)

    def one_half(half, carry):
        def pick(even, odd):
            return jnp.where(half == 0, even, odd)

        bases = [pick(chains[q][0], chains[q + 2][0]) for q in range(2)]
        counts = [pick(chains[q][1], chains[q + 2][1]) for q in range(2)]
        lows = [pick(chains[q][2], chains[q + 2][2]) for q in range(2)]
        starts = [(column * 4 + half * 2 + q) * BLOCK for q in range(2)]
        steps = [(counts[q] + GROUP - 1) // GROUP - 1 for q in range(2)]
        items = steps[0] + steps[1]

        def blocks_of(q, g):
            base = jnp.where(q == 0, bases[0], bases[1])
            count = jnp.where(q == 0, counts[0], counts[1])
            diagonal = column * 4 + half * 2 + q
            blocks, real = [], []
            for i in range(GROUP):
                at = g * GROUP + i
                here = at < count
                index = base + jnp.where(at == 0, 0, jnp.where(at == 1, count - 1, at - 1))
                blocks.append(jnp.where(here, chain[jnp.where(here, index, 0)], diagonal))
                real.append(here)
            return blocks, real

        def item(slot):
            t = slot - 2
            late = t >= steps[0]
            q = jnp.where(slot < 2, slot, late.astype(jnp.int32))
            g = jnp.where(slot < 2, 0, t - jnp.where(late, steps[0], 0) + 1)
            return q, g

        def expd_rows(slot, i=0, n=GROUP):
            return pl.ds(pl.multiple_of(slot * GROUP * BLOCK + i * BLOCK, BLOCK), n * BLOCK)

        def masked_scores(q, g):
            blocks, real = blocks_of(q, g)
            start = (column * 4 + half * 2 + q) * BLOCK
            query_at = start + lax.broadcasted_iota(jnp.int32, (1, ROWS), 1) % BLOCK
            least = jnp.where(query_at >= n0, n0, 0)
            scores = lax.dot_general(gathered(0, blocks), qr[rows_of(half * 2 + q), :], NT,
                                     preferred_element_type=F32)
            parts = []
            for i in range(GROUP):
                first = jnp.where(real[i], blocks[i] * BLOCK, 2 * TOKENS)
                key_at = first + lax.broadcasted_iota(jnp.int32, (BLOCK, ROWS), 0)
                ok = (key_at <= query_at) & (key_at >= least)
                parts.append(jnp.where(ok, scores[i * BLOCK:(i + 1) * BLOCK, :], NEG))
            return jnp.concatenate(parts, axis=0)

        for q in range(2):
            scores = masked_scores(q, 0)
            top = jnp.max(scores, axis=0, keepdims=True)
            e = jnp.exp2((scores - top) * factor)
            expd[expd_rows(q), :] = e
            inv[lines_of(q), :] = fold(e)
            query_at = starts[q] + lax.broadcasted_iota(jnp.int32, (1, ROWS), 1) % BLOCK
            cut = jnp.where((query_at >= n0) & (starts[q] < n0), -NEG, 0.0)
            cuts[lines_of(q), :] = jnp.broadcast_to(top + cut, (8, ROWS))

        def scores_turn(n, c):
            for u in range(SCORES_AT_ONCE):
                slot = 2 + n * SCORES_AT_ONCE + u
                q, g = item(slot)
                blocks, real = blocks_of(q, g)
                scores = lax.dot_general(gathered(0, blocks), qr[rows_of(half * 2 + q), :], NT,
                                         preferred_element_type=F32)
                top = cuts[row_of(q), :]
                sums = None
                for i in range(GROUP):
                    away = top + jnp.where(real[i], 0.0, -NEG)
                    e = jnp.exp2((scores[i * BLOCK:(i + 1) * BLOCK, :] - away) * factor)
                    expd[expd_rows(slot, i, 1), :] = e
                    sums = fold(e) if sums is None else sums + fold(e)
                inv[lines_of(q), :] += sums
            return c

        lax.fori_loop(0, (items + SCORES_AT_ONCE - 1) // SCORES_AT_ONCE, scores_turn, 0)
        totals = [jnp.sum(inv[q * 8:(q + 1) * 8, :], axis=0, keepdims=True) for q in range(2)]
        safe = jnp.max(jnp.maximum(totals[0], totals[1])) < 1e30
        for q in range(2):
            inv[q * 8:(q + 1) * 8, :] = jnp.broadcast_to(1.0 / totals[q], (8, ROWS))

        @pl.when(jnp.logical_not(safe))
        def _():
            cuts[...] = jnp.full_like(cuts, NEG)
            inv[...] = jnp.zeros_like(inv)

            def again(slot, c):
                q, g = item(slot)
                scores = masked_scores(q, g)
                top, total = cuts[row_of(q), :], inv[row_of(q), :]
                new_top = jnp.maximum(top, jnp.max(scores, axis=0, keepdims=True))
                e = jnp.exp2((scores - new_top) * factor)
                expd[expd_rows(slot), :] = e
                total = total * jnp.exp2((top - new_top) * factor) + jnp.sum(
                    e, axis=0, keepdims=True)
                cuts[lines_of(q), :] = jnp.broadcast_to(new_top, (8, ROWS))
                tops[lines_of(slot), :] = jnp.broadcast_to(new_top, (8, ROWS))
                inv[lines_of(q), :] = jnp.broadcast_to(total, (8, ROWS))
                return c

            def settle(slot, c):
                q, g = item(slot)
                share = jnp.exp2((tops[row_of(slot), :] - cuts[row_of(q), :]) * factor)
                expd[expd_rows(slot), :] = expd[expd_rows(slot), :] * (share / inv[row_of(q), :])
                return c

            lax.fori_loop(0, items + 2, again, 0)
            lax.fori_loop(0, items + 2, settle, 0)
            inv[...] = jnp.ones_like(inv)

        def grads_turn(n, c):
            work = []
            for u in range(GRADS_AT_ONCE):
                slot = n * GRADS_AT_ONCE + u
                q, g = item(slot)
                blocks, _ = blocks_of(q, g)
                do_rows = dor[rows_of(half * 2 + q), :]
                weight_grad = lax.dot_general(gathered(1, blocks), do_rows, NT,
                                              preferred_element_type=F32)
                work.append((slot, q, blocks, do_rows, weight_grad))
            for slot, q, blocks, do_rows, weight_grad in work:
                qb = half * 2 + q
                source = ((qb % 2) * 2 + qb // 2) * 2
                pair = dg_ref[source] + dg_ref[source + 1]
                out_dot = jnp.concatenate([pair[h:h + 1, :] for h in range(4)], axis=1)
                weights = expd[expd_rows(slot), :] * inv[row_of(q), :]
                halved = weights.astype(BF16)
                score_grad = (weights * (weight_grad - out_dot)).astype(BF16)
                dv = jnp.dot(halved, do_rows, preferred_element_type=F32)
                dk = jnp.dot(score_grad, qr[rows_of(qb), :], preferred_element_type=F32)
                into = pl.ds(pl.multiple_of(qb * D, D), D)
                dqt[into, :] += lax.dot_general(gathered(0, blocks), score_grad, TN,
                                                preferred_element_type=F32)
                for i, b in enumerate(blocks):
                    rows = block_rows(b)
                    acc[0, rows, :] += dk[i * BLOCK:(i + 1) * BLOCK, :]
                    acc[1, rows, :] += dv[i * BLOCK:(i + 1) * BLOCK, :]
            return c

        lax.fori_loop(0, (items + 2 + GRADS_AT_ONCE - 1) // GRADS_AT_ONCE, grads_turn, 0)
        return carry

    lax.fori_loop(0, 2, one_half, 0)

    for slot in range(NEAR):
        @pl.when(x >= 2 - slot)
        def _():
            for p, by in ((0, SCALE), (1, 1.0)):
                at = slice(slot * SECTION, (slot + 1) * SECTION)
                dkv_ref[p, slot] = (acc[p, at, :] * by).astype(BF16)
    for qb in range(4):
        for h in range(4):
            part = dqt[qb * D:(qb + 1) * D, h * D:(h + 1) * D].T * SCALE
            dq_ref[qb * BLOCK:(qb + 1) * BLOCK, h * D:(h + 1) * D] = part.astype(BF16)


def home_kernel(dkv_ref, dq_ref,
                qg_ref, kg_ref, vg_ref,
                sib, acc, snd, hop, rx, rz, rzz, rx2,
                col_send, q_recv, local_sem, sib_send, sib_recv,
                send_sems, rx_recv, rz_recv, rzz_recv, rx2_recv):
    place = Place()
    x, z, core = place.x, place.z, place.core
    greet(place, True)
    sibling = place.at(core=1 - core)

    def rows_at(dz):
        return pl.ds(pl.multiple_of(((z + dz) % 4) * COLUMN, COLUMN), COLUMN)

    def share(p):
        order = [(d, dz) for dz in FAR_FIRST for d in (2, 1, 0)]
        if p == 1:
            order = [(d, dz) for d in (2, 1, 0) for dz in FAR_FIRST]
        copies = []
        for d, dz in order:
            copy = rcopy(dkv_ref.at[p, 2 - d, rows_at(dz), :], sib.at[d, rows_at(dz), :],
                         sib_send.at[d, dz], sib_recv.at[d, dz], sibling)
            pl.when(x >= d)(copy.start)
            copies.append((d, copy))
        return copies

    pl.when(core == 1)(lambda: share(0) and None)
    pl.when(core == 0)(lambda: share(1) and None)

    columns = Sends(col_send)
    col = pl.multiple_of(place.own * ROWS, ROWS)
    target = qg_ref.at[:, pl.ds(col, ROWS)]
    for away in (4, 5, 2, 3, 6, 7, 1):
        t = ((place.y + away // 2) % 4) * 2 + (core + away) % 2
        src = dq_ref.at[pl.ds(pl.multiple_of(place.home_row(t), 64), 64), :]
        columns.start(None, src, target, q_recv.at[place.own], place.in_column(t))
    src = dq_ref.at[pl.ds(pl.multiple_of(place.home_row(), 64), 64), :]
    stay = pltpu.make_async_copy(src, target, local_sem.at[0])
    stay.start()

    def both(p, d, dz):
        part = sib.at[d, rows_at(dz), :]
        rcopy(part, part, sib_send.at[d, dz], sib_recv.at[d, dz], sibling).wait_recv()
        return dkv_ref[p, 2 - d, rows_at(dz), :].astype(F32) + part[...].astype(F32)

    def arrived(ref, sem):
        rcopy(ref, ref, send_sems.at[0], sem, sibling).wait_recv()
        return ref[...].astype(F32)

    def send_halves(sends, cond, src, start, landing, recv, x_to, z_to, stays):
        for half in range(2):
            rows = src.at[pl.ds(pl.multiple_of(start + half * 256, 256), 256), :]
            away = cond
            if stays:
                here = (place.ylo == half) & (core == place.ylo)
                local = pltpu.make_async_copy(rows, landing, local_sem.at[1])
                pl.when(here)(local.start)
                pl.when(here)(local.wait)
                away = jnp.logical_not(here)
            sends.start(away, rows, landing, recv,
                        place.at(x=x_to, z=z_to, ylo=half, core=place.ylo))

    def keys_home():
        sends = Sends(send_sems)
        for dz in FAR_FIRST:
            for d in (2, 1):
                @pl.when(x >= d)
                def _():
                    snd[d, rows_at(dz), :] = both(0, d, dz).astype(BF16)
                sends.start(x >= d, snd.at[d, rows_at(dz), :], rx.at[d - 1, rows_at(dz), :],
                            rx_recv.at[d - 1, dz], place.at(x=(x + 4 - d) % 4))
            acc[0, rows_at(dz), :] = both(0, 0, dz)
        for dz in FAR_FIRST:
            for d in (1, 2):
                @pl.when(x + d <= 3)
                def _():
                    acc[0, rows_at(dz), :] += arrived(rx.at[d - 1, rows_at(dz), :],
                                                      rx_recv.at[d - 1, dz])
            hop[rows_at(dz), :] = acc[0, rows_at(dz), :].astype(BF16)
            send_halves(sends, None, hop, ((z + dz) % 4) * COLUMN, rz.at[dz], rz_recv.at[dz],
                        x, (z + dz) % 4, dz == 0)
        sends.finish()

    def values_home():
        sends = Sends(send_sems)
        for d in (2, 1, 0):
            for dz in (2, 1, 3):
                @pl.when(x >= d)
                def _():
                    snd[d, rows_at(dz), :] = both(1, d, dz).astype(BF16)
                sends.start(x >= d, snd.at[d, rows_at(dz), :], rzz.at[dz - 1, d],
                            rzz_recv.at[dz - 1, d], place.at(z=(z + dz) % 4))

            @pl.when(x >= d)
            def _():
                acc[d, rows_at(0), :] = both(1, d, 0)
        for d in (2, 1, 0):
            @pl.when(x >= d)
            def _():
                part = acc[d, rows_at(0), :]
                for dz in (1, 3, 2):
                    part = part + arrived(rzz.at[dz - 1, d], rzz_recv.at[dz - 1, d])
                hop[d * COLUMN:(d + 1) * COLUMN, :] = part.astype(BF16)
            send_halves(sends, x >= d, hop, d * COLUMN, rx2.at[d], rx2_recv.at[d],
                        (x + 4 - d) % 4, z, d == 0)
        sends.finish()

    pl.when(core == 0)(keys_home)
    pl.when(core == 1)(values_home)

    def landed(ref, sem, p, stays):
        wait = rcopy(ref, ref, send_sems.at[0], sem, sibling)
        if stays:
            here = (core == p) & (place.ylo == p)
            pl.when(jnp.logical_not(here))(wait.wait_recv)
        else:
            wait.wait_recv()
        return ref[...].astype(F32)

    total = None
    for dz in FAR_FIRST:
        part = landed(rz.at[dz], rz_recv.at[dz], 0, dz == 0)
        total = part if total is None else total + part
    kg_ref[...] = total.astype(BF16)
    acc[0, 0:256, :] = landed(rx2.at[0], rx2_recv.at[0], 1, True)
    for d in (1, 2):
        @pl.when(x + d <= 3)
        def _():
            acc[0, 0:256, :] += landed(rx2.at[d], rx2_recv.at[d], 1, False)
    vg_ref[...] = acc[0, 0:256, :].astype(BF16)
    for t in range(8):
        @pl.when(place.own != t)
        def _():
            src = dq_ref.at[pl.ds(0, 64), :]
            rcopy(src, qg_ref.at[:, pl.ds(t * ROWS, ROWS)], col_send.at[0], q_recv.at[t],
                  sibling).wait_recv()
    stay.wait()
    columns.finish()
    for d in range(NEAR):
        for dz in range(4):
            part = dkv_ref.at[0, 2 - d, rows_at(dz), :]
            pl.when(x >= d)(rcopy(part, part, sib_send.at[d, dz], sib_recv.at[d, dz],
                                  sibling).wait_send)


ANY = pl.BlockSpec(memory_space=pl.ANY)
VMEM = pl.BlockSpec(memory_space=pltpu.VMEM)
HBM = pl.BlockSpec(memory_space=pltpu.HBM)
SMEM = pl.BlockSpec(memory_space=pltpu.SMEM)
DMA = pltpu.SemaphoreType.DMA
MIB = 1 << 20


def struct(shape, dtype):
    return jax.ShapeDtypeStruct(shape, dtype)


def spread(q, do, o, k, v, seg, parents):
    return pl.pallas_call(
        spread_kernel,
        out_shape=(pltpu.VMEM((COLUMN, ROWS), BF16), pltpu.VMEM((COLUMN, ROWS), BF16),
                   pltpu.VMEM((8, 8, 128), F32), pltpu.VMEM((2, TOKENS, D), BF16),
                   pltpu.VMEM((64, 128), jnp.int32), pltpu.VMEM((64,), jnp.int32)),
        in_specs=[HBM] * 7,
        out_specs=(VMEM,) * 6,
        scratch_shapes=[
            pltpu.VMEM((64, 4096), BF16), pltpu.VMEM((64, 4096), BF16), DMA((4,)),
            pltpu.VMEM((8, 8, 128), F32),
            DMA((24,)), DMA((8,)), DMA((8,)), DMA((8,)), DMA((4,)),
            DMA((2,)), DMA((2,)), DMA((32,)), DMA((16, 2)), DMA((16,)), DMA((8,)),
        ],
        compiler_params=pltpu.CompilerParams(
            collective_id=0, has_side_effects=True, vmem_limit_bytes=56 * MIB),
        name="spread",
    )(q, do, o, k, v, seg, parents)


def grads(parents, seg, q, do, dg, kv):
    return pl.pallas_call(
        grad_kernel,
        out_shape=(pltpu.VMEM((2, NEAR, SECTION, D), BF16), pltpu.VMEM((COLUMN, ROWS), BF16)),
        in_specs=[VMEM] * 6,
        out_specs=(VMEM, VMEM),
        scratch_shapes=[
            pltpu.VMEM((2, NEAR * SECTION, D), F32),
            pltpu.VMEM((SLOTS * GROUP * BLOCK, ROWS), F32),
            pltpu.VMEM((4 * ROWS, D), BF16),
            pltpu.VMEM((4 * ROWS, D), BF16),
            pltpu.VMEM((SLOTS * 8, ROWS), F32),
            pltpu.VMEM((16, ROWS), F32),
            pltpu.VMEM((16, ROWS), F32),
            pltpu.VMEM((4 * D, ROWS), F32),
            pltpu.SMEM((256,), jnp.int32), pltpu.SMEM((64,), jnp.int32), DMA,
        ],
        compiler_params=pltpu.CompilerParams(vmem_limit_bytes=38 * MIB),
        name="grads",
    )(parents, seg, q, do, dg, kv)


def home(dkv, dq):
    return pl.pallas_call(
        home_kernel,
        out_shape=(pltpu.VMEM((64, 4096), BF16), pltpu.VMEM((256, D), BF16),
                   pltpu.VMEM((256, D), BF16)),
        in_specs=[VMEM, VMEM],
        out_specs=(VMEM,) * 3,
        scratch_shapes=[
            pltpu.VMEM((NEAR, SECTION, D), BF16),
            pltpu.VMEM((NEAR, SECTION, D), F32),
            pltpu.VMEM((NEAR, SECTION, D), BF16),
            pltpu.VMEM((SECTION, D), BF16),
            pltpu.VMEM((2, SECTION, D), BF16),
            pltpu.VMEM((4, 256, D), BF16),
            pltpu.VMEM((3, NEAR, COLUMN, D), BF16),
            pltpu.VMEM((NEAR, 256, D), BF16),
            DMA((8,)), DMA((8,)), DMA((2,)), DMA((3, 4)), DMA((3, 4)),
            DMA((20,)), DMA((2, 4)), DMA((4,)), DMA((3, 3)), DMA((3,)),
        ],
        compiler_params=pltpu.CompilerParams(
            collective_id=1, has_side_effects=True, vmem_limit_bytes=24 * MIB),
        name="home",
    )(dkv, dq)


def hand_over_kernel(*refs):
    copies = [pltpu.make_async_copy(refs[n], refs[3 + n], refs[6].at[n]) for n in range(3)]
    for copy in copies:
        copy.start()
    for copy in copies:
        copy.wait()


def hand_over(*arrays):
    return pl.pallas_call(
        hand_over_kernel,
        out_shape=tuple(struct(a.shape, a.dtype) for a in arrays),
        in_specs=[VMEM] * 3,
        out_specs=(HBM,) * 3,
        scratch_shapes=[DMA((3,))],
        compiler_params=pltpu.CompilerParams(vmem_limit_bytes=8 * MIB),
        name="hand_over",
    )(*arrays)


def local(query_rows, key_rows, value_rows, attn_output, out_grad, segments, parents):
    q, do, dg, kv, seg, parents = spread(
        query_rows, out_grad, attn_output, key_rows, value_rows, segments.reshape(64, 128), parents)
    dkv, dq = grads(parents, seg, q, do, dg, kv)
    return hand_over(*home(dkv, dq))


def solution(mesh):
    placed = (
        P(("ctx", "head"), None),
        P("ctx", "head"),
        P("ctx", "head"),
        P(("ctx", "head"), None),
        P(("ctx", "head"), None),
        P(),
        P(),
    )
    return jax.shard_map(
        local,
        mesh=mesh,
        in_specs=placed,
        out_specs=(P(("ctx", "head"), None), P("ctx", "head"), P("ctx", "head")),
        check_vma=False,
    )
```

```python
import functools
import math

import jax
import jax.numpy as jnp
from jax import lax
from jax.experimental import pallas as pl
from jax.experimental.pallas import tpu as pltpu
from jax.sharding import PartitionSpec as P

D = 128
BLOCK = 128
TOKENS = 8192
COLUMN = 512
SECTION = 2048
NEAR = 3
FAR_FIRST = (2, 1, 3, 0)
RELAYED = (0, 1)
GROUP = 4
AT_ONCE = 4
SLOTS = 24
ROWS = 512
SCALE = 1.0 / math.sqrt(D)
LOG2E = math.log2(math.e)
NEG = -1e30
F32 = jnp.float32
BF16 = jnp.bfloat16
MESH = pl.DeviceIdType.MESH
NT = (((1,), (1,)), ((), ()))
TN = (((0,), (0,)), ((), ()))


class Place:
    def __init__(self):
        ctx = lax.axis_index("ctx")
        head = lax.axis_index("head")
        self.x = ctx // 8
        self.z = (ctx // 2) % 4
        self.ylo = ctx % 2
        self.yhi = head // 2
        self.core = head % 2
        self.y = self.yhi * 2 + self.ylo

    def at(self, x=None, z=None, ylo=None, yhi=None, core=None):
        x = self.x if x is None else x
        z = self.z if z is None else z
        ylo = self.ylo if ylo is None else ylo
        yhi = self.yhi if yhi is None else yhi
        core = self.core if core is None else core
        return ((x * 4 + z) * 2 + ylo, yhi * 2 + core)

    def in_column(self, t):
        return self.at(ylo=(t // 2) % 2, yhi=t // 4, core=t % 2)

    @property
    def own(self):
        return self.y * 2 + self.core

    def home_row(self, t=None):
        if t is None:
            return (self.ylo * 2 + self.yhi) * 128 + self.core * 64
        return (((t // 2) % 2) * 2 + t // 4) * 128 + (t % 2) * 64


def greet(place, homeward=False):
    barrier = pltpu.get_barrier_semaphore()
    for t in range(8):
        @pl.when(place.own != t)
        def _():
            pl.semaphore_signal(barrier, inc=1, device_id=place.in_column(t), device_id_type=MESH)
    for step in range(1, 4):
        pl.semaphore_signal(
            barrier, inc=1, device_id=place.at(x=(place.x + step) % 4), device_id_type=MESH)
        pl.semaphore_signal(
            barrier, inc=1, device_id=place.at(z=(place.z + step) % 4), device_id_type=MESH)
    if not homeward:
        pl.semaphore_wait(barrier, 13)
        return
    for step in range(1, 4):
        pl.semaphore_signal(
            barrier, inc=1, device_id=place.at(z=(place.z + step) % 4, ylo=place.core, core=0),
            device_id_type=MESH)
    for d in (1, 2):
        @pl.when(place.x + d <= 3)
        def _():
            pl.semaphore_signal(
                barrier, inc=1,
                device_id=place.at(x=(place.x + d) % 4, ylo=place.core, core=1),
                device_id_type=MESH)
    pl.semaphore_wait(barrier, 13 + jnp.where(place.core == 0, 6, 2 * jnp.minimum(place.x, 2)))


def rcopy(src, dst, send, recv, device):
    return pltpu.make_async_remote_copy(
        src_ref=src, dst_ref=dst, send_sem=send, recv_sem=recv,
        device_id=device, device_id_type=MESH)


class Sends:
    def __init__(self, sems):
        self.sems = sems
        self.items = []

    def start(self, cond, src, dst, recv, device):
        copy = rcopy(src, dst, self.sems.at[len(self.items)], recv, device)
        self.items.append((cond, copy))
        if cond is None:
            copy.start()
        else:
            pl.when(cond)(copy.start)

    def finish(self):
        for cond, copy in self.items:
            if cond is None:
                copy.wait_send()
            else:
                pl.when(cond)(copy.wait_send)


def spread_kernel(q_ref, do_ref, o_ref, k_ref, v_ref, seg_ref, parents_ref,
                  qg_ref, dog_ref, dg_ref, kv_ref, seg_near, parents_near,
                  do_near, o_near, near_sem, dsrc, col_send, q_recv, do_recv, d_recv, local_sem,
                  first_send, first_recv, piece_send, prim_recv, sib_recv, dot_send):
    place = Place()
    x, z, core = place.x, place.z, place.core
    nears = [pltpu.make_async_copy(do_ref, do_near, near_sem.at[0]),
             pltpu.make_async_copy(o_ref, o_near, near_sem.at[1]),
             pltpu.make_async_copy(seg_ref, seg_near, near_sem.at[2]),
             pltpu.make_async_copy(parents_ref, parents_near, near_sem.at[3])]
    for copy in nears:
        copy.start()
    greet(place)

    first_row = pl.multiple_of((x * 4 + z) * COLUMN + place.ylo * 256, 256)
    firsts = []
    for p, src in ((0, k_ref), (1, v_ref)):
        dst = kv_ref.at[p, pl.ds(first_row, 256), :]
        here = (place.ylo == core) & (core == p)
        away = jnp.logical_not(here)
        copy = rcopy(src, dst, first_send.at[p], first_recv.at[place.ylo],
                     place.at(ylo=core, core=p))
        local = pltpu.make_async_copy(src, dst, local_sem.at[3])
        pl.when(away)(copy.start)
        pl.when(here)(local.start)
        firsts.append((here, away, copy, local))

    my_row = pl.multiple_of(place.home_row(), 64)
    columns = Sends(col_send)
    locals_ = []

    def across(src, dst, recv, sem):
        target = dst.at[pl.ds(my_row, 64), :]
        for away in (4, 5, 2, 3, 6, 7, 1, 0):
            t = ((place.y + away // 2) % 4) * 2 + (core + away) % 2
            cols = pl.ds(pl.multiple_of(t * ROWS, ROWS), ROWS)
            if away:
                columns.start(None, src.at[:, cols], target, recv.at[place.own],
                              place.in_column(t))
            else:
                local = pltpu.make_async_copy(src.at[:, cols], target, sem)
                local.start()
                locals_.append(local)

    across(q_ref, qg_ref, q_recv, local_sem.at[0])

    lane = lax.broadcasted_iota(jnp.int32, (8, 128), 1)
    line = lax.broadcasted_iota(jnp.int32, (8, 128), 0)
    mine = (lane // 64) == core
    ones = jnp.ones((8, D), BF16)
    for copy in nears:
        copy.wait()
    for t in range(8):
        tile = jnp.zeros((8, 128), F32)
        for r in range(4):
            cols = slice((t * 4 + r) * D, (t * 4 + r + 1) * D)
            prod = do_near[:, cols].astype(F32) * o_near[:, cols].astype(F32)
            high = prod.astype(BF16)
            low = (prod - high.astype(F32)).astype(BF16)
            row = (lax.dot_general(ones, high, NT, preferred_element_type=F32)
                   + lax.dot_general(ones, low, NT, preferred_element_type=F32))
            row = jnp.concatenate([row, row], axis=1)
            tile = jnp.where(mine & (line == r), row, tile)
        dsrc[t] = tile
    dots = Sends(dot_send)
    target = dg_ref.at[place.own]
    for t in range(8):
        dots.start(place.own != t, dsrc.at[t], target, d_recv.at[place.own],
                   place.in_column(t))
    stay = pltpu.make_async_copy(dsrc.at[place.own], target, local_sem.at[2])
    stay.start()

    across(do_ref, dog_ref, do_recv, local_sem.at[1])

    for half in range(2):
        here = (place.ylo == core) & (place.ylo == half)
        wait = rcopy(k_ref, kv_ref.at[core, pl.ds(0, 256), :], first_send.at[0],
                     first_recv.at[half], place.at(core=1 - core))
        pl.when(jnp.logical_not(here))(wait.wait_recv)
    for here, away, copy, local in firsts:
        pl.when(here)(local.wait)

    def piece(p, xx, zz, half=None):
        start = pl.multiple_of((xx * 4 + zz) * COLUMN, COLUMN)
        if half is None:
            return kv_ref.at[p, pl.ds(start, COLUMN), :]
        return kv_ref.at[p, pl.ds(pl.multiple_of(start + half * 256, 256), 256), :]

    sibling = place.at(core=1 - core)

    def run(c):
        sends = Sends(piece_send)

        def share(cond, xx, zz):
            part = piece(c, xx, zz)
            sends.start(cond, part, part, sib_recv.at[xx * 4 + zz], sibling)

        def along_x(zz, dz):
            part = piece(c, x, zz)
            recv = prim_recv.at[x * 4 + zz, 0]
            sends.start(x <= 2, part, part, recv, place.at(x=(x + 1) % 4))
            step = 3 if c == 0 and dz in RELAYED else 2
            sends.start(x <= 1, part, part, recv, place.at(x=(x + step) % 4))

        def pass_on(dz):
            xx, zz = (x + 1) % 4, (z + dz) % 4
            between = (x == 0) | (x == 3)
            arrive(between, xx, zz)
            part = piece(c, xx, zz)
            sends.start(between, part, part, prim_recv.at[xx * 4 + zz, 0],
                        place.at(x=(x + 3) % 4))

        def along_z(cond, xx):
            part = piece(c, xx, z)
            for d in (1, 3, 2):
                sends.start(cond, part, part, prim_recv.at[xx * 4 + z, 0],
                            place.at(z=(z + d) % 4))

        def arrive(cond, xx, zz, halves=False):
            parts = [piece(c, xx, zz, h) for h in (0, 1)] if halves else [piece(c, xx, zz)]
            for h, part in enumerate(parts):
                wait = rcopy(part, part, piece_send.at[0], prim_recv.at[xx * 4 + zz, h], sibling)
                if cond is None:
                    wait.wait_recv()
                else:
                    pl.when(cond)(wait.wait_recv)

        if c == 0:
            along_z(None, x)
            along_x(z, 0)
            share(None, x, z)
            for dz in (1, 3, 2):
                zz = (z + dz) % 4
                arrive(None, x, zz)
                along_x(zz, dz)
                share(None, x, zz)
                if {1: 0, 3: 1, 2: 3}[dz] in RELAYED:
                    pass_on({1: 0, 3: 1, 2: 3}[dz])
            for dz in (0, 1, 3, 2):
                zz = (z + dz) % 4
                for d in (1, 2):
                    xx = (x + 4 - d) % 4
                    arrive(x >= d, xx, zz)
                    share(x >= d, xx, zz)
        else:
            along_x(z, 0)
            along_z(None, x)
            share(None, x, z)
            for d in (1, 2):
                xx = (x + 4 - d) % 4
                arrive(x >= d, xx, z)
                along_z(x >= d, xx)
                share(x >= d, xx, z)
            for dz in (1, 3, 2):
                zz = (z + dz) % 4
                for d in range(NEAR):
                    xx = (x + 4 - d) % 4
                    arrive(x >= d, xx, zz)
                    share(x >= d, xx, zz)
        for d in range(NEAR):
            xx = (x + 4 - d) % 4
            for zz in range(4):
                part = piece(1 - c, xx, zz)
                wait = rcopy(part, part, piece_send.at[0], sib_recv.at[xx * 4 + zz], sibling)
                pl.when(x >= d)(wait.wait_recv)
        sends.finish()

    pl.when(core == 0)(lambda: run(0))
    pl.when(core == 1)(lambda: run(1))

    for t in range(8):
        @pl.when(place.own != t)
        def _():
            row = place.home_row(t)
            for src, dst, recv in ((q_ref, qg_ref, q_recv), (do_ref, dog_ref, do_recv)):
                rcopy(src.at[:, pl.ds(0, ROWS)], dst.at[pl.ds(row, 64), :], col_send.at[0],
                      recv.at[t], place.in_column(t)).wait_recv()
    for local in locals_:
        local.wait()
    for t in range(8):
        pl.when(place.own != t)(rcopy(dsrc.at[t], dg_ref.at[t], dot_send.at[0], d_recv.at[t],
                                      place.in_column(t)).wait_recv)
    stay.wait()
    dots.finish()
    columns.finish()
    for here, away, copy, local in firsts:
        pl.when(away)(copy.wait_send)


def grad_kernel(parents_near, seg_ref, q_all, do_all, dg_ref, kv,
                dkv_ref, dq_ref,
                acc, expd, qr, dor, tops, cuts, inv, dqt, chain,
                parents_ref, parents_sem):
    place = Place()
    x = place.x
    column = x * 4 + place.z
    first_block = (x - (NEAR - 1)) * (SECTION // BLOCK)
    factor = SCALE * LOG2E

    parents_copy = pltpu.make_async_copy(parents_near, parents_ref, parents_sem)
    parents_copy.start()
    n0 = jnp.sum((seg_ref[...] == 0).astype(jnp.int32))

    parents_copy.wait()

    chains = [None] * 4
    free = jnp.int32(0)
    for qb in (3, 2, 1, 0):
        gb = column * 4 + qb
        lowest = jnp.where(gb * BLOCK >= n0, n0, 0)
        if qb == 3:
            shared = jnp.bool_(False)
        else:
            base, count, low = chains[qb + 1]
            shared = (parents_ref[gb + 1] == gb) & (low == lowest)

        def more(state):
            b, n = state
            return (b >= 0) & (b * BLOCK + (BLOCK - 1) >= lowest)

        def note(state):
            b, n = state
            chain[n] = b
            return (parents_ref[b], n + 1)

        _, stop = lax.while_loop(more, note, (jnp.where(shared, -1, gb), free))
        own = (free, stop - free, lowest)
        if qb < 3:
            own = (jnp.where(shared, base + 1, free), jnp.where(shared, count - 1, stop - free), lowest)
        chains[qb] = own
        free = stop

    for slot in range(NEAR):
        @pl.when(x >= 2 - slot)
        def _():
            for p in range(2):
                acc[p, slot * SECTION:(slot + 1) * SECTION, :] = jnp.zeros((SECTION, D), F32)
    dqt[...] = jnp.zeros_like(dqt)

    for qb in range(4):
        for h in range(4):
            rows, cols = slice(qb * BLOCK, (qb + 1) * BLOCK), slice(h * D, (h + 1) * D)
            qr[qb * ROWS + h * D:qb * ROWS + (h + 1) * D, :] = q_all[rows, cols]
            dor[qb * ROWS + h * D:qb * ROWS + (h + 1) * D, :] = do_all[rows, cols]

    def block_rows(b):
        return pl.ds(pl.multiple_of((b - first_block) * BLOCK, BLOCK), BLOCK)

    def gathered(p, blocks):
        return jnp.concatenate(
            [kv[p, pl.ds(pl.multiple_of(b * BLOCK, BLOCK), BLOCK), :] for b in blocks], axis=0)

    def row_of(q):
        return pl.ds(pl.multiple_of(q * 8, 8), 1)

    def lines_of(q):
        return pl.ds(pl.multiple_of(q * 8, 8), 8)

    def rows_of(qb):
        return pl.ds(pl.multiple_of(qb * ROWS, ROWS), ROWS)

    def fold(e):
        return jnp.sum(e.reshape(-1, 8, ROWS), axis=0)

    def in_turns(turn, first, number):
        whole = number // AT_ONCE
        lax.fori_loop(0, whole, functools.partial(turn, first, AT_ONCE), 0)
        done = whole * AT_ONCE
        lax.fori_loop(0, (number - done + 1) // 2, functools.partial(turn, first + done, 2), 0)

    def one_half(half, carry):
        def pick(even, odd):
            return jnp.where(half == 0, even, odd)

        bases = [pick(chains[q][0], chains[q + 2][0]) for q in range(2)]
        counts = [pick(chains[q][1], chains[q + 2][1]) for q in range(2)]
        lows = [pick(chains[q][2], chains[q + 2][2]) for q in range(2)]
        starts = [(column * 4 + half * 2 + q) * BLOCK for q in range(2)]
        steps = [(counts[q] + GROUP - 1) // GROUP - 1 for q in range(2)]
        items = steps[0] + steps[1]

        def blocks_of(q, g):
            base = jnp.where(q == 0, bases[0], bases[1])
            count = jnp.where(q == 0, counts[0], counts[1])
            diagonal = column * 4 + half * 2 + q
            blocks, real = [], []
            for i in range(GROUP):
                at = g * GROUP + i
                here = at < count
                index = base + jnp.where(at == 0, 0, jnp.where(at == 1, count - 1, at - 1))
                blocks.append(jnp.where(here, chain[jnp.where(here, index, 0)], diagonal))
                real.append(here)
            return blocks, real

        def item(slot):
            t = slot - 2
            late = t >= steps[0]
            q = jnp.where(slot < 2, slot, late.astype(jnp.int32))
            g = jnp.where(slot < 2, 0, t - jnp.where(late, steps[0], 0) + 1)
            return q, g

        def expd_rows(slot, i=0, n=GROUP):
            return pl.ds(pl.multiple_of(slot * GROUP * BLOCK + i * BLOCK, BLOCK), n * BLOCK)

        def masked_scores(q, g):
            blocks, real = blocks_of(q, g)
            start = (column * 4 + half * 2 + q) * BLOCK
            query_at = start + lax.broadcasted_iota(jnp.int32, (1, ROWS), 1) % BLOCK
            least = jnp.where(query_at >= n0, n0, 0)
            scores = lax.dot_general(gathered(0, blocks), qr[rows_of(half * 2 + q), :], NT,
                                     preferred_element_type=F32)
            parts = []
            for i in range(GROUP):
                first = jnp.where(real[i], blocks[i] * BLOCK, 2 * TOKENS)
                key_at = first + lax.broadcasted_iota(jnp.int32, (BLOCK, ROWS), 0)
                ok = (key_at <= query_at) & (key_at >= least)
                parts.append(jnp.where(ok, scores[i * BLOCK:(i + 1) * BLOCK, :], NEG))
            return jnp.concatenate(parts, axis=0)

        for q in range(2):
            scores = masked_scores(q, 0)
            top = jnp.max(scores, axis=0, keepdims=True)
            e = jnp.exp2((scores - top) * factor)
            expd[expd_rows(q), :] = e
            inv[lines_of(q), :] = fold(e)
            query_at = starts[q] + lax.broadcasted_iota(jnp.int32, (1, ROWS), 1) % BLOCK
            cut = jnp.where((query_at >= n0) & (starts[q] < n0), -NEG, 0.0)
            cuts[lines_of(q), :] = jnp.broadcast_to(top + cut, (8, ROWS))

        def scores_turn(first, width, n, c):
            for u in range(width):
                slot = first + n * width + u
                q, g = item(slot)
                blocks, real = blocks_of(q, g)
                scores = lax.dot_general(gathered(0, blocks), qr[rows_of(half * 2 + q), :], NT,
                                         preferred_element_type=F32)
                top = cuts[row_of(q), :]
                sums = None
                for i in range(GROUP):
                    away = top + jnp.where(real[i], 0.0, -NEG)
                    e = jnp.exp2((scores[i * BLOCK:(i + 1) * BLOCK, :] - away) * factor)
                    expd[expd_rows(slot, i, 1), :] = e
                    sums = fold(e) if sums is None else sums + fold(e)
                inv[lines_of(q), :] += sums
            return c

        in_turns(scores_turn, 2, items)
        totals = [jnp.sum(inv[q * 8:(q + 1) * 8, :], axis=0, keepdims=True) for q in range(2)]
        safe = jnp.max(jnp.maximum(totals[0], totals[1])) < 1e30
        for q in range(2):
            inv[q * 8:(q + 1) * 8, :] = jnp.broadcast_to(1.0 / totals[q], (8, ROWS))

        @pl.when(jnp.logical_not(safe))
        def _():
            cuts[...] = jnp.full_like(cuts, NEG)
            inv[...] = jnp.zeros_like(inv)

            def again(slot, c):
                q, g = item(slot)
                scores = masked_scores(q, g)
                top, total = cuts[row_of(q), :], inv[row_of(q), :]
                new_top = jnp.maximum(top, jnp.max(scores, axis=0, keepdims=True))
                e = jnp.exp2((scores - new_top) * factor)
                expd[expd_rows(slot), :] = e
                total = total * jnp.exp2((top - new_top) * factor) + jnp.sum(
                    e, axis=0, keepdims=True)
                cuts[lines_of(q), :] = jnp.broadcast_to(new_top, (8, ROWS))
                tops[lines_of(slot), :] = jnp.broadcast_to(new_top, (8, ROWS))
                inv[lines_of(q), :] = jnp.broadcast_to(total, (8, ROWS))
                return c

            def settle(slot, c):
                q, g = item(slot)
                share = jnp.exp2((tops[row_of(slot), :] - cuts[row_of(q), :]) * factor)
                expd[expd_rows(slot), :] = expd[expd_rows(slot), :] * (share / inv[row_of(q), :])
                return c

            lax.fori_loop(0, items + 2, again, 0)
            lax.fori_loop(0, items + 2, settle, 0)
            inv[...] = jnp.ones_like(inv)

        def grads_turn(first, width, n, c):
            work = []
            for u in range(width):
                slot = first + n * width + u
                q, g = item(slot)
                blocks, _ = blocks_of(q, g)
                do_rows = dor[rows_of(half * 2 + q), :]
                weight_grad = lax.dot_general(gathered(1, blocks), do_rows, NT,
                                              preferred_element_type=F32)
                work.append((slot, q, blocks, do_rows, weight_grad))
            for slot, q, blocks, do_rows, weight_grad in work:
                qb = half * 2 + q
                source = ((qb % 2) * 2 + qb // 2) * 2
                pair = dg_ref[source] + dg_ref[source + 1]
                out_dot = jnp.concatenate([pair[h:h + 1, :] for h in range(4)], axis=1)
                weights = expd[expd_rows(slot), :] * inv[row_of(q), :]
                halved = weights.astype(BF16)
                score_grad = (weights * (weight_grad - out_dot)).astype(BF16)
                dv = jnp.dot(halved, do_rows, preferred_element_type=F32)
                dk = jnp.dot(score_grad, qr[rows_of(qb), :], preferred_element_type=F32)
                into = pl.ds(pl.multiple_of(qb * D, D), D)
                dqt[into, :] += lax.dot_general(gathered(0, blocks), score_grad, TN,
                                                preferred_element_type=F32)
                for i, b in enumerate(blocks):
                    rows = block_rows(b)
                    acc[0, rows, :] += dk[i * BLOCK:(i + 1) * BLOCK, :]
                    acc[1, rows, :] += dv[i * BLOCK:(i + 1) * BLOCK, :]
            return c

        in_turns(grads_turn, 0, items + 2)
        return carry

    lax.fori_loop(0, 2, one_half, 0)

    for slot in range(NEAR):
        @pl.when(x >= 2 - slot)
        def _():
            for p, by in ((0, SCALE), (1, 1.0)):
                at = slice(slot * SECTION, (slot + 1) * SECTION)
                dkv_ref[p, slot] = (acc[p, at, :] * by).astype(BF16)
    for qb in range(4):
        for h in range(4):
            part = dqt[qb * D:(qb + 1) * D, h * D:(h + 1) * D].T * SCALE
            dq_ref[qb * BLOCK:(qb + 1) * BLOCK, h * D:(h + 1) * D] = part.astype(BF16)


def home_kernel(dkv_ref, dq_ref,
                qg_ref, kg_ref, vg_ref,
                sib, acc, snd, hop, rx, rz, rzz, rx2,
                col_send, q_recv, local_sem, sib_send, sib_recv,
                send_sems, rx_recv, rz_recv, rzz_recv, rx2_recv):
    place = Place()
    x, z, core = place.x, place.z, place.core
    greet(place, True)
    sibling = place.at(core=1 - core)

    def rows_at(dz):
        return pl.ds(pl.multiple_of(((z + dz) % 4) * COLUMN, COLUMN), COLUMN)

    def share(p):
        order = [(d, dz) for dz in FAR_FIRST for d in (2, 1, 0)]
        if p == 1:
            order = [(d, dz) for d in (2, 1, 0) for dz in FAR_FIRST]
        copies = []
        for d, dz in order:
            copy = rcopy(dkv_ref.at[p, 2 - d, rows_at(dz), :], sib.at[d, rows_at(dz), :],
                         sib_send.at[d, dz], sib_recv.at[d, dz], sibling)
            pl.when(x >= d)(copy.start)
            copies.append((d, copy))
        return copies

    pl.when(core == 1)(lambda: share(0) and None)
    pl.when(core == 0)(lambda: share(1) and None)

    columns = Sends(col_send)
    col = pl.multiple_of(place.own * ROWS, ROWS)
    target = qg_ref.at[:, pl.ds(col, ROWS)]
    for away in (4, 5, 2, 3, 6, 7, 1):
        t = ((place.y + away // 2) % 4) * 2 + (core + away) % 2
        src = dq_ref.at[pl.ds(pl.multiple_of(place.home_row(t), 64), 64), :]
        columns.start(None, src, target, q_recv.at[place.own], place.in_column(t))
    src = dq_ref.at[pl.ds(pl.multiple_of(place.home_row(), 64), 64), :]
    stay = pltpu.make_async_copy(src, target, local_sem.at[0])
    stay.start()

    def both(p, d, dz):
        part = sib.at[d, rows_at(dz), :]
        rcopy(part, part, sib_send.at[d, dz], sib_recv.at[d, dz], sibling).wait_recv()
        return dkv_ref[p, 2 - d, rows_at(dz), :].astype(F32) + part[...].astype(F32)

    def arrived(ref, sem):
        rcopy(ref, ref, send_sems.at[0], sem, sibling).wait_recv()
        return ref[...].astype(F32)

    def send_halves(sends, cond, src, start, landing, recv, x_to, z_to, stays):
        for half in range(2):
            rows = src.at[pl.ds(pl.multiple_of(start + half * 256, 256), 256), :]
            away = cond
            if stays:
                here = (place.ylo == half) & (core == place.ylo)
                local = pltpu.make_async_copy(rows, landing, local_sem.at[1])
                pl.when(here)(local.start)
                pl.when(here)(local.wait)
                away = jnp.logical_not(here)
            sends.start(away, rows, landing, recv,
                        place.at(x=x_to, z=z_to, ylo=half, core=place.ylo))

    def keys_home():
        sends = Sends(send_sems)
        for dz in FAR_FIRST:
            for d in (2, 1):
                @pl.when(x >= d)
                def _():
                    snd[d, rows_at(dz), :] = both(0, d, dz).astype(BF16)
                sends.start(x >= d, snd.at[d, rows_at(dz), :], rx.at[d - 1, rows_at(dz), :],
                            rx_recv.at[d - 1, dz], place.at(x=(x + 4 - d) % 4))
            acc[0, rows_at(dz), :] = both(0, 0, dz)
        for dz in FAR_FIRST:
            for d in (1, 2):
                @pl.when(x + d <= 3)
                def _():
                    acc[0, rows_at(dz), :] += arrived(rx.at[d - 1, rows_at(dz), :],
                                                      rx_recv.at[d - 1, dz])
            hop[rows_at(dz), :] = acc[0, rows_at(dz), :].astype(BF16)
            send_halves(sends, None, hop, ((z + dz) % 4) * COLUMN, rz.at[dz], rz_recv.at[dz],
                        x, (z + dz) % 4, dz == 0)
        sends.finish()

    def values_home():
        sends = Sends(send_sems)
        for d in (2, 1, 0):
            for dz in (2, 1, 3):
                @pl.when(x >= d)
                def _():
                    snd[d, rows_at(dz), :] = both(1, d, dz).astype(BF16)
                sends.start(x >= d, snd.at[d, rows_at(dz), :], rzz.at[dz - 1, d],
                            rzz_recv.at[dz - 1, d], place.at(z=(z + dz) % 4))

            @pl.when(x >= d)
            def _():
                acc[d, rows_at(0), :] = both(1, d, 0)
        for d in (2, 1, 0):
            @pl.when(x >= d)
            def _():
                part = acc[d, rows_at(0), :]
                for dz in (1, 3, 2):
                    part = part + arrived(rzz.at[dz - 1, d], rzz_recv.at[dz - 1, d])
                hop[d * COLUMN:(d + 1) * COLUMN, :] = part.astype(BF16)
            send_halves(sends, x >= d, hop, d * COLUMN, rx2.at[d], rx2_recv.at[d],
                        (x + 4 - d) % 4, z, d == 0)
        sends.finish()

    pl.when(core == 0)(keys_home)
    pl.when(core == 1)(values_home)

    def landed(ref, sem, p, stays):
        wait = rcopy(ref, ref, send_sems.at[0], sem, sibling)
        if stays:
            here = (core == p) & (place.ylo == p)
            pl.when(jnp.logical_not(here))(wait.wait_recv)
        else:
            wait.wait_recv()
        return ref[...].astype(F32)

    total = None
    for dz in FAR_FIRST:
        part = landed(rz.at[dz], rz_recv.at[dz], 0, dz == 0)
        total = part if total is None else total + part
    kg_ref[...] = total.astype(BF16)
    acc[0, 0:256, :] = landed(rx2.at[0], rx2_recv.at[0], 1, True)
    for d in (1, 2):
        @pl.when(x + d <= 3)
        def _():
            acc[0, 0:256, :] += landed(rx2.at[d], rx2_recv.at[d], 1, False)
    vg_ref[...] = acc[0, 0:256, :].astype(BF16)
    for t in range(8):
        @pl.when(place.own != t)
        def _():
            src = dq_ref.at[pl.ds(0, 64), :]
            rcopy(src, qg_ref.at[:, pl.ds(t * ROWS, ROWS)], col_send.at[0], q_recv.at[t],
                  sibling).wait_recv()
    stay.wait()
    columns.finish()
    for d in range(NEAR):
        for dz in range(4):
            part = dkv_ref.at[0, 2 - d, rows_at(dz), :]
            pl.when(x >= d)(rcopy(part, part, sib_send.at[d, dz], sib_recv.at[d, dz],
                                  sibling).wait_send)


ANY = pl.BlockSpec(memory_space=pl.ANY)
VMEM = pl.BlockSpec(memory_space=pltpu.VMEM)
HBM = pl.BlockSpec(memory_space=pltpu.HBM)
SMEM = pl.BlockSpec(memory_space=pltpu.SMEM)
DMA = pltpu.SemaphoreType.DMA
MIB = 1 << 20


def struct(shape, dtype):
    return jax.ShapeDtypeStruct(shape, dtype)


def spread(q, do, o, k, v, seg, parents):
    return pl.pallas_call(
        spread_kernel,
        out_shape=(pltpu.VMEM((COLUMN, ROWS), BF16), pltpu.VMEM((COLUMN, ROWS), BF16),
                   pltpu.VMEM((8, 8, 128), F32), pltpu.VMEM((2, TOKENS, D), BF16),
                   pltpu.VMEM((64, 128), jnp.int32), pltpu.VMEM((64,), jnp.int32)),
        in_specs=[HBM] * 7,
        out_specs=(VMEM,) * 6,
        scratch_shapes=[
            pltpu.VMEM((64, 4096), BF16), pltpu.VMEM((64, 4096), BF16), DMA((4,)),
            pltpu.VMEM((8, 8, 128), F32),
            DMA((24,)), DMA((8,)), DMA((8,)), DMA((8,)), DMA((4,)),
            DMA((2,)), DMA((2,)), DMA((32,)), DMA((16, 2)), DMA((16,)), DMA((8,)),
        ],
        compiler_params=pltpu.CompilerParams(
            collective_id=0, has_side_effects=True, vmem_limit_bytes=56 * MIB),
        name="spread",
    )(q, do, o, k, v, seg, parents)


def grads(parents, seg, q, do, dg, kv):
    return pl.pallas_call(
        grad_kernel,
        out_shape=(pltpu.VMEM((2, NEAR, SECTION, D), BF16), pltpu.VMEM((COLUMN, ROWS), BF16)),
        in_specs=[VMEM] * 6,
        out_specs=(VMEM, VMEM),
        scratch_shapes=[
            pltpu.VMEM((2, NEAR * SECTION, D), F32),
            pltpu.VMEM((SLOTS * GROUP * BLOCK, ROWS), F32),
            pltpu.VMEM((4 * ROWS, D), BF16),
            pltpu.VMEM((4 * ROWS, D), BF16),
            pltpu.VMEM((SLOTS * 8, ROWS), F32),
            pltpu.VMEM((16, ROWS), F32),
            pltpu.VMEM((16, ROWS), F32),
            pltpu.VMEM((4 * D, ROWS), F32),
            pltpu.SMEM((256,), jnp.int32), pltpu.SMEM((64,), jnp.int32), DMA,
        ],
        compiler_params=pltpu.CompilerParams(vmem_limit_bytes=42 * MIB),
        name="grads",
    )(parents, seg, q, do, dg, kv)


def home(dkv, dq):
    return pl.pallas_call(
        home_kernel,
        out_shape=(pltpu.VMEM((64, 4096), BF16), pltpu.VMEM((256, D), BF16),
                   pltpu.VMEM((256, D), BF16)),
        in_specs=[VMEM, VMEM],
        out_specs=(VMEM,) * 3,
        scratch_shapes=[
            pltpu.VMEM((NEAR, SECTION, D), BF16),
            pltpu.VMEM((NEAR, SECTION, D), F32),
            pltpu.VMEM((NEAR, SECTION, D), BF16),
            pltpu.VMEM((SECTION, D), BF16),
            pltpu.VMEM((2, SECTION, D), BF16),
            pltpu.VMEM((4, 256, D), BF16),
            pltpu.VMEM((3, NEAR, COLUMN, D), BF16),
            pltpu.VMEM((NEAR, 256, D), BF16),
            DMA((8,)), DMA((8,)), DMA((2,)), DMA((3, 4)), DMA((3, 4)),
            DMA((20,)), DMA((2, 4)), DMA((4,)), DMA((3, 3)), DMA((3,)),
        ],
        compiler_params=pltpu.CompilerParams(
            collective_id=1, has_side_effects=True, vmem_limit_bytes=24 * MIB),
        name="home",
    )(dkv, dq)


def hand_over_kernel(*refs):
    copies = [pltpu.make_async_copy(refs[n], refs[3 + n], refs[6].at[n]) for n in range(3)]
    for copy in copies:
        copy.start()
    for copy in copies:
        copy.wait()


def hand_over(*arrays):
    return pl.pallas_call(
        hand_over_kernel,
        out_shape=tuple(struct(a.shape, a.dtype) for a in arrays),
        in_specs=[VMEM] * 3,
        out_specs=(HBM,) * 3,
        scratch_shapes=[DMA((3,))],
        compiler_params=pltpu.CompilerParams(vmem_limit_bytes=8 * MIB),
        name="hand_over",
    )(*arrays)


def local(query_rows, key_rows, value_rows, attn_output, out_grad, segments, parents):
    q, do, dg, kv, seg, parents = spread(
        query_rows, out_grad, attn_output, key_rows, value_rows, segments.reshape(64, 128), parents)
    dkv, dq = grads(parents, seg, q, do, dg, kv)
    return hand_over(*home(dkv, dq))


def solution(mesh):
    placed = (
        P(("ctx", "head"), None),
        P("ctx", "head"),
        P("ctx", "head"),
        P(("ctx", "head"), None),
        P(("ctx", "head"), None),
        P(),
        P(),
    )
    return jax.shard_map(
        local,
        mesh=mesh,
        in_specs=placed,
        out_specs=(P(("ctx", "head"), None), P("ctx", "head"), P("ctx", "head")),
        check_vma=False,
    )
```

```python
import functools
import math

import jax
import jax.numpy as jnp
from jax import lax
from jax.experimental import pallas as pl
from jax.experimental.pallas import tpu as pltpu
from jax.sharding import PartitionSpec as P

D = 128
BLOCK = 128
TOKENS = 8192
COLUMN = 512
SECTION = 2048
NEAR = 3
FAR_FIRST = (2, 1, 3, 0)
RELAYED = (0, 1)
GROUP = 4
WIDTHS = (4, 2, 1)
SLOTS = 24
ROWS = 512
SCALE = 1.0 / math.sqrt(D)
LOG2E = math.log2(math.e)
NEG = -1e30
F32 = jnp.float32
BF16 = jnp.bfloat16
MESH = pl.DeviceIdType.MESH
NT = (((1,), (1,)), ((), ()))
TN = (((0,), (0,)), ((), ()))


class Place:
    def __init__(self):
        ctx = lax.axis_index("ctx")
        head = lax.axis_index("head")
        self.x = ctx // 8
        self.z = (ctx // 2) % 4
        self.ylo = ctx % 2
        self.yhi = head // 2
        self.core = head % 2
        self.y = self.yhi * 2 + self.ylo

    def at(self, x=None, z=None, ylo=None, yhi=None, core=None):
        x = self.x if x is None else x
        z = self.z if z is None else z
        ylo = self.ylo if ylo is None else ylo
        yhi = self.yhi if yhi is None else yhi
        core = self.core if core is None else core
        return ((x * 4 + z) * 2 + ylo, yhi * 2 + core)

    def in_column(self, t):
        return self.at(ylo=(t // 2) % 2, yhi=t // 4, core=t % 2)

    @property
    def own(self):
        return self.y * 2 + self.core

    def home_row(self, t=None):
        if t is None:
            return (self.ylo * 2 + self.yhi) * 128 + self.core * 64
        return (((t // 2) % 2) * 2 + t // 4) * 128 + (t % 2) * 64


def greet(place, homeward=False):
    barrier = pltpu.get_barrier_semaphore()
    for t in range(8):
        @pl.when(place.own != t)
        def _():
            pl.semaphore_signal(barrier, inc=1, device_id=place.in_column(t), device_id_type=MESH)
    for step in range(1, 4):
        pl.semaphore_signal(
            barrier, inc=1, device_id=place.at(x=(place.x + step) % 4), device_id_type=MESH)
        pl.semaphore_signal(
            barrier, inc=1, device_id=place.at(z=(place.z + step) % 4), device_id_type=MESH)
    if not homeward:
        pl.semaphore_wait(barrier, 13)
        return
    for step in range(1, 4):
        pl.semaphore_signal(
            barrier, inc=1, device_id=place.at(z=(place.z + step) % 4, ylo=place.core, core=0),
            device_id_type=MESH)
    for d in (1, 2):
        @pl.when(place.x + d <= 3)
        def _():
            pl.semaphore_signal(
                barrier, inc=1,
                device_id=place.at(x=(place.x + d) % 4, ylo=place.core, core=1),
                device_id_type=MESH)
    pl.semaphore_wait(barrier, 13 + jnp.where(place.core == 0, 6, 2 * jnp.minimum(place.x, 2)))


def rcopy(src, dst, send, recv, device):
    return pltpu.make_async_remote_copy(
        src_ref=src, dst_ref=dst, send_sem=send, recv_sem=recv,
        device_id=device, device_id_type=MESH)


class Sends:
    def __init__(self, sems):
        self.sems = sems
        self.items = []

    def start(self, cond, src, dst, recv, device):
        copy = rcopy(src, dst, self.sems.at[len(self.items)], recv, device)
        self.items.append((cond, copy))
        if cond is None:
            copy.start()
        else:
            pl.when(cond)(copy.start)

    def finish(self):
        for cond, copy in self.items:
            if cond is None:
                copy.wait_send()
            else:
                pl.when(cond)(copy.wait_send)


def spread_kernel(q_ref, do_ref, o_ref, k_ref, v_ref, seg_ref, parents_ref,
                  qg_ref, dog_ref, dg_ref, kv_ref, seg_near, parents_near,
                  do_near, o_near, near_sem, dsrc, col_send, q_recv, do_recv, d_recv, local_sem,
                  first_send, first_recv, piece_send, prim_recv, sib_recv, dot_send):
    place = Place()
    x, z, core = place.x, place.z, place.core
    nears = [pltpu.make_async_copy(do_ref, do_near, near_sem.at[0]),
             pltpu.make_async_copy(o_ref, o_near, near_sem.at[1]),
             pltpu.make_async_copy(seg_ref, seg_near, near_sem.at[2]),
             pltpu.make_async_copy(parents_ref, parents_near, near_sem.at[3])]
    for copy in nears:
        copy.start()
    greet(place)

    first_row = pl.multiple_of((x * 4 + z) * COLUMN + place.ylo * 256, 256)
    firsts = []
    for p, src in ((0, k_ref), (1, v_ref)):
        dst = kv_ref.at[p, pl.ds(first_row, 256), :]
        here = (place.ylo == core) & (core == p)
        away = jnp.logical_not(here)
        copy = rcopy(src, dst, first_send.at[p], first_recv.at[place.ylo],
                     place.at(ylo=core, core=p))
        local = pltpu.make_async_copy(src, dst, local_sem.at[3])
        pl.when(away)(copy.start)
        pl.when(here)(local.start)
        firsts.append((here, away, copy, local))

    my_row = pl.multiple_of(place.home_row(), 64)
    columns = Sends(col_send)
    locals_ = []

    def across(src, dst, recv, sem):
        target = dst.at[pl.ds(my_row, 64), :]
        for away in (4, 5, 2, 3, 6, 7, 1, 0):
            t = ((place.y + away // 2) % 4) * 2 + (core + away) % 2
            cols = pl.ds(pl.multiple_of(t * ROWS, ROWS), ROWS)
            if away:
                columns.start(None, src.at[:, cols], target, recv.at[place.own],
                              place.in_column(t))
            else:
                local = pltpu.make_async_copy(src.at[:, cols], target, sem)
                local.start()
                locals_.append(local)

    across(q_ref, qg_ref, q_recv, local_sem.at[0])

    lane = lax.broadcasted_iota(jnp.int32, (8, 128), 1)
    line = lax.broadcasted_iota(jnp.int32, (8, 128), 0)
    mine = (lane // 64) == core
    ones = jnp.ones((8, D), BF16)
    for copy in nears:
        copy.wait()
    for t in range(8):
        tile = jnp.zeros((8, 128), F32)
        for r in range(4):
            cols = slice((t * 4 + r) * D, (t * 4 + r + 1) * D)
            prod = do_near[:, cols].astype(F32) * o_near[:, cols].astype(F32)
            high = prod.astype(BF16)
            low = (prod - high.astype(F32)).astype(BF16)
            row = (lax.dot_general(ones, high, NT, preferred_element_type=F32)
                   + lax.dot_general(ones, low, NT, preferred_element_type=F32))
            row = jnp.concatenate([row, row], axis=1)
            tile = jnp.where(mine & (line == r), row, tile)
        dsrc[t] = tile
    dots = Sends(dot_send)
    target = dg_ref.at[place.own]
    for t in range(8):
        dots.start(place.own != t, dsrc.at[t], target, d_recv.at[place.own],
                   place.in_column(t))
    stay = pltpu.make_async_copy(dsrc.at[place.own], target, local_sem.at[2])
    stay.start()

    across(do_ref, dog_ref, do_recv, local_sem.at[1])

    for half in range(2):
        here = (place.ylo == core) & (place.ylo == half)
        wait = rcopy(k_ref, kv_ref.at[core, pl.ds(0, 256), :], first_send.at[0],
                     first_recv.at[half], place.at(core=1 - core))
        pl.when(jnp.logical_not(here))(wait.wait_recv)
    for here, away, copy, local in firsts:
        pl.when(here)(local.wait)

    def piece(p, xx, zz, half=None):
        start = pl.multiple_of((xx * 4 + zz) * COLUMN, COLUMN)
        if half is None:
            return kv_ref.at[p, pl.ds(start, COLUMN), :]
        return kv_ref.at[p, pl.ds(pl.multiple_of(start + half * 256, 256), 256), :]

    sibling = place.at(core=1 - core)

    def run(c):
        sends = Sends(piece_send)

        def share(cond, xx, zz):
            part = piece(c, xx, zz)
            sends.start(cond, part, part, sib_recv.at[xx * 4 + zz], sibling)

        def along_x(zz, dz):
            part = piece(c, x, zz)
            recv = prim_recv.at[x * 4 + zz, 0]
            sends.start(x <= 2, part, part, recv, place.at(x=(x + 1) % 4))
            step = 3 if c == 0 and dz in RELAYED else 2
            sends.start(x <= 1, part, part, recv, place.at(x=(x + step) % 4))

        def pass_on(dz):
            xx, zz = (x + 1) % 4, (z + dz) % 4
            between = (x == 0) | (x == 3)
            arrive(between, xx, zz)
            part = piece(c, xx, zz)
            sends.start(between, part, part, prim_recv.at[xx * 4 + zz, 0],
                        place.at(x=(x + 3) % 4))

        def along_z(cond, xx):
            part = piece(c, xx, z)
            for d in (1, 3, 2):
                sends.start(cond, part, part, prim_recv.at[xx * 4 + z, 0],
                            place.at(z=(z + d) % 4))

        def arrive(cond, xx, zz, halves=False):
            parts = [piece(c, xx, zz, h) for h in (0, 1)] if halves else [piece(c, xx, zz)]
            for h, part in enumerate(parts):
                wait = rcopy(part, part, piece_send.at[0], prim_recv.at[xx * 4 + zz, h], sibling)
                if cond is None:
                    wait.wait_recv()
                else:
                    pl.when(cond)(wait.wait_recv)

        if c == 0:
            along_z(None, x)
            along_x(z, 0)
            share(None, x, z)
            for dz in (1, 3, 2):
                zz = (z + dz) % 4
                arrive(None, x, zz)
                along_x(zz, dz)
                share(None, x, zz)
                if {1: 0, 3: 1, 2: 3}[dz] in RELAYED:
                    pass_on({1: 0, 3: 1, 2: 3}[dz])
            for dz in (0, 1, 3, 2):
                zz = (z + dz) % 4
                for d in (1, 2):
                    xx = (x + 4 - d) % 4
                    arrive(x >= d, xx, zz)
                    share(x >= d, xx, zz)
        else:
            along_x(z, 0)
            along_z(None, x)
            share(None, x, z)
            for d in (1, 2):
                xx = (x + 4 - d) % 4
                arrive(x >= d, xx, z)
                along_z(x >= d, xx)
                share(x >= d, xx, z)
            for dz in (1, 3, 2):
                zz = (z + dz) % 4
                for d in range(NEAR):
                    xx = (x + 4 - d) % 4
                    arrive(x >= d, xx, zz)
                    share(x >= d, xx, zz)
        for d in range(NEAR):
            xx = (x + 4 - d) % 4
            for zz in range(4):
                part = piece(1 - c, xx, zz)
                wait = rcopy(part, part, piece_send.at[0], sib_recv.at[xx * 4 + zz], sibling)
                pl.when(x >= d)(wait.wait_recv)
        sends.finish()

    pl.when(core == 0)(lambda: run(0))
    pl.when(core == 1)(lambda: run(1))

    for t in range(8):
        @pl.when(place.own != t)
        def _():
            row = place.home_row(t)
            for src, dst, recv in ((q_ref, qg_ref, q_recv), (do_ref, dog_ref, do_recv)):
                rcopy(src.at[:, pl.ds(0, ROWS)], dst.at[pl.ds(row, 64), :], col_send.at[0],
                      recv.at[t], place.in_column(t)).wait_recv()
    for local in locals_:
        local.wait()
    for t in range(8):
        pl.when(place.own != t)(rcopy(dsrc.at[t], dg_ref.at[t], dot_send.at[0], d_recv.at[t],
                                      place.in_column(t)).wait_recv)
    stay.wait()
    dots.finish()
    columns.finish()
    for here, away, copy, local in firsts:
        pl.when(away)(copy.wait_send)


def grad_kernel(parents_near, seg_ref, q_all, do_all, dg_ref, kv,
                dkv_ref, dq_ref,
                acc, expd, qr, dor, tops, cuts, inv, dqt, chain,
                parents_ref, parents_sem):
    place = Place()
    x = place.x
    column = x * 4 + place.z
    first_block = (x - (NEAR - 1)) * (SECTION // BLOCK)
    factor = SCALE * LOG2E

    parents_copy = pltpu.make_async_copy(parents_near, parents_ref, parents_sem)
    parents_copy.start()
    n0 = jnp.sum((seg_ref[...] == 0).astype(jnp.int32))

    parents_copy.wait()

    chains = [None] * 4
    free = jnp.int32(0)
    for qb in (3, 2, 1, 0):
        gb = column * 4 + qb
        lowest = jnp.where(gb * BLOCK >= n0, n0, 0)
        if qb == 3:
            shared = jnp.bool_(False)
        else:
            base, count, low = chains[qb + 1]
            shared = (parents_ref[gb + 1] == gb) & (low == lowest)

        def more(state):
            b, n = state
            return (b >= 0) & (b * BLOCK + (BLOCK - 1) >= lowest)

        def note(state):
            b, n = state
            chain[n] = b
            return (parents_ref[b], n + 1)

        _, stop = lax.while_loop(more, note, (jnp.where(shared, -1, gb), free))
        own = (free, stop - free, lowest)
        if qb < 3:
            own = (jnp.where(shared, base + 1, free), jnp.where(shared, count - 1, stop - free), lowest)
        chains[qb] = own
        free = stop

    for slot in range(NEAR):
        @pl.when(x >= 2 - slot)
        def _():
            for p in range(2):
                acc[p, slot * SECTION:(slot + 1) * SECTION, :] = jnp.zeros((SECTION, D), F32)
    dqt[...] = jnp.zeros_like(dqt)

    for qb in range(4):
        for h in range(4):
            rows, cols = slice(qb * BLOCK, (qb + 1) * BLOCK), slice(h * D, (h + 1) * D)
            qr[qb * ROWS + h * D:qb * ROWS + (h + 1) * D, :] = q_all[rows, cols]
            dor[qb * ROWS + h * D:qb * ROWS + (h + 1) * D, :] = do_all[rows, cols]

    def block_rows(b):
        return pl.ds(pl.multiple_of((b - first_block) * BLOCK, BLOCK), BLOCK)

    def gathered(p, blocks):
        return jnp.concatenate(
            [kv[p, pl.ds(pl.multiple_of(b * BLOCK, BLOCK), BLOCK), :] for b in blocks], axis=0)

    def row_of(q):
        return pl.ds(pl.multiple_of(q * 8, 8), 1)

    def lines_of(q):
        return pl.ds(pl.multiple_of(q * 8, 8), 8)

    def rows_of(qb):
        return pl.ds(pl.multiple_of(qb * ROWS, ROWS), ROWS)

    def fold(e):
        return jnp.sum(e.reshape(-1, 8, ROWS), axis=0)

    def in_turns(turn, first, number):
        for width in WIDTHS:
            turns = number // width
            lax.fori_loop(0, turns, functools.partial(turn, first, width), 0)
            first, number = first + turns * width, number - turns * width

    def one_half(half, carry):
        def pick(even, odd):
            return jnp.where(half == 0, even, odd)

        bases = [pick(chains[q][0], chains[q + 2][0]) for q in range(2)]
        counts = [pick(chains[q][1], chains[q + 2][1]) for q in range(2)]
        lows = [pick(chains[q][2], chains[q + 2][2]) for q in range(2)]
        starts = [(column * 4 + half * 2 + q) * BLOCK for q in range(2)]
        steps = [(counts[q] + GROUP - 1) // GROUP - 1 for q in range(2)]
        items = steps[0] + steps[1]

        def blocks_of(q, g):
            base = jnp.where(q == 0, bases[0], bases[1])
            count = jnp.where(q == 0, counts[0], counts[1])
            diagonal = column * 4 + half * 2 + q
            blocks, real = [], []
            for i in range(GROUP):
                at = g * GROUP + i
                here = at < count
                index = base + jnp.where(at == 0, 0, jnp.where(at == 1, count - 1, at - 1))
                blocks.append(jnp.where(here, chain[jnp.where(here, index, 0)], diagonal))
                real.append(here)
            return blocks, real

        def item(slot):
            t = slot - 2
            late = t >= steps[0]
            q = jnp.where(slot < 2, slot, late.astype(jnp.int32))
            g = jnp.where(slot < 2, 0, t - jnp.where(late, steps[0], 0) + 1)
            return q, g

        def expd_rows(slot, i=0, n=GROUP):
            return pl.ds(pl.multiple_of(slot * GROUP * BLOCK + i * BLOCK, BLOCK), n * BLOCK)

        def masked_scores(q, g):
            blocks, real = blocks_of(q, g)
            start = (column * 4 + half * 2 + q) * BLOCK
            query_at = start + lax.broadcasted_iota(jnp.int32, (1, ROWS), 1) % BLOCK
            least = jnp.where(query_at >= n0, n0, 0)
            scores = lax.dot_general(gathered(0, blocks), qr[rows_of(half * 2 + q), :], NT,
                                     preferred_element_type=F32)
            parts = []
            for i in range(GROUP):
                first = jnp.where(real[i], blocks[i] * BLOCK, 2 * TOKENS)
                key_at = first + lax.broadcasted_iota(jnp.int32, (BLOCK, ROWS), 0)
                ok = (key_at <= query_at) & (key_at >= least)
                parts.append(jnp.where(ok, scores[i * BLOCK:(i + 1) * BLOCK, :], NEG))
            return jnp.concatenate(parts, axis=0)

        for q in range(2):
            scores = masked_scores(q, 0)
            top = jnp.max(scores, axis=0, keepdims=True)
            e = jnp.exp2((scores - top) * factor)
            expd[expd_rows(q), :] = e
            inv[lines_of(q), :] = fold(e)
            query_at = starts[q] + lax.broadcasted_iota(jnp.int32, (1, ROWS), 1) % BLOCK
            cut = jnp.where((query_at >= n0) & (starts[q] < n0), -NEG, 0.0)
            cuts[lines_of(q), :] = jnp.broadcast_to(top + cut, (8, ROWS))

        def scores_turn(first, width, n, c):
            for u in range(width):
                slot = first + n * width + u
                q, g = item(slot)
                blocks, real = blocks_of(q, g)
                scores = lax.dot_general(gathered(0, blocks), qr[rows_of(half * 2 + q), :], NT,
                                         preferred_element_type=F32)
                top = cuts[row_of(q), :]
                sums = None
                for i in range(GROUP):
                    away = top + jnp.where(real[i], 0.0, -NEG)
                    e = jnp.exp2((scores[i * BLOCK:(i + 1) * BLOCK, :] - away) * factor)
                    expd[expd_rows(slot, i, 1), :] = e
                    sums = fold(e) if sums is None else sums + fold(e)
                inv[lines_of(q), :] += sums
            return c

        in_turns(scores_turn, 2, items)
        totals = [jnp.sum(inv[q * 8:(q + 1) * 8, :], axis=0, keepdims=True) for q in range(2)]
        safe = jnp.max(jnp.maximum(totals[0], totals[1])) < 1e30
        for q in range(2):
            inv[q * 8:(q + 1) * 8, :] = jnp.broadcast_to(1.0 / totals[q], (8, ROWS))

        @pl.when(jnp.logical_not(safe))
        def _():
            cuts[...] = jnp.full_like(cuts, NEG)
            inv[...] = jnp.zeros_like(inv)

            def again(slot, c):
                q, g = item(slot)
                scores = masked_scores(q, g)
                top, total = cuts[row_of(q), :], inv[row_of(q), :]
                new_top = jnp.maximum(top, jnp.max(scores, axis=0, keepdims=True))
                e = jnp.exp2((scores - new_top) * factor)
                expd[expd_rows(slot), :] = e
                total = total * jnp.exp2((top - new_top) * factor) + jnp.sum(
                    e, axis=0, keepdims=True)
                cuts[lines_of(q), :] = jnp.broadcast_to(new_top, (8, ROWS))
                tops[lines_of(slot), :] = jnp.broadcast_to(new_top, (8, ROWS))
                inv[lines_of(q), :] = jnp.broadcast_to(total, (8, ROWS))
                return c

            def settle(slot, c):
                q, g = item(slot)
                share = jnp.exp2((tops[row_of(slot), :] - cuts[row_of(q), :]) * factor)
                expd[expd_rows(slot), :] = expd[expd_rows(slot), :] * (share / inv[row_of(q), :])
                return c

            lax.fori_loop(0, items + 2, again, 0)
            lax.fori_loop(0, items + 2, settle, 0)
            inv[...] = jnp.ones_like(inv)

        def grads_turn(first, width, n, c):
            work = []
            for u in range(width):
                slot = first + n * width + u
                q, g = item(slot)
                blocks, _ = blocks_of(q, g)
                do_rows = dor[rows_of(half * 2 + q), :]
                weight_grad = lax.dot_general(gathered(1, blocks), do_rows, NT,
                                              preferred_element_type=F32)
                work.append((slot, q, blocks, do_rows, weight_grad))
            for slot, q, blocks, do_rows, weight_grad in work:
                qb = half * 2 + q
                source = ((qb % 2) * 2 + qb // 2) * 2
                pair = dg_ref[source] + dg_ref[source + 1]
                out_dot = jnp.concatenate([pair[h:h + 1, :] for h in range(4)], axis=1)
                weights = expd[expd_rows(slot), :] * inv[row_of(q), :]
                halved = weights.astype(BF16)
                score_grad = (weights * (weight_grad - out_dot)).astype(BF16)
                dv = jnp.dot(halved, do_rows, preferred_element_type=F32)
                dk = jnp.dot(score_grad, qr[rows_of(qb), :], preferred_element_type=F32)
                into = pl.ds(pl.multiple_of(qb * D, D), D)
                dqt[into, :] += lax.dot_general(gathered(0, blocks), score_grad, TN,
                                                preferred_element_type=F32)
                for i, b in enumerate(blocks):
                    rows = block_rows(b)
                    acc[0, rows, :] += dk[i * BLOCK:(i + 1) * BLOCK, :]
                    acc[1, rows, :] += dv[i * BLOCK:(i + 1) * BLOCK, :]
            return c

        in_turns(grads_turn, 0, items + 2)
        return carry

    lax.fori_loop(0, 2, one_half, 0)

    for slot in range(NEAR):
        @pl.when(x >= 2 - slot)
        def _():
            for p, by in ((0, SCALE), (1, 1.0)):
                at = slice(slot * SECTION, (slot + 1) * SECTION)
                dkv_ref[p, slot] = (acc[p, at, :] * by).astype(BF16)
    for qb in range(4):
        for h in range(4):
            part = dqt[qb * D:(qb + 1) * D, h * D:(h + 1) * D].T * SCALE
            dq_ref[qb * BLOCK:(qb + 1) * BLOCK, h * D:(h + 1) * D] = part.astype(BF16)


def home_kernel(dkv_ref, dq_ref,
                qg_ref, kg_ref, vg_ref,
                sib, acc, snd, hop, rx, rz, rzz, rx2,
                col_send, q_recv, local_sem, sib_send, sib_recv,
                send_sems, rx_recv, rz_recv, rzz_recv, rx2_recv):
    place = Place()
    x, z, core = place.x, place.z, place.core
    greet(place, True)
    sibling = place.at(core=1 - core)

    def rows_at(dz):
        return pl.ds(pl.multiple_of(((z + dz) % 4) * COLUMN, COLUMN), COLUMN)

    def share(p):
        order = [(d, dz) for dz in FAR_FIRST for d in (2, 1, 0)]
        if p == 1:
            order = [(d, dz) for d in (2, 1, 0) for dz in FAR_FIRST]
        copies = []
        for d, dz in order:
            copy = rcopy(dkv_ref.at[p, 2 - d, rows_at(dz), :], sib.at[d, rows_at(dz), :],
                         sib_send.at[d, dz], sib_recv.at[d, dz], sibling)
            pl.when(x >= d)(copy.start)
            copies.append((d, copy))
        return copies

    pl.when(core == 1)(lambda: share(0) and None)
    pl.when(core == 0)(lambda: share(1) and None)

    columns = Sends(col_send)
    col = pl.multiple_of(place.own * ROWS, ROWS)
    target = qg_ref.at[:, pl.ds(col, ROWS)]
    for away in (4, 5, 2, 3, 6, 7, 1):
        t = ((place.y + away // 2) % 4) * 2 + (core + away) % 2
        src = dq_ref.at[pl.ds(pl.multiple_of(place.home_row(t), 64), 64), :]
        columns.start(None, src, target, q_recv.at[place.own], place.in_column(t))
    src = dq_ref.at[pl.ds(pl.multiple_of(place.home_row(), 64), 64), :]
    stay = pltpu.make_async_copy(src, target, local_sem.at[0])
    stay.start()

    def both(p, d, dz):
        part = sib.at[d, rows_at(dz), :]
        rcopy(part, part, sib_send.at[d, dz], sib_recv.at[d, dz], sibling).wait_recv()
        return dkv_ref[p, 2 - d, rows_at(dz), :].astype(F32) + part[...].astype(F32)

    def arrived(ref, sem):
        rcopy(ref, ref, send_sems.at[0], sem, sibling).wait_recv()
        return ref[...].astype(F32)

    def send_halves(sends, cond, src, start, landing, recv, x_to, z_to, stays):
        for half in range(2):
            rows = src.at[pl.ds(pl.multiple_of(start + half * 256, 256), 256), :]
            away = cond
            if stays:
                here = (place.ylo == half) & (core == place.ylo)
                local = pltpu.make_async_copy(rows, landing, local_sem.at[1])
                pl.when(here)(local.start)
                pl.when(here)(local.wait)
                away = jnp.logical_not(here)
            sends.start(away, rows, landing, recv,
                        place.at(x=x_to, z=z_to, ylo=half, core=place.ylo))

    def keys_home():
        sends = Sends(send_sems)
        for dz in FAR_FIRST:
            for d in (2, 1):
                @pl.when(x >= d)
                def _():
                    snd[d, rows_at(dz), :] = both(0, d, dz).astype(BF16)
                sends.start(x >= d, snd.at[d, rows_at(dz), :], rx.at[d - 1, rows_at(dz), :],
                            rx_recv.at[d - 1, dz], place.at(x=(x + 4 - d) % 4))
            acc[0, rows_at(dz), :] = both(0, 0, dz)
        for dz in FAR_FIRST:
            for d in (1, 2):
                @pl.when(x + d <= 3)
                def _():
                    acc[0, rows_at(dz), :] += arrived(rx.at[d - 1, rows_at(dz), :],
                                                      rx_recv.at[d - 1, dz])
            hop[rows_at(dz), :] = acc[0, rows_at(dz), :].astype(BF16)
            send_halves(sends, None, hop, ((z + dz) % 4) * COLUMN, rz.at[dz], rz_recv.at[dz],
                        x, (z + dz) % 4, dz == 0)
        sends.finish()

    def values_home():
        sends = Sends(send_sems)
        for d in (2, 1, 0):
            for dz in (2, 1, 3):
                @pl.when(x >= d)
                def _():
                    snd[d, rows_at(dz), :] = both(1, d, dz).astype(BF16)
                sends.start(x >= d, snd.at[d, rows_at(dz), :], rzz.at[dz - 1, d],
                            rzz_recv.at[dz - 1, d], place.at(z=(z + dz) % 4))

            @pl.when(x >= d)
            def _():
                acc[d, rows_at(0), :] = both(1, d, 0)
        for d in (2, 1, 0):
            @pl.when(x >= d)
            def _():
                part = acc[d, rows_at(0), :]
                for dz in (1, 3, 2):
                    part = part + arrived(rzz.at[dz - 1, d], rzz_recv.at[dz - 1, d])
                hop[d * COLUMN:(d + 1) * COLUMN, :] = part.astype(BF16)
            send_halves(sends, x >= d, hop, d * COLUMN, rx2.at[d], rx2_recv.at[d],
                        (x + 4 - d) % 4, z, d == 0)
        sends.finish()

    pl.when(core == 0)(keys_home)
    pl.when(core == 1)(values_home)

    def landed(ref, sem, p, stays):
        wait = rcopy(ref, ref, send_sems.at[0], sem, sibling)
        if stays:
            here = (core == p) & (place.ylo == p)
            pl.when(jnp.logical_not(here))(wait.wait_recv)
        else:
            wait.wait_recv()
        return ref[...].astype(F32)

    total = None
    for dz in FAR_FIRST:
        part = landed(rz.at[dz], rz_recv.at[dz], 0, dz == 0)
        total = part if total is None else total + part
    kg_ref[...] = total.astype(BF16)
    acc[0, 0:256, :] = landed(rx2.at[0], rx2_recv.at[0], 1, True)
    for d in (1, 2):
        @pl.when(x + d <= 3)
        def _():
            acc[0, 0:256, :] += landed(rx2.at[d], rx2_recv.at[d], 1, False)
    vg_ref[...] = acc[0, 0:256, :].astype(BF16)
    for t in range(8):
        @pl.when(place.own != t)
        def _():
            src = dq_ref.at[pl.ds(0, 64), :]
            rcopy(src, qg_ref.at[:, pl.ds(t * ROWS, ROWS)], col_send.at[0], q_recv.at[t],
                  sibling).wait_recv()
    stay.wait()
    columns.finish()
    for d in range(NEAR):
        for dz in range(4):
            part = dkv_ref.at[0, 2 - d, rows_at(dz), :]
            pl.when(x >= d)(rcopy(part, part, sib_send.at[d, dz], sib_recv.at[d, dz],
                                  sibling).wait_send)


ANY = pl.BlockSpec(memory_space=pl.ANY)
VMEM = pl.BlockSpec(memory_space=pltpu.VMEM)
HBM = pl.BlockSpec(memory_space=pltpu.HBM)
SMEM = pl.BlockSpec(memory_space=pltpu.SMEM)
DMA = pltpu.SemaphoreType.DMA
MIB = 1 << 20


def struct(shape, dtype):
    return jax.ShapeDtypeStruct(shape, dtype)


def spread(q, do, o, k, v, seg, parents):
    return pl.pallas_call(
        spread_kernel,
        out_shape=(pltpu.VMEM((COLUMN, ROWS), BF16), pltpu.VMEM((COLUMN, ROWS), BF16),
                   pltpu.VMEM((8, 8, 128), F32), pltpu.VMEM((2, TOKENS, D), BF16),
                   pltpu.VMEM((64, 128), jnp.int32), pltpu.VMEM((64,), jnp.int32)),
        in_specs=[HBM] * 7,
        out_specs=(VMEM,) * 6,
        scratch_shapes=[
            pltpu.VMEM((64, 4096), BF16), pltpu.VMEM((64, 4096), BF16), DMA((4,)),
            pltpu.VMEM((8, 8, 128), F32),
            DMA((24,)), DMA((8,)), DMA((8,)), DMA((8,)), DMA((4,)),
            DMA((2,)), DMA((2,)), DMA((32,)), DMA((16, 2)), DMA((16,)), DMA((8,)),
        ],
        compiler_params=pltpu.CompilerParams(
            collective_id=0, has_side_effects=True, vmem_limit_bytes=56 * MIB),
        name="spread",
    )(q, do, o, k, v, seg, parents)


def grads(parents, seg, q, do, dg, kv):
    return pl.pallas_call(
        grad_kernel,
        out_shape=(pltpu.VMEM((2, NEAR, SECTION, D), BF16), pltpu.VMEM((COLUMN, ROWS), BF16)),
        in_specs=[VMEM] * 6,
        out_specs=(VMEM, VMEM),
        scratch_shapes=[
            pltpu.VMEM((2, NEAR * SECTION, D), F32),
            pltpu.VMEM((SLOTS * GROUP * BLOCK, ROWS), F32),
            pltpu.VMEM((4 * ROWS, D), BF16),
            pltpu.VMEM((4 * ROWS, D), BF16),
            pltpu.VMEM((SLOTS * 8, ROWS), F32),
            pltpu.VMEM((16, ROWS), F32),
            pltpu.VMEM((16, ROWS), F32),
            pltpu.VMEM((4 * D, ROWS), F32),
            pltpu.SMEM((256,), jnp.int32), pltpu.SMEM((64,), jnp.int32), DMA,
        ],
        compiler_params=pltpu.CompilerParams(vmem_limit_bytes=42 * MIB),
        name="grads",
    )(parents, seg, q, do, dg, kv)


def home(dkv, dq):
    return pl.pallas_call(
        home_kernel,
        out_shape=(pltpu.VMEM((64, 4096), BF16), pltpu.VMEM((256, D), BF16),
                   pltpu.VMEM((256, D), BF16)),
        in_specs=[VMEM, VMEM],
        out_specs=(VMEM,) * 3,
        scratch_shapes=[
            pltpu.VMEM((NEAR, SECTION, D), BF16),
            pltpu.VMEM((NEAR, SECTION, D), F32),
            pltpu.VMEM((NEAR, SECTION, D), BF16),
            pltpu.VMEM((SECTION, D), BF16),
            pltpu.VMEM((2, SECTION, D), BF16),
            pltpu.VMEM((4, 256, D), BF16),
            pltpu.VMEM((3, NEAR, COLUMN, D), BF16),
            pltpu.VMEM((NEAR, 256, D), BF16),
            DMA((8,)), DMA((8,)), DMA((2,)), DMA((3, 4)), DMA((3, 4)),
            DMA((20,)), DMA((2, 4)), DMA((4,)), DMA((3, 3)), DMA((3,)),
        ],
        compiler_params=pltpu.CompilerParams(
            collective_id=1, has_side_effects=True, vmem_limit_bytes=24 * MIB),
        name="home",
    )(dkv, dq)


def hand_over_kernel(*refs):
    copies = [pltpu.make_async_copy(refs[n], refs[3 + n], refs[6].at[n]) for n in range(3)]
    for copy in copies:
        copy.start()
    for copy in copies:
        copy.wait()


def hand_over(*arrays):
    return pl.pallas_call(
        hand_over_kernel,
        out_shape=tuple(struct(a.shape, a.dtype) for a in arrays),
        in_specs=[VMEM] * 3,
        out_specs=(HBM,) * 3,
        scratch_shapes=[DMA((3,))],
        compiler_params=pltpu.CompilerParams(vmem_limit_bytes=8 * MIB),
        name="hand_over",
    )(*arrays)


def local(query_rows, key_rows, value_rows, attn_output, out_grad, segments, parents):
    q, do, dg, kv, seg, parents = spread(
        query_rows, out_grad, attn_output, key_rows, value_rows, segments.reshape(64, 128), parents)
    dkv, dq = grads(parents, seg, q, do, dg, kv)
    return hand_over(*home(dkv, dq))


def solution(mesh):
    placed = (
        P(("ctx", "head"), None),
        P("ctx", "head"),
        P("ctx", "head"),
        P(("ctx", "head"), None),
        P(("ctx", "head"), None),
        P(),
        P(),
    )
    return jax.shard_map(
        local,
        mesh=mesh,
        in_specs=placed,
        out_specs=(P(("ctx", "head"), None), P("ctx", "head"), P("ctx", "head")),
        check_vma=False,
    )
```
